32 devices in a mesh: head: 4 (over y, x), row: 8 (over z, core).
Axes of the slice: x: 2, y: 2, z: 4, core: 2. Of those that a mesh axis runs over, the one named last changes fastest.
Arguments:
- token_ids: int32 [16384], P('row'), may hold values from 0 to 30719
- segment_ids: int32 [16384], P('row'), may hold values from 0 to 511, as said below
- masked_pos: int32 [8, 256], P('row'), may hold values from 0 to 2047, as said below
- masked_target: int32 [8, 256], P('row'), may hold values from 0 to 30719
- embedding: float32 [30720, 768], P(('head', 'row')), may hold values from -1 to 1
- position_table: float32 [512, 768], P(None, ('head', 'row')), may hold values from -0.3 to 0.3
- qkv_weight: float32 [768, 2304], P('row', 'head'), may hold values from -0.21875 to 0.21875
- out_weight: float32 [768, 768], P(None, ('head', 'row')), may hold values from -0.625 to 0.625
- up_weight: float32 [768, 3072], P(None, ('head', 'row')), may hold values from -0.21875 to 0.21875
- down_weight: float32 [3072, 768], P(('head', 'row')), may hold values from -0.109375 to 0.109375
- norm_params: float32 [8, 768], P(None, ('head', 'row')), may hold values from -1 to 4
- up_bias: float32 [3072], P(('head', 'row')), may hold values from -2.5 to 2.5
- m_embedding: float32 [30720, 768], P(('head', 'row')), may hold values from -2.3841858e-06 to 2.3841858e-06
- m_position: float32 [512, 768], P(None, ('head', 'row')), may hold values from -2.3841858e-06 to 2.3841858e-06
- m_qkv: float32 [768, 2304], P('row', 'head'), may hold values from -2.3841858e-06 to 2.3841858e-06
- m_out: float32 [768, 768], P(None, ('head', 'row')), may hold values from -2.3841858e-06 to 2.3841858e-06
- m_up: float32 [768, 3072], P(None, ('head', 'row')), may hold values from -2.3841858e-06 to 2.3841858e-06
- m_down: float32 [3072, 768], P(('head', 'row')), may hold values from -2.3841858e-06 to 2.3841858e-06
- m_norm: float32 [8, 768], P(None, ('head', 'row')), may hold values from -9.536743e-06 to 9.536743e-06
- m_bias: float32 [3072], P(('head', 'row')), may hold values from -9.536743e-06 to 9.536743e-06
- v_embedding: float32 [30720, 768], P(('head', 'row')), may hold values from 1.2872796e-14 to 5.1491184e-14
- v_position: float32 [512, 768], P(None, ('head', 'row')), may hold values from 1.2872796e-14 to 5.1491184e-14
- v_qkv: float32 [768, 2304], P('row', 'head'), may hold values from 1.2872796e-14 to 5.1491184e-14
- v_out: float32 [768, 768], P(None, ('head', 'row')), may hold values from 1.2872796e-14 to 5.1491184e-14
- v_up: float32 [768, 3072], P(None, ('head', 'row')), may hold values from 1.2872796e-14 to 5.1491184e-14
- v_down: float32 [3072, 768], P(('head', 'row')), may hold values from 1.2872796e-14 to 5.1491184e-14
- v_norm: float32 [8, 768], P(None, ('head', 'row')), may hold values from 2.0596473e-13 to 8.2385894e-13
- v_bias: float32 [3072], P(('head', 'row')), may hold values from 5.1491184e-14 to 2.0596473e-13
Outputs:
- new_embedding: float32 [30720, 768], P(('head', 'row'))
- new_position: float32 [512, 768], P(None, ('head', 'row'))
- new_qkv: float32 [768, 2304], P('row', 'head')
- new_out: float32 [768, 768], P(None, ('head', 'row'))
- new_up: float32 [768, 3072], P(None, ('head', 'row'))
- new_down: float32 [3072, 768], P(('head', 'row'))
- new_norm: float32 [8, 768], P(None, ('head', 'row'))
- new_bias: float32 [3072], P(('head', 'row'))
- new_m_embedding: float32 [30720, 768], P(('head', 'row'))
- new_m_position: float32 [512, 768], P(None, ('head', 'row'))
- new_m_qkv: float32 [768, 2304], P('row', 'head')
- new_m_out: float32 [768, 768], P(None, ('head', 'row'))
- new_m_up: float32 [768, 3072], P(None, ('head', 'row'))
- new_m_down: float32 [3072, 768], P(('head', 'row'))
- new_m_norm: float32 [8, 768], P(None, ('head', 'row'))
- new_m_bias: float32 [3072], P(('head', 'row'))
- new_v_embedding: float32 [30720, 768], P(('head', 'row'))
- new_v_position: float32 [512, 768], P(None, ('head', 'row'))
- new_v_qkv: float32 [768, 2304], P('row', 'head')
- new_v_out: float32 [768, 768], P(None, ('head', 'row'))
- new_v_up: float32 [768, 3072], P(None, ('head', 'row'))
- new_v_down: float32 [3072, 768], P(('head', 'row'))
- new_v_norm: float32 [8, 768], P(None, ('head', 'row'))
- new_v_bias: float32 [3072], P(('head', 'row'))
- loss_sum: float32 [], replicated
- live_count: float32 [], replicated
- grad_norm: float32 [], replicated
The draws below stay inside these ranges and needn't reach their ends.
Inputs may be any that keep to these rules, and one draw needn't show every extreme that they name: `segment_ids`: within each sequence of 512 tokens the documents are numbered from 0 upward, never falling; the tokens after the last document carry 512 - 1 and form padding, which every sequence has. `masked_pos`: entry k of a row lies in [8 k, 8 k + 8) among the group's 2048 tokens.
All inputs are finite; a program needn't handle non-finite values.
Results may differ from the reference program's by a relative error of at most 0.019.
The reference program's roundings to bfloat16 on the way count: a program that leaves them out, or rounds other values in their place, can miss the bound.
Values may be sent and summed in bfloat16 or wider, within the bound.
A program may use at most 256 MiB of HBM per device.

```python
import math
import jax
import jax.numpy as jnp
from jax import lax

D = 768
H = 12
HD = 64
FF = 3072
V = 30720
SEQ = 512
SEQS_G = 4
STEP = 5
RAMP = 10
OLD_HEADS = 8
OLD_FF = 2048
TG = 2048
GROUPS = 8
TOKENS = 16384
PARAMS = 31073280


def draw_segment_ids(key, part):
    key = jax.random.fold_in(key, 11)
    first_key, second_key = jax.random.split(key)
    count = GROUPS * SEQS_G
    numbers = jnp.arange(count)
    group = numbers // SEQS_G
    within = numbers % SEQS_G
    rise = SEQ * 7 // 20
    live = SEQ * 3 // 10 + rise * group // max(GROUPS - 1, 1) + rise * within // max(SEQS_G - 1, 1)
    live = live - jax.random.randint(first_key, (count,), 1, SEQ // 16 + 1)
    starts = jax.random.randint(second_key, (count, SEQ), 0, SEQ // 4) == 0
    starts = starts.at[:, 0].set(False)
    document = jnp.cumsum(starts.astype(jnp.int32), axis=1)
    place = jnp.arange(SEQ)[None, :]
    labels = jnp.where(place < live[:, None], document, SEQ - 1)
    return labels.reshape(-1).astype(jnp.int32)


def draw_masked_pos(key, part):
    key = jax.random.fold_in(key, 12)
    windows = TG // 8
    jitter = jax.random.randint(key, (GROUPS, windows), 0, 8)
    return (jnp.arange(windows)[None, :] * 8 + jitter).astype(jnp.int32)


def draw_embedding(key, part):
    key = jax.random.fold_in(key, 13)
    slope = jnp.arange(V, dtype=jnp.float32)[:, None] / V
    base = jnp.clip(jax.random.normal(key, (V, D), jnp.float32), -5.0, 5.0)
    spread = 1.0 + 2.0 * slope
    return base * spread * D ** (-0.5)


def draw_norm_params(key, part):
    key = jax.random.fold_in(key, 14)
    first_key, second_key = jax.random.split(key)
    slope = jnp.arange(D, dtype=jnp.float32)[None, :] / D
    gains = jax.random.uniform(first_key, (8, D), jnp.float32, 0.7, 1.3) * (1.0 + 2.0 * slope)
    shifts = jnp.clip(0.2 * jax.random.normal(second_key, (8, D), jnp.float32), -0.8, 0.8)
    rows = jnp.arange(8)[:, None]
    is_gain = (rows % 2 == 0) & (rows < 6)
    return jnp.where(is_gain, gains, shifts)


def touch_ends(values, rng, least, largest):
    longest = values.shape.index(max(values.shape))
    spots = []
    for shift in (0, 1):
        where = [jax.random.randint(jax.random.fold_in(rng, axis), (), 0, length) for axis, length in enumerate(values.shape)]
        where[longest] = (where[longest] + shift) % values.shape[longest]
        spots.append(tuple(where))
    return values.at[spots[0]].set(least).at[spots[1]].set(largest)


def block_scale(rng, dims, cuts, smallest, top_value):
    loudness, own = 1.0, jax.random.fold_in(rng, 6)
    for position, parts in cuts:
        steps = jnp.exp(jax.random.uniform(jax.random.fold_in(own, position), (parts,), jnp.float32, smallest / len(cuts), top_value / len(cuts)))
        loudness = loudness * jnp.repeat(steps, dims[position] // parts).reshape([-1 if axis == position else 1 for axis in range(len(dims))])
    return loudness


def centred(own_key, extent, deviation, limit, shards=(), kind=jnp.bfloat16):
    result = deviation * jax.random.normal(own_key, extent, jnp.float32)
    if shards:
        result = result * block_scale(own_key, extent, shards, -0.22, 0.18)
    return jnp.clip(result, -limit, limit).astype(kind)


def setup_inputs(seed: int = 0) -> dict:
    streams_of = jax.random.split(jax.random.key(seed), 29)
    token_ids = touch_ends(jax.random.randint(streams_of[0], (TOKENS,), 0, V), jax.random.fold_in(streams_of[0], 1), 0, V - 1).astype(jnp.int32)
    segment_ids = draw_segment_ids(jax.random.fold_in(streams_of[28], 71), 0)
    masked_pos = draw_masked_pos(jax.random.fold_in(streams_of[28], 71), 0)
    masked_target = touch_ends(jax.random.randint(streams_of[3], (GROUPS, TG // 8), 0, V), jax.random.fold_in(streams_of[3], 1), 0, V - 1).astype(jnp.int32)
    embedding = draw_embedding(jax.random.fold_in(streams_of[28], 71), 0)
    position_table = centred(streams_of[5], (SEQ, D), 0.05, 0.3, ((1, 32),), jnp.float32)
    qkv_weight = centred(streams_of[6], (D, 3 * D), D ** -0.5, 0.21875, ((0, 8), (1, 4)), jnp.float32)
    out_weight = centred(streams_of[7], (D, D), (D // 8) ** -0.5, 0.625, ((1, 32),), jnp.float32)
    up_weight = centred(streams_of[8], (D, FF), D ** -0.5, 0.21875, ((1, 32),), jnp.float32)
    down_weight = centred(streams_of[9], (FF, D), FF ** -0.5, 0.109375, ((0, 32),), jnp.float32)
    norm_params = draw_norm_params(jax.random.fold_in(streams_of[28], 71), 0)
    up_bias = centred(streams_of[11], (FF,), 0.5, 2.5, ((0, 32),), jnp.float32)
    m_embedding = centred(streams_of[12], (V, D), (0.0022 * PARAMS ** -0.5), 2.384185791015625e-06, ((0, 32),), jnp.float32)
    m_position = centred(streams_of[13], (SEQ, D), (0.0022 * PARAMS ** -0.5), 2.384185791015625e-06, ((1, 32),), jnp.float32)
    m_qkv = centred(streams_of[14], (D, 3 * D), (0.0022 * PARAMS ** -0.5), 2.384185791015625e-06, ((0, 8), (1, 4)), jnp.float32)
    m_out = centred(streams_of[15], (D, D), (0.0022 * PARAMS ** -0.5), 2.384185791015625e-06, ((1, 32),), jnp.float32)
    m_up = centred(streams_of[16], (D, FF), (0.0022 * PARAMS ** -0.5), 2.384185791015625e-06, ((1, 32),), jnp.float32)
    m_down = centred(streams_of[17], (FF, D), (0.0022 * PARAMS ** -0.5), 2.384185791015625e-06, ((0, 32),), jnp.float32)
    m_norm = centred(streams_of[18], (8, D), (0.0088 * PARAMS ** -0.5), 9.5367431640625e-06, ((1, 32),), jnp.float32)
    m_bias = centred(streams_of[19], (FF,), (0.0088 * PARAMS ** -0.5), 9.5367431640625e-06, ((0, 32),), jnp.float32)
    v_embedding = jnp.clip(jnp.exp(math.log(5.149118368556575e-14) - 1.3862944 * jax.random.uniform(streams_of[20], (V, D), jnp.float32) ** block_scale(streams_of[20], (V, D), ((0, 32),), -0.2, 0.2)), 1.2872795921391438e-14, 5.149118368556575e-14)
    v_position = jnp.clip(jnp.exp(math.log(5.149118368556575e-14) - 1.3862944 * jax.random.uniform(streams_of[21], (SEQ, D), jnp.float32) ** block_scale(streams_of[21], (SEQ, D), ((1, 32),), -0.2, 0.2)), 1.2872795921391438e-14, 5.149118368556575e-14)
    v_qkv = jnp.clip(jnp.exp(math.log(5.149118368556575e-14) - 1.3862944 * jax.random.uniform(streams_of[22], (D, 3 * D), jnp.float32) ** block_scale(streams_of[22], (D, 3 * D), ((0, 8), (1, 4)), -0.2, 0.2)), 1.2872795921391438e-14, 5.149118368556575e-14)
    v_out = jnp.clip(jnp.exp(math.log(5.149118368556575e-14) - 1.3862944 * jax.random.uniform(streams_of[23], (D, D), jnp.float32) ** block_scale(streams_of[23], (D, D), ((1, 32),), -0.2, 0.2)), 1.2872795921391438e-14, 5.149118368556575e-14)
    v_up = jnp.clip(jnp.exp(math.log(5.149118368556575e-14) - 1.3862944 * jax.random.uniform(streams_of[24], (D, FF), jnp.float32) ** block_scale(streams_of[24], (D, FF), ((1, 32),), -0.2, 0.2)), 1.2872795921391438e-14, 5.149118368556575e-14)
    v_down = jnp.clip(jnp.exp(math.log(5.149118368556575e-14) - 1.3862944 * jax.random.uniform(streams_of[25], (FF, D), jnp.float32) ** block_scale(streams_of[25], (FF, D), ((0, 32),), -0.2, 0.2)), 1.2872795921391438e-14, 5.149118368556575e-14)
    v_norm = jnp.clip(jnp.exp(math.log(8.23858938969052e-13) - 1.3862944 * jax.random.uniform(streams_of[26], (8, D), jnp.float32) ** block_scale(streams_of[26], (8, D), ((1, 32),), -0.2, 0.2)), 2.05964734742263e-13, 8.23858938969052e-13)
    v_bias = jnp.clip(jnp.exp(math.log(2.05964734742263e-13) - 1.3862944 * jax.random.uniform(streams_of[27], (FF,), jnp.float32) ** block_scale(streams_of[27], (FF,), ((0, 32),), -0.2, 0.2)), 5.149118368556575e-14, 2.05964734742263e-13)
    return {"token_ids": token_ids, "segment_ids": segment_ids, "masked_pos": masked_pos, "masked_target": masked_target, "embedding": embedding, "position_table": position_table, "qkv_weight": qkv_weight, "out_weight": out_weight, "up_weight": up_weight, "down_weight": down_weight, "norm_params": norm_params, "up_bias": up_bias, "m_embedding": m_embedding, "m_position": m_position, "m_qkv": m_qkv, "m_out": m_out, "m_up": m_up, "m_down": m_down, "m_norm": m_norm, "m_bias": m_bias, "v_embedding": v_embedding, "v_position": v_position, "v_qkv": v_qkv, "v_out": v_out, "v_up": v_up, "v_down": v_down, "v_norm": v_norm, "v_bias": v_bias}


@jax.custom_vjp
def low(v):
    return lax.optimization_barrier(v.astype(jnp.bfloat16)).astype(jnp.float32)

@jax.custom_vjp
def low_back(v):
    return v

def low_keep(v):
    return (low(v), None)

def low_pass(kept, grad):
    return (grad,)

def back_keep(v):
    return (v, None)

def back_low(kept, grad):
    return (low(grad),)
low.defvjp(low_keep, low_pass)
low_back.defvjp(back_keep, back_low)
EPSILON = 1e-05
LEARN_RATE = 0.03
GAIN_RATE = 0.5
BETA_ONE = 0.9
BETA_TWO = 0.999
ADAM_EPSILON = 1e-08
DECAY = 0.01
CLIP = 0.02

def matmul(left, right):
    return jnp.dot(left, right, precision=lax.Precision.HIGHEST)

def normalize(values, gain, shift):
    center = values - lax.optimization_barrier(jnp.mean(values, axis=-1, keepdims=True))
    scale = lax.rsqrt(lax.optimization_barrier(jnp.mean(center * center, axis=-1, keepdims=True)) + EPSILON)
    return center * scale * gain + shift

def attend(block):
    mixed, labels = block
    query, keys, values = (mixed[:, :, 0], mixed[:, :, 1], mixed[:, :, 2])
    scores = low_back(jnp.einsum('qhe,khe->hqk', query, keys, precision=lax.Precision.HIGHEST) * HD ** (-0.5))
    allowed = labels[:, None] == labels[None, :]
    scores = jnp.where(allowed[None], scores, -1000000000.0)
    probs = jax.nn.softmax(scores, axis=-1)
    return jnp.einsum('hqk,khe->qhe', low(probs), values, precision=lax.Precision.HIGHEST)

def group_loss(weights, ids, labels, chosen, targets):
    embedding, position_table, qkv_weight, out_weight, up_weight, down_weight, norm_params, up_bias = weights
    table = low(embedding)
    norms = low(norm_params)
    tokens = ids.shape[0]
    sequences = tokens // SEQ
    start_sum = (table[ids].reshape(sequences, SEQ, D) + low(position_table)[None]).reshape(tokens, D)
    normed = normalize(start_sum, norms[0], norms[1])
    mixed = low(low_back(matmul(low(normed), low(qkv_weight))))
    attended = lax.map(jax.checkpoint(attend), (mixed.reshape(sequences, SEQ, H, 3, HD), labels.reshape(sequences, SEQ)))
    head_ramp = jnp.where(jnp.arange(H) < OLD_HEADS, 1.0, STEP / RAMP)
    heads = low(low_back((attended * head_ramp[:, None]).reshape(tokens, D)))
    hidden = normalize(normed + low_back(matmul(heads, low(out_weight))) + norms[6], norms[2], norms[3])
    upper = low_back(matmul(low(hidden), low(up_weight))) + low(up_bias)
    neuron_ramp = jnp.where(jnp.arange(FF) < OLD_FF, 1.0, STEP / RAMP)
    active = low(jax.nn.gelu(upper, approximate=False) * neuron_ramp)
    final = normalize(hidden + low_back(matmul(active, low(down_weight))) + norms[7], norms[4], norms[5])
    picked = low(final[chosen])
    logits = low_back(matmul(picked, table.T))
    log_total = jax.nn.logsumexp(logits, axis=1)
    target_logit = jnp.take_along_axis(logits, targets[:, None], axis=1)[:, 0]
    valid = (labels[chosen] != SEQ - 1).astype(jnp.float32)
    return (jnp.sum((log_total - target_logit) * valid), jnp.sum(valid))

def adamw(weight, grad, first, second, decay, rate):
    first = BETA_ONE * first + (1 - BETA_ONE) * grad
    second = BETA_TWO * second + (1 - BETA_TWO) * grad * grad
    moved = first / (1 - BETA_ONE ** STEP) / (jnp.sqrt(second / (1 - BETA_TWO ** STEP)) + ADAM_EPSILON)
    return (weight - rate * (moved + decay * weight), first, second)

def reference(token_ids, segment_ids, masked_pos, masked_target, embedding, position_table, qkv_weight, out_weight, up_weight, down_weight, norm_params, up_bias, m_embedding, m_position, m_qkv, m_out, m_up, m_down, m_norm, m_bias, v_embedding, v_position, v_qkv, v_out, v_up, v_down, v_norm, v_bias):
    params = (embedding, position_table, qkv_weight, out_weight, up_weight, down_weight, norm_params, up_bias)
    firsts = (m_embedding, m_position, m_qkv, m_out, m_up, m_down, m_norm, m_bias)
    seconds = (v_embedding, v_position, v_qkv, v_out, v_up, v_down, v_norm, v_bias)
    groups = token_ids.shape[0] // TG
    data = (token_ids.reshape(groups, TG), segment_ids.reshape(groups, TG), masked_pos, masked_target)

    def one(carry, block):
        ids, labels, chosen, targets = block

        def loss_of(*weights):
            return group_loss(weights, ids, labels, chosen, targets)
        loss, pull, count = jax.vjp(loss_of, *params, has_aux=True)
        grads = pull(jnp.ones_like(loss))
        total, live, sums = carry
        return ((total + loss, live + count, tuple((a + b for a, b in zip(sums, grads)))), None)
    zeros = tuple((jnp.zeros_like(p) for p in params))
    start = (jnp.zeros((), jnp.float32), jnp.zeros((), jnp.float32), zeros)
    (loss_sum, live_count, sums), _ = lax.scan(one, start, data)
    scaled = tuple((g / live_count for g in sums))
    grad_norm = jnp.sqrt(sum((jnp.sum(g * g) for g in scaled)))
    factor = jnp.minimum(1.0, CLIP / grad_norm)
    decays = (DECAY, DECAY, DECAY, DECAY, DECAY, DECAY, 0.0, 0.0)
    rates = (LEARN_RATE, LEARN_RATE, LEARN_RATE, LEARN_RATE, LEARN_RATE, LEARN_RATE, GAIN_RATE, GAIN_RATE)
    results = [adamw(w, g * factor, m, v, d, r) for w, g, m, v, d, r in zip(params, scaled, firsts, seconds, decays, rates)]
    news = [r[0] for r in results]
    moms = [r[1] for r in results]
    secs = [r[2] for r in results]
    return (news[0], news[1], news[2], news[3], news[4], news[5], news[6], news[7], moms[0], moms[1], moms[2], moms[3], moms[4], moms[5], moms[6], moms[7], secs[0], secs[1], secs[2], secs[3], secs[4], secs[5], secs[6], secs[7], loss_sum, live_count, grad_norm)
```

```python
import functools

import jax
import jax.numpy as jnp
from jax import lax
from jax.experimental import pallas as pl
from jax.experimental.pallas import tpu as pltpu
from jax.sharding import PartitionSpec as P

HD = 64
SEQ = 512
STEP = 5
RAMP = 10
OLD_HEADS = 8
OLD_FF = 2048


EPSILON = 1e-05
LEARN_RATE = 0.03
GAIN_RATE = 0.5
BETA_ONE = 0.9
BETA_TWO = 0.999
ADAM_EPSILON = 1e-08
DECAY = 0.01
CLIP = 0.02

ROOM = 64
HEADS = 4
MESH = pl.DeviceIdType.MESH
ANY = pl.BlockSpec(memory_space=pl.ANY)
VMEM = pl.BlockSpec(memory_space=pltpu.VMEM)


def place():
    h = lax.axis_index("head")
    r = lax.axis_index("row")
    return h, lax.div(r, 2), lax.rem(r, 2)


def across(h, q):
    if q == 0:
        return h
    if q == 1:
        return h + 1 - 2 * lax.rem(h, 2)
    if q == 2:
        return lax.rem(h + 2, 4)
    return 3 - h


class Wires:
    def __init__(self, send, recv):
        self.send, self.recv, self.used, self.made = send, recv, 0, []

    def copy(self, src, dst, to):
        i = self.used
        self.used += 1
        one = pltpu.make_async_remote_copy(
            src_ref=src,
            dst_ref=dst,
            send_sem=self.send.at[i],
            recv_sem=self.recv.at[i],
            device_id=to,
            device_id_type=MESH,
        )
        one.start()
        self.made.append(one)
        return one

    def sent(self):
        for one in self.made:
            one.wait_send()


def greet(peers):
    barrier = pltpu.get_barrier_semaphore()
    for to in peers:
        pl.semaphore_signal(barrier, inc=1, device_id=to, device_id_type=MESH)
    pl.semaphore_wait(barrier, len(peers))


def near(planes):
    h, z, c = place()
    peers = [(h, 2 * z + 1 - c), (across(h, 1), 2 * z + c), (across(h, 2), 2 * z + c)]
    peers += [(h, 2 * lax.rem(z + s, planes) + c) for s in range(1, planes)]
    return peers


def every_chip(planes):
    h, z, c = place()
    peers = [(h, 2 * z + 1 - c)]
    for q in range(4):
        for s in range(planes):
            if q or s:
                peers.append((across(h, q), 2 * lax.rem(z + s, planes) + c))
    return peers


def split(rows):
    first = -(-rows // 32) * 16
    return pl.ds(0, first), pl.ds(first, rows - first)


def gather_steps(wires, local, planes, pairs):
    h, z, c = place()
    row = 2 * z + c
    sib = (h, 2 * z + 1 - c)
    hx, hy, hd = across(h, 1), across(h, 2), across(h, 3)
    xn, yn = (hx, row), (hy, row)
    zs = [lax.rem(z - s + planes, planes) for s in range(planes)]
    count = len(pairs)
    here = []
    for k, (x, out) in enumerate(pairs):
        one = pltpu.make_async_copy(x, out.at[h, z, c], local.at[k])
        one.start()
        here.append(one)
    from_z = {}
    for k, (x, out) in enumerate(pairs):
        for s in range(1, planes):
            from_z[k, s] = wires.copy(x, out.at[h, z, c], (h, 2 * lax.rem(z + s, planes) + c))
    from_x, from_y, from_xd, from_yd, from_sib = {}, {}, {}, {}, []

    def launch(k, s):
        x, out = pairs[k]
        src = x if s == 0 else out.at[h, zs[s], c]
        if s:
            from_z[k, s].wait_recv()
        dst = out.at[h, zs[s], c]
        from_x[k, s] = wires.copy(src, dst, xn)
        from_y[k, s] = wires.copy(src, dst, yn)
        from_sib.append(wires.copy(src, dst, sib))

    def relay(k, s):
        _, out = pairs[k]
        first, second = split(out.shape[3])
        from_x[k, s].wait_recv()
        got = out.at[hx, zs[s], c]
        from_yd[k, s] = wires.copy(got.at[second], got.at[second], yn)
        from_sib.append(wires.copy(got, got, sib))
        from_y[k, s].wait_recv()
        got = out.at[hy, zs[s], c]
        from_xd[k, s] = wires.copy(got.at[first], got.at[first], xn)
        from_sib.append(wires.copy(got, got, sib))

    def finish(k, s):
        _, out = pairs[k]
        from_yd[k, s].wait_recv()
        from_xd[k, s].wait_recv()
        got = out.at[hd, zs[s], c]
        from_sib.append(wires.copy(got, got, sib))

    order = [(k, s) for k in range(count) for s in range(planes)]
    for i in range(len(order) + 2):
        if i < len(order):
            launch(*order[i])
        if 1 <= i <= len(order):
            relay(*order[i - 1])
        if i >= 2:
            finish(*order[i - 2])
    for one in from_sib:
        one.wait_recv()
    for one in here:
        one.wait()


def spread_start(wires, local, planes, parcels, out):
    h, z, c = place()
    sib = (h, 2 * z + 1 - c)
    got = {}
    for q in range(4):
        for s in range(planes):
            if q or s:
                th, tz = across(h, q), lax.rem(z + s, planes)
                got[q, s] = wires.copy(parcels(th, tz), out.at[c, h, z], (th, 2 * tz + c))
    mine = pltpu.make_async_copy(parcels(h, z), out.at[c, h, z], local)
    mine.start()
    passed = [wires.copy(parcels(h, z), out.at[c, h, z], sib)]
    return got, mine, passed


def spread_finish(wires, planes, out, state):
    h, z, c = place()
    sib = (h, 2 * z + 1 - c)
    got, mine, passed = state
    for (q, s), one in got.items():
        one.wait_recv()
        there = out.at[c, across(h, q), lax.rem(z - s + planes, planes)]
        passed.append(wires.copy(there, there, sib))
    for one in passed:
        one.wait_recv()
    mine.wait()


def small_kernel(planes, x, out, send, recv, local):
    greet(every_chip(planes))
    wires = Wires(send, recv)
    state = spread_start(wires, local, planes, lambda h, z: x, out)
    spread_finish(wires, planes, out, state)
    wires.sent()


def ids_kernel(planes, x, out, send, recv, local):
    h, z, c = place()
    offsets = [(s, e) for s in range(planes) for e in range(2) if s or e]
    peers = [(h, 2 * lax.rem(z + s, planes) + lax.rem(c + e, 2)) for s, e in offsets]
    greet(peers)
    wires = Wires(send, recv)
    mine = pltpu.make_async_copy(x, out.at[2 * z + c], local)
    mine.start()
    for to in peers:
        wires.copy(x, out.at[2 * z + c], to)
    for one in wires.made:
        one.wait_recv()
    mine.wait()
    wires.sent()


def gather_kernel(planes, count, *refs):
    xs, outs = refs[:count], refs[count : 2 * count]
    send, recv, local = refs[2 * count :]
    greet(near(planes))
    wires = Wires(send, recv)
    gather_steps(wires, local, planes, list(zip(xs, outs)))
    wires.sent()


def fetch_kernel(planes, count, *refs):
    parcels, xs = refs[0], refs[1 : 1 + count]
    out, outs = refs[1 + count], refs[2 + count : 2 + 2 * count]
    send, recv, local = refs[2 + 2 * count :]
    greet(every_chip(planes))
    wires = Wires(send, recv)
    state = spread_start(wires, local.at[count], planes, lambda h, z: parcels.at[h, z], out)
    gather_steps(wires, local, planes, list(zip(xs, outs)))
    spread_finish(wires, planes, out, state)
    wires.sent()


def deliver_kernel(planes, parcels, out, send, recv, local):
    greet(every_chip(planes))
    wires = Wires(send, recv)
    state = spread_start(wires, local, planes, lambda h, z: parcels.at[h, z], out)
    spread_finish(wires, planes, out, state)
    wires.sent()


def add_rows(target, others, rows):
    @pl.loop(0, rows // 16)
    def _(i):
        at = pl.ds(pl.multiple_of(i * 16, 16), 16)
        total = target[at, :].astype(jnp.float32)
        for other in others:
            total = total + other[at, :].astype(jnp.float32)
        target[at, :] = total.astype(target.dtype)


def scatter_steps(wires, local, planes, groups):
    h, z, c = place()
    row = 2 * z + c
    sib = (h, 2 * z + 1 - c)
    hx, hy, hd = across(h, 1), across(h, 2), across(h, 3)
    xn, yn = (hx, row), (hy, row)
    zs = [lax.rem(z + 1 + s, planes) for s in range(planes)]
    order = [(k, s) for k in range(len(groups)) for s in range(planes)]
    from_sib, loads = {}, {}
    for i, (k, s) in enumerate(order):
        grads, out, own, sibs, px, pz = groups[k]
        for q in (3, 1, 2, 0):
            th = across(h, q)
            from_sib[k, s, q] = wires.copy(grads.at[th, zs[s], 1 - c], sibs.at[th, zs[s]], sib)
        loads[k, s] = pltpu.make_async_copy(grads.at[:, zs[s], c], own.at[:, zs[s]], local.at[i])
        loads[k, s].start()
    first, second, from_z = {}, {}, {}

    def pair(k, s):
        grads, out, own, sibs, px, pz = groups[k]
        a, b = split(own.shape[2])
        loads[k, s].wait()
        for q in (3, 1, 2, 0):
            from_sib[k, s, q].wait_recv()
            th = across(h, q)
            add_rows(own.at[th, zs[s]], [sibs.at[th, zs[s]]], own.shape[2])
            if q == 3:
                first[k, s, "xd"] = wires.copy(
                    own.at[hd, zs[s]].at[a], px.at[zs[s], 0].at[a], xn
                )
                first[k, s, "yd"] = wires.copy(
                    own.at[hd, zs[s]].at[b], px.at[zs[s], 0].at[b], yn
                )
            if q == 1:
                first[k, s, "x"] = wires.copy(own.at[hx, zs[s]].at[a], px.at[zs[s], 1].at[a], xn)
            if q == 2:
                first[k, s, "y"] = wires.copy(own.at[hy, zs[s]].at[b], px.at[zs[s], 1].at[b], yn)

    def plane(k, s):
        grads, out, own, sibs, px, pz = groups[k]
        a, b = split(own.shape[2])
        first[k, s, "xd"].wait_recv()
        add_rows(own.at[hy, zs[s]].at[a], [px.at[zs[s], 0].at[a]], a.size)
        second[k, s, "y"] = wires.copy(own.at[hy, zs[s]].at[a], px.at[zs[s], 2].at[a], yn)
        first[k, s, "yd"].wait_recv()
        add_rows(own.at[hx, zs[s]].at[b], [px.at[zs[s], 0].at[b]], b.size)
        second[k, s, "x"] = wires.copy(own.at[hx, zs[s]].at[b], px.at[zs[s], 2].at[b], xn)

    def line(k, s):
        grads, out, own, sibs, px, pz = groups[k]
        for part in ("x", "y"):
            first[k, s, part].wait_recv()
            second[k, s, part].wait_recv()
        add_rows(own.at[h, zs[s]], [px.at[zs[s], 1], px.at[zs[s], 2]], own.shape[2])
        if s < planes - 1:
            from_z[k, s] = wires.copy(own.at[h, zs[s]], pz.at[s], (h, 2 * zs[s] + c))

    def total(k):
        grads, out, own, sibs, px, pz = groups[k]
        for s in range(planes - 1):
            from_z[k, s].wait_recv()

        @pl.loop(0, out.shape[0] // 16)
        def _(i):
            at = pl.ds(pl.multiple_of(i * 16, 16), 16)
            value = own[h, z, at, :].astype(jnp.float32)
            for s in range(planes - 1):
                value = value + pz[s, at, :].astype(jnp.float32)
            out[at, :] = value

    for i in range(len(order) + 2):
        if i < len(order):
            pair(*order[i])
        if 1 <= i <= len(order):
            plane(*order[i - 1])
        if i >= 2:
            line(*order[i - 2])
    for k in range(len(groups)):
        total(k)


def scatter_kernel(planes, count, *refs):
    grads, outs = refs[:count], refs[count : 2 * count]
    held = refs[2 * count : 2 * count + 4 * count]
    send, recv, local = refs[6 * count :]
    greet(near(planes))
    wires = Wires(send, recv)
    groups = [(grads[k], outs[k], *held[4 * k : 4 * k + 4]) for k in range(count)]
    scatter_steps(wires, local, planes, groups)
    wires.sent()


def give_kernel(planes, count, *refs):
    parcels, grads = refs[0], refs[1 : 1 + count]
    out, outs = refs[1 + count], refs[2 + count : 2 + 2 * count]
    held = refs[2 + 2 * count : 2 + 6 * count]
    mine, other, send, recv, local, extra = refs[2 + 6 * count :]
    greet(every_chip(planes))
    wires = Wires(send, recv)
    give_steps(wires, extra, planes, parcels, out, mine, other)
    groups = [(grads[k], outs[k], *held[4 * k : 4 * k + 4]) for k in range(count)]
    scatter_steps(wires, local, planes, groups)
    for one in wires.given:
        one.wait_recv()
    wires.sent()


def give_steps(wires, local, planes, parcels, out, mine, other):
    h, z, c = place()
    sib = (h, 2 * z + 1 - c)
    passed = wires.copy(parcels.at[1 - c], other, sib)
    load = pltpu.make_async_copy(parcels.at[c], mine, local.at[0])
    load.start()
    load.wait()
    passed.wait_recv()
    wires.given = []
    for q in (3, 1, 2, 0):
        for s in range(planes - 1, -1, -1):
            th, tz = across(h, q), lax.rem(z + s, planes)
            add_rows(mine.at[th, tz], [other.at[th, tz]], mine.shape[2])
            if q or s:
                wires.given.append(
                    wires.copy(mine.at[th, tz], out.at[h, z], (th, 2 * tz + c))
                )
    keep = pltpu.make_async_copy(mine.at[h, z], out.at[h, z], local.at[1])
    keep.start()
    keep.wait()


def return_kernel(planes, parcels, out, mine, other, send, recv, extra):
    greet(every_chip(planes))
    wires = Wires(send, recv)
    give_steps(wires, extra, planes, parcels, out, mine, other)
    for one in wires.given:
        one.wait_recv()
    wires.sent()


def params(number):
    return pltpu.CompilerParams(
        collective_id=number, has_side_effects=True, vmem_limit_bytes=56 << 20
    )


def dma(count):
    return pltpu.SemaphoreType.DMA((count,))


def gather_wires(planes, count):
    return count * (planes - 1 + planes * 8)


def spread_wires(planes):
    return 2 * 4 * planes


def scatter_wires(planes, count):
    return count * planes * 11


def held_scratch(planes, shape):
    rows, lanes = shape
    return [
        pltpu.VMEM((4, planes, rows, lanes), jnp.bfloat16),
        pltpu.VMEM((4, planes, rows, lanes), jnp.bfloat16),
        pltpu.VMEM((planes, 3, rows, lanes), jnp.bfloat16),
        pltpu.VMEM((planes - 1, rows, lanes), jnp.bfloat16),
    ]


class Kernels:
    def __init__(self, planes):
        self.planes = planes

    def ids(self, block):
        planes = self.planes
        wires = 2 * planes - 1
        return pl.pallas_call(
            functools.partial(ids_kernel, planes),
            out_shape=jax.ShapeDtypeStruct((2 * planes, *block.shape), block.dtype),
            in_specs=[ANY],
            out_specs=ANY,
            scratch_shapes=[dma(wires), dma(wires), pltpu.SemaphoreType.DMA],
            compiler_params=params(1),
            name="ids",
        )(block)

    def fetch(self, parcels, blocks):
        planes, count = self.planes, len(blocks)
        wires = gather_wires(planes, count) + spread_wires(planes)
        result = pl.pallas_call(
            functools.partial(fetch_kernel, planes, count),
            out_shape=[jax.ShapeDtypeStruct((2, *parcels.shape), parcels.dtype)]
            + [jax.ShapeDtypeStruct((4, planes, 2, *b.shape), b.dtype) for b in blocks],
            in_specs=[ANY] * (1 + count),
            out_specs=[ANY] * (1 + count),
            scratch_shapes=[dma(wires), dma(wires), dma(count + 1)],
            compiler_params=params(2),
            name="fetch",
        )(parcels, *blocks)
        return result[0], result[1:]

    def deliver(self, parcels):
        planes = self.planes
        wires = spread_wires(planes)
        return pl.pallas_call(
            functools.partial(deliver_kernel, planes),
            out_shape=jax.ShapeDtypeStruct((2, *parcels.shape), parcels.dtype),
            in_specs=[ANY],
            out_specs=ANY,
            scratch_shapes=[dma(wires), dma(wires), pltpu.SemaphoreType.DMA],
            compiler_params=params(3),
            name="deliver",
        )(parcels)

    def rows(self, block):
        planes = self.planes
        wires = gather_wires(planes, 1)
        return pl.pallas_call(
            functools.partial(gather_kernel, planes, 1),
            out_shape=jax.ShapeDtypeStruct((4, planes, 2, *block.shape), block.dtype),
            in_specs=[ANY],
            out_specs=ANY,
            scratch_shapes=[dma(wires), dma(wires), dma(1)],
            compiler_params=params(4),
            name="rows",
        )(block)

    def small(self, block, number):
        planes = self.planes
        wires = spread_wires(planes)
        return pl.pallas_call(
            functools.partial(small_kernel, planes),
            out_shape=jax.ShapeDtypeStruct((2, 4, planes, *block.shape), block.dtype),
            in_specs=[VMEM],
            out_specs=VMEM,
            scratch_shapes=[dma(wires), dma(wires), pltpu.SemaphoreType.DMA],
            compiler_params=params(number),
            name="small",
        )(block)

    def scatter_rows(self, grads):
        planes = self.planes
        shape = grads.shape[3:]
        wires = scatter_wires(planes, 1)
        return pl.pallas_call(
            functools.partial(scatter_kernel, planes, 1),
            out_shape=jax.ShapeDtypeStruct(shape, jnp.float32),
            in_specs=[ANY],
            out_specs=VMEM,
            scratch_shapes=held_scratch(planes, shape) + [dma(wires), dma(wires), dma(planes)],
            compiler_params=params(7),
            name="scatter_rows",
        )(grads)

    def give(self, parcels, grads):
        planes, count = self.planes, len(grads)
        shapes = [g.shape[3:] for g in grads]
        wires = scatter_wires(planes, count) + spread_wires(planes)
        held = [s for shape in shapes for s in held_scratch(planes, shape)]
        layer = parcels.shape[1:]
        result = pl.pallas_call(
            functools.partial(give_kernel, planes, count),
            out_shape=[jax.ShapeDtypeStruct(layer, parcels.dtype)]
            + [jax.ShapeDtypeStruct(shape, jnp.float32) for shape in shapes],
            in_specs=[ANY] * (1 + count),
            out_specs=[ANY] + [VMEM] * count,
            scratch_shapes=held
            + [pltpu.VMEM(layer, parcels.dtype), pltpu.VMEM(layer, parcels.dtype)]
            + [dma(wires), dma(wires), dma(planes * count), dma(2)],
            compiler_params=params(8),
            name="give",
        )(parcels, *grads)
        return result[0], result[1:]

    def hand_back(self, parcels):
        planes = self.planes
        layer = parcels.shape[1:]
        wires = spread_wires(planes)
        return pl.pallas_call(
            functools.partial(return_kernel, planes),
            out_shape=jax.ShapeDtypeStruct(layer, parcels.dtype),
            in_specs=[ANY],
            out_specs=ANY,
            scratch_shapes=[pltpu.VMEM(layer, parcels.dtype), pltpu.VMEM(layer, parcels.dtype)]
            + [dma(wires), dma(wires), dma(2)],
            compiler_params=params(9),
            name="hand_back",
        )(parcels)


class Plain:
    def __init__(self, planes):
        self.planes = planes

    def ids(self, block):
        return lax.all_gather(block, "row")

    def gather(self, block):
        whole = lax.all_gather(block, ("head", "row"))
        return whole.reshape(4, self.planes, 2, *block.shape)

    def fetch(self, parcels, blocks):
        return self.deliver(parcels), [self.gather(b) for b in blocks]

    def deliver(self, parcels):
        shape = parcels.shape
        both = jnp.broadcast_to(parcels[:, :, None], (*shape[:2], 2, *shape[2:]))
        flat = both.reshape(8 * self.planes, *shape[2:])
        got = lax.all_to_all(flat, ("head", "row"), split_axis=0, concat_axis=0, tiled=True)
        return jnp.moveaxis(got.reshape(4, self.planes, 2, *shape[2:]), 2, 0)

    def rows(self, block):
        return self.gather(block)

    def small(self, block, number):
        return jnp.moveaxis(self.gather(block), 2, 0)

    def scatter_rows(self, grads):
        flat = grads.reshape(-1, grads.shape[-1]).astype(jnp.float32)
        return lax.psum_scatter(flat, ("head", "row"), scatter_dimension=0, tiled=True)

    def give(self, parcels, grads):
        return self.hand_back(parcels), [self.scatter_rows(g) for g in grads]

    def hand_back(self, parcels):
        shape = parcels.shape
        flat = jnp.moveaxis(parcels, 0, 2).reshape(8 * self.planes, *shape[3:])
        got = lax.all_to_all(flat, ("head", "row"), split_axis=0, concat_axis=0, tiled=True)
        got = got.reshape(4, self.planes, 2, *shape[3:]).astype(jnp.float32)
        return jnp.sum(got, axis=2).astype(parcels.dtype)


def contract(left, right, left_dim, right_dim):
    return lax.dot_general(
        left, right, (((left_dim,), (right_dim,)), ((), ())), preferred_element_type=jnp.float32
    )


def normalize(values, gain, shift):
    center = values - jnp.mean(values, axis=-1, keepdims=True)
    scale = lax.rsqrt(jnp.mean(center * center, axis=-1, keepdims=True) + EPSILON)
    unit = center * scale
    return (unit * gain + shift, unit, scale)


def normalize_back(grad, unit, scale, gain):
    inner = grad * gain
    back = scale * (
        inner
        - jnp.mean(inner, axis=-1, keepdims=True)
        - unit * jnp.mean(inner * unit, axis=-1, keepdims=True)
    )
    return (back, grad * unit)


def score_block(query, keys, labels):
    scores = jnp.einsum("qhe,khe->hqk", query, keys, preferred_element_type=jnp.float32) * HD ** (
        -0.5
    )
    allowed = labels[:, None] == labels[None, :]
    return jnp.where(allowed[None], scores, -1000000000.0)


def attend_fwd(query, keys, values, labels):
    scores = score_block(query, keys, labels)
    top = jnp.max(scores, axis=-1, keepdims=True)
    weights = jnp.exp(scores - top)
    total = jnp.sum(weights, axis=-1, keepdims=True)
    probs = weights / total
    output = jnp.einsum(
        "hqk,khe->qhe", probs.astype(jnp.bfloat16), values, preferred_element_type=jnp.float32
    )
    return (output, (top + jnp.log(total))[..., 0])


def attend_back(query, keys, values, labels, summary, grad_out):
    scores = score_block(query, keys, labels)
    probs = jnp.exp(scores - summary[..., None])
    grad_values = jnp.einsum(
        "hqk,qhe->khe", probs.astype(jnp.bfloat16), grad_out, preferred_element_type=jnp.float32
    )
    grad_probs = jnp.einsum("qhe,khe->hqk", grad_out, values, preferred_element_type=jnp.float32)
    grad_scores = probs * (grad_probs - jnp.sum(grad_probs * probs, axis=-1, keepdims=True))
    grad_low = grad_scores.astype(jnp.bfloat16)
    grad_query = jnp.einsum(
        "hqk,khe->qhe", grad_low, keys, preferred_element_type=jnp.float32
    ) * HD ** (-0.5)
    grad_keys = jnp.einsum(
        "hqk,qhe->khe", grad_low, query, preferred_element_type=jnp.float32
    ) * HD ** (-0.5)
    return jnp.stack([grad_query, grad_keys, grad_values], axis=2)


def adamw(weight, grad, first, second, decay, rate):
    first = BETA_ONE * first + (1 - BETA_ONE) * grad
    second = BETA_TWO * second + (1 - BETA_TWO) * grad * grad
    moved = first / (1 - BETA_ONE**STEP) / (jnp.sqrt(second / (1 - BETA_TWO**STEP)) + ADAM_EPSILON)
    return (weight - rate * (moved + decay * weight), first, second)


def padded(flat, rows, lanes):
    return jnp.pad(flat, (0, rows * lanes - flat.shape[0])).reshape(rows, lanes)


def on_device(
    token_ids,
    segment_ids,
    masked_pos,
    masked_target,
    embedding,
    position_table,
    qkv_weight,
    out_weight,
    up_weight,
    down_weight,
    norm_params,
    up_bias,
    m_embedding,
    m_position,
    m_qkv,
    m_out,
    m_up,
    m_down,
    m_norm,
    m_bias,
    v_embedding,
    v_position,
    v_qkv,
    v_out,
    v_up,
    v_down,
    v_norm,
    v_bias,
):
    low = jnp.bfloat16
    row_count = lax.axis_size("row")
    devices = HEADS * row_count
    planes = row_count // 2
    wire = Kernels(planes) if planes <= 4 else Plain(planes)
    head = lax.axis_index("head")
    row = lax.axis_index("row")
    core = row % 2
    device = head * row_count + row
    vocab_part, width = embedding.shape
    tokens = token_ids.shape[0] // HEADS
    inner = up_weight.shape[1] * devices

    labels_all = segment_ids.reshape(HEADS, tokens)
    slots = masked_pos.shape[1] // HEADS
    live = labels_at(segment_ids, masked_pos[0])
    target = jnp.where(live, masked_target[0], -1)
    words = token_ids.shape[0] + target.shape[0]
    lines = -(-words // 1024) * 8
    numbers = wire.ids(padded(jnp.concatenate([token_ids, target]), lines, 128))
    numbers = numbers.reshape(row_count, lines * 128)
    ids = numbers[:, : token_ids.shape[0]].reshape(planes, 2, HEADS, tokens)
    ids = ids.transpose(2, 0, 1, 3).reshape(HEADS * planes, 2 * tokens)
    targets = numbers[:, token_ids.shape[0] : words].reshape(row_count, HEADS, slots)
    targets = targets.transpose(1, 0, 2).reshape(-1)

    owner = ids // vocab_part
    counts = jnp.sum(owner[:, :, None] == jnp.arange(devices), axis=1)
    rounds = -(-jnp.max(counts) // ROOM)
    inside = owner == device
    order = jnp.arange(2 * tokens)
    before = (order[:, None] < order[None, :]).astype(low)
    rank = jnp.dot(inside.astype(low), before, preferred_element_type=jnp.float32).astype(jnp.int32)
    rank = jnp.where(inside, rank, -1)
    local = ids - device * vocab_part
    chip = head * planes + row // 2
    own_owner = lax.dynamic_index_in_dim(owner, chip, 0, keepdims=False)
    own_marks = own_owner[:, None] == jnp.arange(devices)
    own_before = contract(before, own_marks.astype(low), 0, 0).astype(jnp.int32)
    own_rank = jnp.sum(jnp.where(own_marks, own_before, 0), axis=1)
    own_owner = lax.dynamic_slice_in_dim(own_owner, core * tokens, tokens, 0)
    own_rank = lax.dynamic_slice_in_dim(own_rank, core * tokens, tokens, 0)
    own_home = (own_owner % 2) * (devices // 2) + own_owner // 2
    table = embedding.astype(low)

    def parcel_marks(turn):
        spot = jnp.arange(ROOM) + turn * ROOM
        hit = rank[:, None, :] == spot[None, :, None]
        which = jnp.sum(jnp.where(hit, local[:, None, :] + 1, 0), axis=2) - 1
        marks = which.reshape(-1)[:, None] == jnp.arange(vocab_part)[None, :]
        return marks.astype(low)

    def token_marks(turn):
        seat = own_rank - turn * ROOM
        seat = jnp.where((seat >= 0) & (seat < ROOM), own_home * ROOM + seat, -1)
        return (seat[:, None] == jnp.arange(devices * ROOM)[None, :]).astype(low)

    def parcels_of(turn):
        picked = jnp.dot(parcel_marks(turn), table, preferred_element_type=jnp.float32)
        return picked.astype(low).reshape(HEADS, planes, ROOM, width)

    def opened(parcels, turn):
        return jnp.dot(
            token_marks(turn),
            parcels.reshape(devices * ROOM, width),
            preferred_element_type=jnp.float32,
        )

    share = width // devices
    share_inner = inner // devices
    misc = jnp.concatenate(
        [
            out_weight.T.reshape(-1),
            position_table.T.reshape(-1),
            norm_params.reshape(-1),
            up_bias,
        ]
    ).astype(low)
    misc_rows = -(-misc.shape[0] // (16 * width)) * 16
    parcels, gathered = wire.fetch(
        parcels_of(0),
        [
            padded(misc, misc_rows, width),
            qkv_weight.astype(low),
            up_weight.T.astype(low),
            down_weight.astype(low),
        ],
    )
    looked = opened(parcels, 0)

    def again(state):
        turn, so_far = state
        return turn + 1, so_far + opened(wire.deliver(parcels_of(turn)), turn)

    _, looked = lax.while_loop(lambda state: state[0] < rounds, again, (jnp.int32(1), looked))

    misc_all = gathered[0].reshape(devices, misc_rows * width)
    qkv_full = gathered[1].reshape(HEADS, width, qkv_weight.shape[1])
    up_full = gathered[2].reshape(inner, width)
    down_full = gathered[3].reshape(inner, width)
    cuts = [share * width, share * SEQ, share * 8, share_inner]
    starts = [sum(cuts[:i]) for i in range(5)]
    pieces = [misc_all[:, starts[i] : starts[i + 1]] for i in range(4)]
    out_full = pieces[0].reshape(width, width)
    places = pieces[1].reshape(width, SEQ).T
    norms = pieces[2].reshape(devices, 8, share).transpose(1, 0, 2).reshape(8, width)
    norms = norms.astype(jnp.float32)
    bias = pieces[3].reshape(inner).astype(jnp.float32)

    labels = lax.dynamic_index_in_dim(labels_all, head, 0, keepdims=False)
    start_sum = looked + places.astype(jnp.float32)
    normed, unit_zero, scale_zero = normalize(start_sum, norms[0], norms[1])
    normed_low = normed.astype(low)
    mixed = jnp.einsum("td,hdj->thj", normed_low, qkv_full, preferred_element_type=jnp.float32)
    mixed = mixed.astype(low).reshape(tokens, -1, 3, HD)
    heads = mixed.shape[1]
    query, keys, values = (mixed[:, :, 0], mixed[:, :, 1], mixed[:, :, 2])
    attended, summary = attend_fwd(query, keys, values, labels)
    head_ramp = jnp.where(jnp.arange(heads) < OLD_HEADS, 1.0, STEP / RAMP).astype(jnp.float32)
    heads_low = (attended * head_ramp[:, None]).astype(low).reshape(tokens, heads * HD)
    projected = contract(heads_low, out_full, 1, 1)
    hidden, unit_one, scale_one = normalize(normed + projected + norms[6], norms[2], norms[3])
    hidden_low = hidden.astype(low)
    upper = contract(hidden_low, up_full, 1, 1) + bias
    neuron_ramp = jnp.where(jnp.arange(inner) < OLD_FF, 1.0, STEP / RAMP).astype(jnp.float32)
    activated, gelu_pull = jax.vjp(
        lambda u: jax.nn.gelu(u, approximate=False) * neuron_ramp, upper
    )
    active_low = activated.astype(low)
    lowered = jnp.dot(active_low, down_full, preferred_element_type=jnp.float32) + norms[7]
    final, unit_two, scale_two = normalize(hidden + lowered, norms[4], norms[5])

    chosen = lax.dynamic_slice_in_dim(masked_pos[0], head * slots, slots, 0) - head * tokens
    chosen_marks = chosen[:, None] == jnp.arange(tokens)[None, :]
    picked = jnp.dot(chosen_marks.astype(low), final.astype(low), preferred_element_type=jnp.float32)
    all_rows = wire.rows(picked.astype(low)).reshape(devices * slots, width)
    valid = (targets >= 0).astype(jnp.float32)
    logits = contract(all_rows, table, 1, 1)
    hits = jnp.arange(vocab_part)[None, :] == (targets - device * vocab_part)[:, None]
    top = jnp.max(logits, axis=1)
    part = top + jnp.log(jnp.sum(jnp.exp(logits - top[:, None]), axis=1))
    parts = wire.small(part.reshape(-1, 128), 5).reshape(devices, -1)
    peak = jnp.max(parts, axis=0)
    log_total = peak + jnp.log(jnp.sum(jnp.exp(parts - peak), axis=0))
    target_part = jnp.sum(jnp.where(hits, logits, 0.0))
    log_own = lax.dynamic_slice_in_dim(log_total * valid, device * slots, slots, 0)
    valid_own = lax.dynamic_slice_in_dim(valid, device * slots, slots, 0)
    loss_own = jnp.sum(log_own) - target_part
    count_own = jnp.sum(valid_own)
    grad_logits = (
        valid[:, None] * (jnp.exp(logits - log_total[:, None]) - hits.astype(jnp.float32))
    ).astype(low)
    grad_table = contract(grad_logits, all_rows, 0, 0)
    grad_rows = jnp.dot(grad_logits, table, preferred_element_type=jnp.float32).astype(low)
    grad_picked = wire.scatter_rows(grad_rows.reshape(HEADS, planes, 2, slots, width))

    grad_final = lax.dot_general(
        chosen_marks.astype(jnp.float32),
        grad_picked,
        (((0,), (0,)), ((), ())),
        precision=lax.Precision.HIGHEST,
    )
    grad_sum, gain_two = normalize_back(grad_final, unit_two, scale_two, norms[4])
    grad_sum_low = grad_sum.astype(low)
    grad_down = contract(active_low, grad_sum_low, 0, 0)
    grad_upper = gelu_pull(contract(grad_sum_low, down_full, 1, 1))[0]
    grad_upper_low = grad_upper.astype(low)
    grad_up = contract(grad_upper_low, hidden_low, 0, 0)
    grad_hidden = grad_sum + jnp.dot(grad_upper_low, up_full, preferred_element_type=jnp.float32)
    grad_res, gain_one = normalize_back(grad_hidden, unit_one, scale_one, norms[2])
    grad_res_low = grad_res.astype(low)
    grad_out = contract(grad_res_low, heads_low, 0, 0)
    grad_heads = jnp.dot(grad_res_low, out_full, preferred_element_type=jnp.float32).astype(low)
    grad_attended = (
        grad_heads.reshape(tokens, heads, HD).astype(jnp.float32) * head_ramp[:, None]
    ).astype(low)
    grad_mixed = attend_back(query, keys, values, labels, summary, grad_attended)
    grad_mixed_low = grad_mixed.astype(low).reshape(tokens, HEADS, -1)
    grad_qkv = jnp.einsum(
        "td,thj->hdj", normed_low, grad_mixed_low, preferred_element_type=jnp.float32
    )
    grad_normed = grad_res + jnp.einsum(
        "thj,hdj->td", grad_mixed_low, qkv_full, preferred_element_type=jnp.float32
    )
    grad_start, gain_zero = normalize_back(grad_normed, unit_zero, scale_zero, norms[0])
    grad_start_low = grad_start.astype(low)
    grad_norms = jnp.stack(
        [
            jnp.sum(gain_zero, axis=0),
            jnp.sum(grad_normed, axis=0),
            jnp.sum(gain_one, axis=0),
            jnp.sum(grad_hidden, axis=0),
            jnp.sum(gain_two, axis=0),
            jnp.sum(grad_final, axis=0),
            jnp.sum(grad_res, axis=0),
            jnp.sum(grad_sum, axis=0),
        ]
    )
    grad_bias = jnp.sum(grad_upper, axis=0)

    def parcels_back(turn):
        back = contract(token_marks(turn), grad_start_low, 0, 0).astype(low)
        return back.reshape(2, HEADS, planes, ROOM, width)

    def unpacked(parcels, turn):
        return contract(parcel_marks(turn), parcels.reshape(-1, width), 0, 0)

    grad_misc = jnp.concatenate(
        [
            grad_out.reshape(devices, -1),
            grad_start.T.reshape(devices, -1),
            grad_norms.reshape(8, devices, share).transpose(1, 0, 2).reshape(devices, -1),
            grad_bias.reshape(devices, -1),
        ],
        axis=1,
    ).astype(low)
    grad_misc = jnp.pad(grad_misc, ((0, 0), (0, misc_rows * width - grad_misc.shape[1])))
    parcels, summed = wire.give(
        parcels_back(0),
        [
            grad_misc.reshape(HEADS, planes, 2, misc_rows, width),
            grad_qkv.astype(low).reshape(HEADS, planes, 2, *qkv_weight.shape),
            grad_up.astype(low).reshape(HEADS, planes, 2, share_inner, width),
            grad_down.astype(low).reshape(HEADS, planes, 2, share_inner, width),
        ],
    )
    grad_table = grad_table + unpacked(parcels, 0)

    def again_back(state):
        turn, so_far = state
        return turn + 1, so_far + unpacked(wire.hand_back(parcels_back(turn)), turn)

    _, grad_table = lax.while_loop(
        lambda state: state[0] < rounds, again_back, (jnp.int32(1), grad_table)
    )
    misc_sum = summed[0].reshape(-1)
    grads = (
        grad_table,
        misc_sum[starts[1] : starts[2]].reshape(share, SEQ).T,
        summed[1],
        misc_sum[starts[0] : starts[1]].reshape(share, width).T,
        summed[2].T,
        summed[3],
        misc_sum[starts[2] : starts[3]].reshape(8, share),
        misc_sum[starts[3] : starts[4]],
    )
    squares = sum((jnp.sum(g * g) for g in grads))
    scalars = padded(jnp.stack([squares, loss_own, count_own]), 8, 128)
    scalars = jnp.sum(wire.small(scalars, 6).reshape(devices, 8, 128)[:, 0, :3], axis=0)
    squares, loss_sum, live_count = scalars[0], scalars[1], scalars[2]
    grad_norm = jnp.sqrt(squares) / live_count
    factor = jnp.minimum(1.0, CLIP / grad_norm) / live_count
    weights = (
        embedding,
        position_table,
        qkv_weight,
        out_weight,
        up_weight,
        down_weight,
        norm_params,
        up_bias,
    )
    firsts = (m_embedding, m_position, m_qkv, m_out, m_up, m_down, m_norm, m_bias)
    seconds = (v_embedding, v_position, v_qkv, v_out, v_up, v_down, v_norm, v_bias)
    decays = (DECAY,) * 6 + (0.0, 0.0)
    rates = (LEARN_RATE,) * 6 + (GAIN_RATE,) * 2
    results = [
        adamw(w, g * factor, m, v, d, r)
        for w, g, m, v, d, r in zip(weights, grads, firsts, seconds, decays, rates)
    ]
    return (
        *(r[0] for r in results),
        *(r[1] for r in results),
        *(r[2] for r in results),
        loss_sum,
        live_count,
        grad_norm,
    )


def labels_at(segment_ids, positions):
    at = positions[:, None] == jnp.arange(segment_ids.shape[0])[None, :]
    return jnp.sum(jnp.where(at, segment_ids[None, :], 0), axis=1) != SEQ - 1


def solution(mesh):
    vocab = P(("head", "row"), None)
    columns = P(None, ("head", "row"))
    flat = P(("head", "row"))
    weights = (vocab, columns, P("row", "head"), columns, columns, vocab, columns, flat)
    data = (P("row"), P("row"), P("row", None), P("row", None))
    return jax.shard_map(
        on_device,
        mesh=mesh,
        in_specs=(*data, *weights, *weights, *weights),
        out_specs=(*weights, *weights, *weights, P(), P(), P()),
        check_vma=False,
    )
```

```python
import functools

import jax
import jax.numpy as jnp
from jax import lax
from jax.experimental import pallas as pl
from jax.experimental.pallas import tpu as pltpu
from jax.sharding import PartitionSpec as P

HD = 64
SEQ = 512
STEP = 5
RAMP = 10
OLD_HEADS = 8
OLD_FF = 2048


EPSILON = 1e-05
LEARN_RATE = 0.03
GAIN_RATE = 0.5
BETA_ONE = 0.9
BETA_TWO = 0.999
ADAM_EPSILON = 1e-08
DECAY = 0.01
CLIP = 0.02

ROOM = 64
HEADS = 4
MESH = pl.DeviceIdType.MESH
ANY = pl.BlockSpec(memory_space=pl.ANY)
VMEM = pl.BlockSpec(memory_space=pltpu.VMEM)


def place():
    h = lax.axis_index("head")
    r = lax.axis_index("row")
    return h, lax.div(r, 2), lax.rem(r, 2)


def across(h, q):
    if q == 0:
        return h
    if q == 1:
        return h + 1 - 2 * lax.rem(h, 2)
    if q == 2:
        return lax.rem(h + 2, 4)
    return 3 - h


class Wires:
    def __init__(self, send, recv):
        self.send, self.recv, self.used, self.made = send, recv, 0, []

    def copy(self, src, dst, to):
        i = self.used
        self.used += 1
        one = pltpu.make_async_remote_copy(
            src_ref=src,
            dst_ref=dst,
            send_sem=self.send.at[i],
            recv_sem=self.recv.at[i],
            device_id=to,
            device_id_type=MESH,
        )
        one.start()
        self.made.append(one)
        return one

    def sent(self):
        for one in self.made:
            one.wait_send()


def greet(peers):
    barrier = pltpu.get_barrier_semaphore()
    for to in peers:
        pl.semaphore_signal(barrier, inc=1, device_id=to, device_id_type=MESH)
    pl.semaphore_wait(barrier, len(peers))


def near(planes):
    h, z, c = place()
    peers = [(h, 2 * z + 1 - c), (across(h, 1), 2 * z + c), (across(h, 2), 2 * z + c)]
    peers += [(h, 2 * lax.rem(z + s, planes) + c) for s in range(1, planes)]
    return peers


def every_chip(planes):
    h, z, c = place()
    peers = [(h, 2 * z + 1 - c)]
    for q in range(4):
        for s in range(planes):
            if q or s:
                peers.append((across(h, q), 2 * lax.rem(z + s, planes) + c))
    return peers


def split(rows):
    first = -(-rows // 32) * 16
    return pl.ds(0, first), pl.ds(first, rows - first)


def gather_steps(wires, local, planes, pairs):
    h, z, c = place()
    row = 2 * z + c
    sib = (h, 2 * z + 1 - c)
    hx, hy, hd = across(h, 1), across(h, 2), across(h, 3)
    xn, yn = (hx, row), (hy, row)
    zs = [lax.rem(z - s + planes, planes) for s in range(planes)]
    count = len(pairs)
    here = []
    for k, (x, out) in enumerate(pairs):
        one = pltpu.make_async_copy(x, out.at[h, z, c], local.at[k])
        one.start()
        here.append(one)
    from_z = {}
    for k, (x, out) in enumerate(pairs):
        for s in range(1, planes):
            from_z[k, s] = wires.copy(x, out.at[h, z, c], (h, 2 * lax.rem(z + s, planes) + c))
    from_x, from_y, from_xd, from_yd, from_sib = {}, {}, {}, {}, []

    def launch(k, s):
        x, out = pairs[k]
        src = x if s == 0 else out.at[h, zs[s], c]
        if s:
            from_z[k, s].wait_recv()
        dst = out.at[h, zs[s], c]
        from_x[k, s] = wires.copy(src, dst, xn)
        from_y[k, s] = wires.copy(src, dst, yn)
        from_sib.append(wires.copy(src, dst, sib))

    def relay(k, s):
        _, out = pairs[k]
        first, second = split(out.shape[3])
        from_x[k, s].wait_recv()
        got = out.at[hx, zs[s], c]
        from_yd[k, s] = wires.copy(got.at[second], got.at[second], yn)
        from_sib.append(wires.copy(got, got, sib))
        from_y[k, s].wait_recv()
        got = out.at[hy, zs[s], c]
        from_xd[k, s] = wires.copy(got.at[first], got.at[first], xn)
        from_sib.append(wires.copy(got, got, sib))

    def finish(k, s):
        _, out = pairs[k]
        from_yd[k, s].wait_recv()
        from_xd[k, s].wait_recv()
        got = out.at[hd, zs[s], c]
        from_sib.append(wires.copy(got, got, sib))

    order = [(k, s) for k in range(count) for s in range(planes)]
    for i in range(len(order) + 2):
        if i < len(order):
            launch(*order[i])
        if 1 <= i <= len(order):
            relay(*order[i - 1])
        if i >= 2:
            finish(*order[i - 2])
    for one in from_sib:
        one.wait_recv()
    for one in here:
        one.wait()


def spread_start(wires, local, planes, parcels, out):
    h, z, c = place()
    sib = (h, 2 * z + 1 - c)
    got = {}
    for q in range(4):
        for s in range(planes):
            if q or s:
                th, tz = across(h, q), lax.rem(z + s, planes)
                got[q, s] = wires.copy(parcels(th, tz), out.at[c, h, z], (th, 2 * tz + c))
    mine = pltpu.make_async_copy(parcels(h, z), out.at[c, h, z], local)
    mine.start()
    passed = [wires.copy(parcels(h, z), out.at[c, h, z], sib)]
    return got, mine, passed


def spread_finish(wires, planes, out, state):
    h, z, c = place()
    sib = (h, 2 * z + 1 - c)
    got, mine, passed = state
    for (q, s), one in got.items():
        one.wait_recv()
        there = out.at[c, across(h, q), lax.rem(z - s + planes, planes)]
        passed.append(wires.copy(there, there, sib))
    for one in passed:
        one.wait_recv()
    mine.wait()


def small_kernel(planes, x, out, send, recv, local):
    greet(every_chip(planes))
    wires = Wires(send, recv)
    state = spread_start(wires, local, planes, lambda h, z: x, out)
    spread_finish(wires, planes, out, state)
    wires.sent()


def ids_kernel(planes, x, small, out, small_out, send, recv, local):
    h, z, c = place()
    offsets = [(s, e) for s in range(planes) for e in range(2) if s or e]
    peers = [(h, 2 * lax.rem(z + s, planes) + lax.rem(c + e, 2)) for s, e in offsets]
    chips = [(across(h, q), 2 * lax.rem(z + s, planes) + c) for q in (1, 2, 3) for s in range(planes)]
    greet(peers + chips)
    wires = Wires(send, recv)
    mine = pltpu.make_async_copy(x, out.at[2 * z + c], local.at[0])
    mine.start()
    ids = [wires.copy(x, out.at[2 * z + c], to) for to in peers]
    state = spread_start(wires, local.at[1], planes, lambda th, tz: small, small_out)
    spread_finish(wires, planes, small_out, state)
    for one in ids:
        one.wait_recv()
    mine.wait()
    wires.sent()


def gather_kernel(planes, count, *refs):
    xs, outs = refs[:count], refs[count : 2 * count]
    send, recv, local = refs[2 * count :]
    greet(near(planes))
    wires = Wires(send, recv)
    gather_steps(wires, local, planes, list(zip(xs, outs)))
    wires.sent()


def deliver_kernel(planes, parcels, out, send, recv, local):
    greet(every_chip(planes))
    wires = Wires(send, recv)
    state = spread_start(wires, local, planes, lambda h, z: parcels.at[h, z], out)
    spread_finish(wires, planes, out, state)
    wires.sent()


def add_rows(target, others, rows):
    @pl.loop(0, rows // 16)
    def _(i):
        at = pl.ds(pl.multiple_of(i * 16, 16), 16)
        total = target[at, :].astype(jnp.float32)
        for other in others:
            total = total + other[at, :].astype(jnp.float32)
        target[at, :] = total.astype(target.dtype)


def scatter_steps(wires, local, planes, groups):
    h, z, c = place()
    row = 2 * z + c
    sib = (h, 2 * z + 1 - c)
    hx, hy, hd = across(h, 1), across(h, 2), across(h, 3)
    xn, yn = (hx, row), (hy, row)
    zs = [lax.rem(z + 1 + s, planes) for s in range(planes)]
    order = [(k, s) for k in range(len(groups)) for s in range(planes)]
    from_sib, loads = {}, {}
    for i, (k, s) in enumerate(order):
        grads, out, own, sibs, px, pz = groups[k]
        for q in (3, 1, 2, 0):
            th = across(h, q)
            from_sib[k, s, q] = wires.copy(grads.at[th, zs[s], 1 - c], sibs.at[th, zs[s]], sib)
        loads[k, s] = pltpu.make_async_copy(grads.at[:, zs[s], c], own.at[:, zs[s]], local.at[i])
        loads[k, s].start()
    first, second, from_z = {}, {}, {}

    def pair(k, s):
        grads, out, own, sibs, px, pz = groups[k]
        a, b = split(own.shape[2])
        loads[k, s].wait()
        for q in (3, 1, 2, 0):
            from_sib[k, s, q].wait_recv()
            th = across(h, q)
            add_rows(own.at[th, zs[s]], [sibs.at[th, zs[s]]], own.shape[2])
            if q == 3:
                first[k, s, "xd"] = wires.copy(
                    own.at[hd, zs[s]].at[a], px.at[zs[s], 0].at[a], xn
                )
                first[k, s, "yd"] = wires.copy(
                    own.at[hd, zs[s]].at[b], px.at[zs[s], 0].at[b], yn
                )
            if q == 1:
                first[k, s, "x"] = wires.copy(own.at[hx, zs[s]].at[a], px.at[zs[s], 1].at[a], xn)
            if q == 2:
                first[k, s, "y"] = wires.copy(own.at[hy, zs[s]].at[b], px.at[zs[s], 1].at[b], yn)

    def plane(k, s):
        grads, out, own, sibs, px, pz = groups[k]
        a, b = split(own.shape[2])
        first[k, s, "xd"].wait_recv()
        add_rows(own.at[hy, zs[s]].at[a], [px.at[zs[s], 0].at[a]], a.size)
        second[k, s, "y"] = wires.copy(own.at[hy, zs[s]].at[a], px.at[zs[s], 2].at[a], yn)
        first[k, s, "yd"].wait_recv()
        add_rows(own.at[hx, zs[s]].at[b], [px.at[zs[s], 0].at[b]], b.size)
        second[k, s, "x"] = wires.copy(own.at[hx, zs[s]].at[b], px.at[zs[s], 2].at[b], xn)

    def line(k, s):
        grads, out, own, sibs, px, pz = groups[k]
        for part in ("x", "y"):
            first[k, s, part].wait_recv()
            second[k, s, part].wait_recv()
        add_rows(own.at[h, zs[s]], [px.at[zs[s], 1], px.at[zs[s], 2]], own.shape[2])
        if s < planes - 1:
            from_z[k, s] = wires.copy(own.at[h, zs[s]], pz.at[s], (h, 2 * zs[s] + c))

    def total(k):
        grads, out, own, sibs, px, pz = groups[k]
        for s in range(planes - 1):
            from_z[k, s].wait_recv()

        @pl.loop(0, out.shape[0] // 16)
        def _(i):
            at = pl.ds(pl.multiple_of(i * 16, 16), 16)
            value = own[h, z, at, :].astype(jnp.float32)
            for s in range(planes - 1):
                value = value + pz[s, at, :].astype(jnp.float32)
            out[at, :] = value

    for i in range(len(order) + 2):
        if i < len(order):
            pair(*order[i])
        if 1 <= i <= len(order):
            plane(*order[i - 1])
        if i >= 2:
            line(*order[i - 2])
    for k in range(len(groups)):
        total(k)


def scatter_kernel(planes, count, *refs):
    grads, outs = refs[:count], refs[count : 2 * count]
    held = refs[2 * count : 2 * count + 4 * count]
    send, recv, local = refs[6 * count :]
    greet(near(planes))
    wires = Wires(send, recv)
    groups = [(grads[k], outs[k], *held[4 * k : 4 * k + 4]) for k in range(count)]
    scatter_steps(wires, local, planes, groups)
    wires.sent()


def give_kernel(planes, count, *refs):
    parcels, grads = refs[0], refs[1 : 1 + count]
    out, outs = refs[1 + count], refs[2 + count : 2 + 2 * count]
    held = refs[2 + 2 * count : 2 + 6 * count]
    mine, other, send, recv, local, extra = refs[2 + 6 * count :]
    greet(every_chip(planes))
    wires = Wires(send, recv)
    give_steps(wires, extra, planes, parcels, out, mine, other)
    groups = [(grads[k], outs[k], *held[4 * k : 4 * k + 4]) for k in range(count)]
    scatter_steps(wires, local, planes, groups)
    for one in wires.given:
        one.wait_recv()
    wires.sent()


def give_steps(wires, local, planes, parcels, out, mine, other):
    h, z, c = place()
    sib = (h, 2 * z + 1 - c)
    passed = wires.copy(parcels.at[1 - c], other, sib)
    load = pltpu.make_async_copy(parcels.at[c], mine, local.at[0])
    load.start()
    load.wait()
    passed.wait_recv()
    wires.given = []
    for q in (3, 1, 2, 0):
        for s in range(planes - 1, -1, -1):
            th, tz = across(h, q), lax.rem(z + s, planes)
            add_rows(mine.at[th, tz], [other.at[th, tz]], mine.shape[2])
            if q or s:
                wires.given.append(
                    wires.copy(mine.at[th, tz], out.at[h, z], (th, 2 * tz + c))
                )
    keep = pltpu.make_async_copy(mine.at[h, z], out.at[h, z], local.at[1])
    keep.start()
    keep.wait()


def return_kernel(planes, parcels, out, mine, other, send, recv, extra):
    greet(every_chip(planes))
    wires = Wires(send, recv)
    give_steps(wires, extra, planes, parcels, out, mine, other)
    for one in wires.given:
        one.wait_recv()
    wires.sent()


def guarded(ok, act):
    if ok is None:
        act()
    else:
        pl.when(ok)(act)


class Lines:
    def __init__(self, send, recv):
        self.send, self.recv, self.used, self.made = send, recv, 0, []

    def make(self, src, dst, to, ok):
        i = self.used
        self.used += 1
        one = pltpu.make_async_remote_copy(
            src_ref=src,
            dst_ref=dst,
            send_sem=self.send.at[i],
            recv_sem=self.recv.at[i],
            device_id=to,
            device_id_type=MESH,
        )
        self.made.append((one, ok))
        return one

    def sent(self):
        for one, ok in self.made:
            guarded(ok, one.wait_send)


def line_steps(planes):
    return [0] + [d * s for s in range(1, planes) for d in (1, -1)]


class Gather:
    def __init__(self, wires, local, planes, pairs):
        self.wires, self.planes, self.pairs = wires, planes, pairs
        h, z, c = place()
        self.h, self.z, self.c = h, z, c
        row = 2 * z + c
        self.sib = (h, 2 * z + 1 - c)
        self.hx, self.hy, self.hd = across(h, 1), across(h, 2), across(h, 3)
        self.xn, self.yn = (self.hx, row), (self.hy, row)
        self.at, self.have, self.on = {0: z}, {0: None}, {}
        for s in line_steps(planes)[1:]:
            t = z - s
            self.have[s] = (t >= 0) & (t < planes)
            self.at[s] = jnp.clip(t, 0, planes - 1)
        for s in range(planes - 1):
            for d in (1, -1):
                u = z + d
                ok = (u >= 0) & (u < planes)
                self.on[d, s] = (ok & self.have[d * s]) if s else ok
        self.here = []
        for k, (x, out) in enumerate(pairs):
            one = pltpu.make_async_copy(x, out.at[h, z, c], local.at[k])
            one.start()
            self.here.append(one)
        self.line, self.copies = {}, {}

    def onward(self, k, d, s):
        x, out = self.pairs[k]
        t = self.at[d * s]
        ref = x if s == 0 else out.at[self.h, t, self.c]
        u = jnp.clip(self.z + d, 0, self.planes - 1)
        ok = self.on[d, s]
        one = self.wires.make(ref, out.at[self.h, t, self.c], (self.h, 2 * u + self.c), ok)
        self.line[k, d, s] = one
        guarded(ok, one.start)

    def launch(self, k, s):
        x, out = self.pairs[k]
        t, ok = self.at[s], self.have[s]
        here = out.at[self.h, t, self.c]
        ref = x if s == 0 else here
        if s == 0:
            self.onward(k, 1, 0)
            self.onward(k, -1, 0)
        else:
            d, a = (1, s) if s > 0 else (-1, -s)
            guarded(ok, self.line[k, d, a - 1].wait_recv)
            if a < self.planes - 1:
                self.onward(k, d, a)
        make = self.wires.make
        ones = [make(ref, here, to, ok) for to in (self.xn, self.yn, self.sib)]
        self.copies[k, s, "x"], self.copies[k, s, "y"], self.copies[k, s, "s"] = ones

        def act():
            for one in ones:
                one.start()

        guarded(ok, act)

    def relay(self, k, s):
        out = self.pairs[k][1]
        t, ok = self.at[s], self.have[s]
        first, second = split(out.shape[3])
        make, got = self.wires.make, self.copies
        gx, gy = out.at[self.hx, t, self.c], out.at[self.hy, t, self.c]
        got[k, s, "yd"] = make(gx.at[second], gx.at[second], self.yn, ok)
        got[k, s, "sx"] = make(gx, gx, self.sib, ok)
        got[k, s, "xd"] = make(gy.at[first], gy.at[first], self.xn, ok)
        got[k, s, "sy"] = make(gy, gy, self.sib, ok)

        def act():
            got[k, s, "x"].wait_recv()
            got[k, s, "yd"].start()
            got[k, s, "sx"].start()
            got[k, s, "y"].wait_recv()
            got[k, s, "xd"].start()
            got[k, s, "sy"].start()

        guarded(ok, act)

    def finish(self, k, s):
        out = self.pairs[k][1]
        t, ok = self.at[s], self.have[s]
        got = self.copies
        gd = out.at[self.hd, t, self.c]
        got[k, s, "sd"] = self.wires.make(gd, gd, self.sib, ok)

        def act():
            got[k, s, "yd"].wait_recv()
            got[k, s, "xd"].wait_recv()
            got[k, s, "sd"].start()

        guarded(ok, act)

    def done(self, k, s):
        if s == 0:
            self.here[k].wait()

        def act():
            for part in ("s", "sx", "sy", "sd"):
                self.copies[k, s, part].wait_recv()

        guarded(self.have[s], act)


def line_wires(planes, count):
    return count * (2 * planes - 1) * 9


def mul(left, right, left_dim=1, right_dim=0):
    return lax.dot_general(
        left, right, (((left_dim,), (right_dim,)), ((), ())), preferred_element_type=jnp.float32
    )


def unit_of(values):
    center = values - jnp.mean(values, axis=-1, keepdims=True)
    scale = lax.rsqrt(jnp.mean(center * center, axis=-1, keepdims=True) + EPSILON)
    return center * scale, scale


ERF_TOP = (
    -2.72614225801306e-10,
    2.77068142495902e-08,
    -2.10102402082508e-06,
    -5.69250639462346e-05,
    -7.34990630326855e-04,
    -2.95459980854025e-03,
    -1.60960333262415e-02,
)
ERF_LOW = (
    -1.45660718464996e-05,
    -2.13374055278905e-04,
    -1.68282697438203e-03,
    -7.37332916720468e-03,
    -1.42647390514189e-02,
)


def erf(x):
    x = jnp.clip(x, -4.0, 4.0)
    square = x * x
    top = jnp.full_like(x, ERF_TOP[0])
    for c in ERF_TOP[1:]:
        top = top * square + c
    bottom = jnp.full_like(x, ERF_LOW[0])
    for c in ERF_LOW[1:]:
        bottom = bottom * square + c
    return x * top / bottom


def gelu_parts(u, ramp):
    cdf = 0.5 + 0.5 * erf(u * (0.5**0.5))
    density = jnp.exp(-0.5 * u * u) * 0.3989422804014327
    return u * cdf * ramp, (cdf + u * density) * ramp


def head_slice(ref, head, part):
    group, i = head // 3, head % 3
    start = (3 * i + part) * HD
    return ref[group, :, start : start + HD]


def masked_scores(q, k, labels_col, labels_row):
    s = mul(q, k, 1, 1) * HD**-0.5
    return jnp.where(labels_col == labels_row, s, -1000000000.0)


def forward_kernel(planes, room, *refs):
    (parcels, misc, wq, wu, wd, home, extra, lab_col, lab_row, norms, bias, ramp, chosen) = refs[:13]
    (misc_all, wq_all, wu_all, wd_all) = refs[13:17]
    (unit0, scale0, mixed, lse, heads, unit1, scale1, active, slope, unit2, scale2, picked) = refs[
        17:29
    ]
    (box, misc_v, wq_v, wu_v, wd_v, hidden, total) = refs[29:36]
    send, recv, local, send2, recv2, loads = refs[36:]
    low = jnp.bfloat16
    h, z, c = place()
    greet(every_chip(planes))
    lines = Lines(send, recv)
    posts = Wires(send2, recv2)
    pairs = [(misc, misc_all), (wq, wq_all), (wu, wu_all), (wd, wd_all)]
    gather = Gather(lines, local, planes, pairs)
    tokens, width = unit0.shape
    state = {}

    def post():
        state["post"] = spread_start(posts, local.at[4], planes, lambda th, tz: parcels.at[th, tz], box)

    def opened():
        spread_finish(posts, planes, box, state["post"])

    def load(k, view):
        ones = []
        for t in range(planes):
            one = pltpu.make_async_copy(
                pairs[k][1].at[:, t], view.at[:, t], loads.at[k * planes + t]
            )
            one.start()
            ones.append(one)
        return ones

    def wait(ones):
        for one in ones:
            one.wait()

    def start_norm():
        wait(load(0, misc_v))
        spots = lax.broadcasted_iota(jnp.int32, (tokens, box.shape[3] * 8 * planes), 1)
        marks = (home[...] == spots).astype(jnp.float32).astype(low)
        rows = box[...].reshape(-1, width)
        looked = mul(marks, rows) + extra[...]
        pieces = misc_v[...].astype(jnp.float32)
        share = misc_v.shape[3] // 2
        places = pieces[:, :, :, share:, :SEQ].reshape(width, SEQ).T
        unit, scale = unit_of(looked + places)
        unit0[...] = unit
        scale0[...] = scale
        hidden[...] = unit * norms[0:1, :] + norms[1:2, :]

    def project(group):
        weight = wq_v[group].reshape(width, wq_v.shape[4])
        mixed[group] = mul(hidden[...].astype(low), weight).astype(low)

    def attend(pair):
        outs = []
        for head in (2 * pair, 2 * pair + 1):
            q, k, v = (head_slice(mixed, head, j) for j in range(3))
            s = masked_scores(q, k, lab_col[...], lab_row[...])
            top = jnp.max(s, axis=1, keepdims=True)
            e = jnp.exp(s - top)
            sums = jnp.sum(e, axis=1, keepdims=True)
            lse[:, head : head + 1] = top + jnp.log(sums)
            p = (e / sums).astype(low)
            scale = 1.0 if head < OLD_HEADS else STEP / RAMP
            outs.append((mul(p, v) * scale).astype(low))
        heads[:, 2 * HD * pair : 2 * HD * (pair + 1)] = jnp.concatenate(outs, axis=1)

    def middle():
        share = misc_v.shape[3] // 2
        weight = misc_v[...].astype(jnp.float32)[:, :, :, :share].reshape(width, width).astype(low)
        value = hidden[...] + mul(heads[...], weight, 1, 1) + norms[6:7, :]
        unit, scale = unit_of(value)
        unit1[...] = unit
        scale1[...] = scale
        hidden[...] = unit * norms[2:3, :] + norms[3:4, :]
        total[...] = hidden[...] + norms[7:8, :]

    def chunk(t):
        one = pltpu.make_async_copy(wu_all.at[:, t], wu_v.at[0], loads.at[2 * planes])
        two = pltpu.make_async_copy(wd_all.at[:, t], wd_v.at[0], loads.at[2 * planes + 1])
        one.start()
        two.start()
        one.wait()
        units = wu_v.shape[1] * 2 * wu_v.shape[3]
        u = mul(hidden[...].astype(low), wu_v[0].reshape(units, width), 1, 1) + bias[t]
        value, rise = gelu_parts(u, ramp[t])
        value = value.astype(low)
        active[t] = value
        slope[t] = rise.astype(low)
        two.wait()
        total[...] += mul(value, wd_v[0].reshape(units, width))

    def last():
        unit, scale = unit_of(total[...])
        unit2[...] = unit
        scale2[...] = scale
        final = (unit * norms[4:5, :] + norms[5:6, :]).astype(low)
        spots = lax.broadcasted_iota(jnp.int32, (chosen.shape[0], tokens), 1)
        marks = (chosen[...] == spots).astype(jnp.float32).astype(low)
        picked[...] = mul(marks, final).astype(low)

    near_first = []
    for j in range(planes):
        spot = jnp.int32(0)
        for zz in range(planes):
            ranked = sorted(range(planes), key=lambda t: (abs(t - zz), t))
            spot = jnp.where(z == zz, ranked[j], spot)
        near_first.append(spot)

    lag = 3
    steps = line_steps(planes)
    far = [s for s in steps if abs(s) > 1]
    early = [(k, s) for k in range(2) for s in (0,)]
    early += [(k, s) for k in range(2) for s in (1, -1)] + [(k, s) for k in range(2) for s in far]
    whole = early + [(k, 0) for k in (2, 3)]
    whole += [(k, s) for a in range(1, planes) for k in (2, 3) for s in (a, -a)]
    events = []
    for i in range(len(whole) + 2 * lag):
        if i < len(whole):
            events.append((gather.launch, *whole[i]))
        if lag <= i < len(whole) + lag:
            events.append((gather.relay, *whole[i - lag]))
        if i >= 2 * lag:
            events.append((gather.finish, *whole[i - 2 * lag]))
    position = events.index((gather.launch, *whole[6]))
    ready = events.index((gather.finish, *early[-1])) + 1
    for event, k, s in events[:position]:
        event(k, s)
    post()
    for event, k, s in events[position:ready]:
        event(k, s)
    opened()
    for s in steps:
        gather.done(0, s)
    rest = events[ready:]
    later = rest.index((gather.finish, 3, -2)) + 1 if planes > 2 else len(rest)

    def settle():
        for s in steps:
            gather.done(1, s)
        wait(load(1, wq_v))

    def settle_far(a):
        for k in (2, 3):
            for s in (a, -a) if a else (0,):
                gather.done(k, s)

    work = [start_norm, lambda: (settle(), project(0))]
    work += [functools.partial(project, g) for g in range(1, 4)]
    work += [functools.partial(attend, p) for p in range(6)]
    work.append(middle)
    work.append(lambda: (settle_far(0), chunk(near_first[0])))
    work.append(lambda: (settle_far(1), chunk(near_first[1])))
    count = len(work)
    for i, act in enumerate(work):
        act()
        for event, k, s in rest[later * i // count : later * (i + 1) // count]:
            event(k, s)
    for a in range(2, planes):
        settle_far(a)
        chunk(near_first[a])
        if a == 2:
            for event, k, s in rest[later:]:
                event(k, s)
    last()
    posts.sent()
    lines.sent()


def params(number):
    return pltpu.CompilerParams(
        collective_id=number, has_side_effects=True, vmem_limit_bytes=56 << 20
    )


def dma(count):
    return pltpu.SemaphoreType.DMA((count,))


def gather_wires(planes, count):
    return count * (planes - 1 + planes * 8)


def spread_wires(planes):
    return 2 * 4 * planes


def scatter_wires(planes, count):
    return count * planes * 11


def held_scratch(planes, shape):
    rows, lanes = shape
    return [
        pltpu.VMEM((4, planes, rows, lanes), jnp.bfloat16),
        pltpu.VMEM((4, planes, rows, lanes), jnp.bfloat16),
        pltpu.VMEM((planes, 3, rows, lanes), jnp.bfloat16),
        pltpu.VMEM((planes - 1, rows, lanes), jnp.bfloat16),
    ]


class Kernels:
    def __init__(self, planes):
        self.planes = planes

    def ids(self, block, small):
        planes = self.planes
        wires = 2 * planes - 1 + spread_wires(planes)
        return pl.pallas_call(
            functools.partial(ids_kernel, planes),
            out_shape=[
                jax.ShapeDtypeStruct((2 * planes, *block.shape), block.dtype),
                jax.ShapeDtypeStruct((2, 4, planes, *small.shape), small.dtype),
            ],
            in_specs=[VMEM] * 2,
            out_specs=[VMEM] * 2,
            scratch_shapes=[dma(wires), dma(wires), dma(2)],
            compiler_params=params(1),
            name="ids",
        )(block, small)

    def forward(self, parcels, blocks, home, extra, labels, norms, bias, ramp, chosen):
        planes = self.planes
        low, f32 = jnp.bfloat16, jnp.float32
        tokens, width = extra.shape
        units = bias.shape[2]
        gathered = [jax.ShapeDtypeStruct((4, planes, 2, *b.shape), b.dtype) for b in blocks]
        saved = [
            ((tokens, width), f32),
            ((tokens, 1), f32),
            ((4, tokens, blocks[1].shape[1]), low),
            ((tokens, 128), f32),
            ((tokens, width), low),
            ((tokens, width), f32),
            ((tokens, 1), f32),
            ((planes, tokens, units), low),
            ((planes, tokens, units), low),
            ((tokens, width), f32),
            ((tokens, 1), f32),
            ((chosen.shape[0], width), low),
        ]
        count = line_wires(planes, 4)
        spread = spread_wires(planes)
        share = blocks[2].shape[0]
        result = pl.pallas_call(
            functools.partial(forward_kernel, planes, ROOM),
            out_shape=gathered + [jax.ShapeDtypeStruct(s, t) for s, t in saved],
            in_specs=[ANY] * 5 + [VMEM] * 8,
            out_specs=[ANY] * 4 + [VMEM] * len(saved),
            scratch_shapes=[
                pltpu.VMEM((2, *parcels.shape), low),
                pltpu.VMEM(gathered[0].shape, low),
                pltpu.VMEM(gathered[1].shape, low),
                pltpu.VMEM((1, 4, 2, share, width), low),
                pltpu.VMEM((1, 4, 2, share, width), low),
                pltpu.VMEM((tokens, width), f32),
                pltpu.VMEM((tokens, width), f32),
                dma(count),
                dma(count),
                dma(5),
                dma(spread),
                dma(spread),
                dma(2 * planes + 2),
            ],
            compiler_params=params(2),
            name="forward",
        )(
            parcels,
            *blocks,
            home,
            extra,
            labels.reshape(-1, 1),
            labels.reshape(1, -1),
            norms,
            bias,
            ramp,
            chosen.reshape(-1, 1),
        )
        return result[:4], result[4:]

    def deliver(self, parcels):
        planes = self.planes
        wires = spread_wires(planes)
        return pl.pallas_call(
            functools.partial(deliver_kernel, planes),
            out_shape=jax.ShapeDtypeStruct((2, *parcels.shape), parcels.dtype),
            in_specs=[ANY],
            out_specs=ANY,
            scratch_shapes=[dma(wires), dma(wires), pltpu.SemaphoreType.DMA],
            compiler_params=params(3),
            name="deliver",
        )(parcels)

    def rows(self, block):
        planes = self.planes
        wires = gather_wires(planes, 1)
        return pl.pallas_call(
            functools.partial(gather_kernel, planes, 1),
            out_shape=jax.ShapeDtypeStruct((4, planes, 2, *block.shape), block.dtype),
            in_specs=[ANY],
            out_specs=ANY,
            scratch_shapes=[dma(wires), dma(wires), dma(1)],
            compiler_params=params(4),
            name="rows",
        )(block)

    def small(self, block, number):
        planes = self.planes
        wires = spread_wires(planes)
        return pl.pallas_call(
            functools.partial(small_kernel, planes),
            out_shape=jax.ShapeDtypeStruct((2, 4, planes, *block.shape), block.dtype),
            in_specs=[VMEM],
            out_specs=VMEM,
            scratch_shapes=[dma(wires), dma(wires), pltpu.SemaphoreType.DMA],
            compiler_params=params(number),
            name="small",
        )(block)

    def scatter_rows(self, grads):
        planes = self.planes
        shape = grads.shape[3:]
        wires = scatter_wires(planes, 1)
        return pl.pallas_call(
            functools.partial(scatter_kernel, planes, 1),
            out_shape=jax.ShapeDtypeStruct(shape, jnp.float32),
            in_specs=[ANY],
            out_specs=VMEM,
            scratch_shapes=held_scratch(planes, shape) + [dma(wires), dma(wires), dma(planes)],
            compiler_params=params(7),
            name="scatter_rows",
        )(grads)

    def give(self, parcels, grads):
        planes, count = self.planes, len(grads)
        shapes = [g.shape[3:] for g in grads]
        wires = scatter_wires(planes, count) + spread_wires(planes)
        held = [s for shape in shapes for s in held_scratch(planes, shape)]
        layer = parcels.shape[1:]
        result = pl.pallas_call(
            functools.partial(give_kernel, planes, count),
            out_shape=[jax.ShapeDtypeStruct(layer, parcels.dtype)]
            + [jax.ShapeDtypeStruct(shape, jnp.float32) for shape in shapes],
            in_specs=[ANY] * (1 + count),
            out_specs=[ANY] + [VMEM] * count,
            scratch_shapes=held
            + [pltpu.VMEM(layer, parcels.dtype), pltpu.VMEM(layer, parcels.dtype)]
            + [dma(wires), dma(wires), dma(planes * count), dma(2)],
            compiler_params=params(8),
            name="give",
        )(parcels, *grads)
        return result[0], result[1:]

    def hand_back(self, parcels):
        planes = self.planes
        layer = parcels.shape[1:]
        wires = spread_wires(planes)
        return pl.pallas_call(
            functools.partial(return_kernel, planes),
            out_shape=jax.ShapeDtypeStruct(layer, parcels.dtype),
            in_specs=[ANY],
            out_specs=ANY,
            scratch_shapes=[pltpu.VMEM(layer, parcels.dtype), pltpu.VMEM(layer, parcels.dtype)]
            + [dma(wires), dma(wires), dma(2)],
            compiler_params=params(9),
            name="hand_back",
        )(parcels)


class Plain:
    def __init__(self, planes):
        self.planes = planes

    def ids(self, block, small):
        return lax.all_gather(block, "row"), self.small(small, 0)

    def gather(self, block):
        whole = lax.all_gather(block, ("head", "row"))
        return whole.reshape(4, self.planes, 2, *block.shape)

    def forward(self, parcels, blocks, home, extra, labels, norms, bias, ramp, chosen):
        parcels = self.deliver(parcels)
        gathered = [self.gather(b) for b in blocks]
        return gathered, forward_plain(
            parcels, gathered, home, extra, labels, norms, bias, ramp, chosen
        )

    def deliver(self, parcels):
        shape = parcels.shape
        both = jnp.broadcast_to(parcels[:, :, None], (*shape[:2], 2, *shape[2:]))
        flat = both.reshape(8 * self.planes, *shape[2:])
        got = lax.all_to_all(flat, ("head", "row"), split_axis=0, concat_axis=0, tiled=True)
        return jnp.moveaxis(got.reshape(4, self.planes, 2, *shape[2:]), 2, 0)

    def rows(self, block):
        return self.gather(block)

    def small(self, block, number):
        return jnp.moveaxis(self.gather(block), 2, 0)

    def scatter_rows(self, grads):
        flat = grads.reshape(-1, grads.shape[-1]).astype(jnp.float32)
        return lax.psum_scatter(flat, ("head", "row"), scatter_dimension=0, tiled=True)

    def give(self, parcels, grads):
        return self.hand_back(parcels), [self.scatter_rows(g) for g in grads]

    def hand_back(self, parcels):
        shape = parcels.shape
        flat = jnp.moveaxis(parcels, 0, 2).reshape(8 * self.planes, *shape[3:])
        got = lax.all_to_all(flat, ("head", "row"), split_axis=0, concat_axis=0, tiled=True)
        got = got.reshape(4, self.planes, 2, *shape[3:]).astype(jnp.float32)
        return jnp.sum(got, axis=2).astype(parcels.dtype)


def contract(left, right, left_dim, right_dim):
    return lax.dot_general(
        left, right, (((left_dim,), (right_dim,)), ((), ())), preferred_element_type=jnp.float32
    )


def unit_back(grad, unit, scale, gain):
    inner = grad * gain
    back = scale * (
        inner
        - jnp.mean(inner, axis=-1, keepdims=True)
        - unit * jnp.mean(inner * unit, axis=-1, keepdims=True)
    )
    return (back, grad * unit)


def by_plane(blocks):
    planes, lanes = blocks.shape[1], blocks.shape[4]
    return blocks.transpose(1, 0, 2, 3, 4).reshape(planes, -1, lanes)


def heads_of(mixed):
    tokens = mixed.shape[1]
    parts = mixed.reshape(4, tokens, -1, 3, HD).transpose(3, 1, 0, 2, 4)
    parts = parts.reshape(3, tokens, -1, HD)
    return parts[0], parts[1], parts[2]


def forward_plain(parcels, gathered, home, extra, labels, norms, bias, ramp, chosen):
    low = jnp.bfloat16
    misc, wq, wu, wd = gathered
    tokens, width = extra.shape
    share = misc.shape[3] // 2
    rows = parcels.reshape(-1, width)
    looked = jnp.dot(
        (home == jnp.arange(rows.shape[0])[None, :]).astype(low),
        rows,
        preferred_element_type=jnp.float32,
    )
    places = misc[:, :, :, share:, :SEQ].reshape(width, SEQ).T.astype(jnp.float32)
    unit0, scale0 = unit_of(looked + extra + places)
    normed = unit0 * norms[0] + norms[1]
    weight = wq.reshape(4, width, wq.shape[4])
    mixed = jnp.einsum("td,hdj->htj", normed.astype(low), weight, preferred_element_type=jnp.float32)
    mixed = mixed.astype(low)
    query, keys, values = heads_of(mixed)
    attended, summary = attend_fwd(query, keys, values, labels)
    head_ramp = jnp.where(jnp.arange(query.shape[1]) < OLD_HEADS, 1.0, STEP / RAMP)
    heads = (attended * head_ramp[:, None]).astype(low).reshape(tokens, width)
    lse = jnp.pad(summary.T, ((0, 0), (0, 128 - summary.shape[0])))
    weight = misc[:, :, :, :share].reshape(width, width)
    unit1, scale1 = unit_of(normed + contract(heads, weight, 1, 1) + norms[6])
    hidden = unit1 * norms[2] + norms[3]
    u = jnp.einsum(
        "td,pud->ptu", hidden.astype(low), by_plane(wu), preferred_element_type=jnp.float32
    )
    value, rise = gelu_parts(u + bias, ramp)
    active = value.astype(low)
    down = jnp.einsum("ptu,pud->td", active, by_plane(wd), preferred_element_type=jnp.float32)
    unit2, scale2 = unit_of(hidden + down + norms[7])
    final = (unit2 * norms[4] + norms[5]).astype(low)
    marks = (chosen[:, None] == jnp.arange(tokens)[None, :]).astype(low)
    picked = jnp.dot(marks, final, preferred_element_type=jnp.float32).astype(low)
    slope = rise.astype(low)
    return (unit0, scale0, mixed, lse, heads, unit1, scale1, active, slope, unit2, scale2, picked)


def score_block(query, keys, labels):
    scores = jnp.einsum("qhe,khe->hqk", query, keys, preferred_element_type=jnp.float32) * HD ** (
        -0.5
    )
    allowed = labels[:, None] == labels[None, :]
    return jnp.where(allowed[None], scores, -1000000000.0)


def attend_fwd(query, keys, values, labels):
    scores = score_block(query, keys, labels)
    top = jnp.max(scores, axis=-1, keepdims=True)
    weights = jnp.exp(scores - top)
    total = jnp.sum(weights, axis=-1, keepdims=True)
    probs = weights / total
    output = jnp.einsum(
        "hqk,khe->qhe", probs.astype(jnp.bfloat16), values, preferred_element_type=jnp.float32
    )
    return (output, (top + jnp.log(total))[..., 0])


def attend_back(query, keys, values, labels, summary, grad_out):
    scores = score_block(query, keys, labels)
    probs = jnp.exp(scores - summary[..., None])
    grad_values = jnp.einsum(
        "hqk,qhe->khe", probs.astype(jnp.bfloat16), grad_out, preferred_element_type=jnp.float32
    )
    grad_probs = jnp.einsum("qhe,khe->hqk", grad_out, values, preferred_element_type=jnp.float32)
    grad_scores = probs * (grad_probs - jnp.sum(grad_probs * probs, axis=-1, keepdims=True))
    grad_low = grad_scores.astype(jnp.bfloat16)
    grad_query = jnp.einsum(
        "hqk,khe->qhe", grad_low, keys, preferred_element_type=jnp.float32
    ) * HD ** (-0.5)
    grad_keys = jnp.einsum(
        "hqk,qhe->khe", grad_low, query, preferred_element_type=jnp.float32
    ) * HD ** (-0.5)
    return jnp.stack([grad_query, grad_keys, grad_values], axis=2)


def adamw(weight, grad, first, second, decay, rate):
    first = BETA_ONE * first + (1 - BETA_ONE) * grad
    second = BETA_TWO * second + (1 - BETA_TWO) * grad * grad
    moved = first / (1 - BETA_ONE**STEP) / (jnp.sqrt(second / (1 - BETA_TWO**STEP)) + ADAM_EPSILON)
    return (weight - rate * (moved + decay * weight), first, second)


def padded(flat, rows, lanes):
    return jnp.pad(flat, (0, rows * lanes - flat.shape[0])).reshape(rows, lanes)


def on_device(
    token_ids,
    segment_ids,
    masked_pos,
    masked_target,
    embedding,
    position_table,
    qkv_weight,
    out_weight,
    up_weight,
    down_weight,
    norm_params,
    up_bias,
    m_embedding,
    m_position,
    m_qkv,
    m_out,
    m_up,
    m_down,
    m_norm,
    m_bias,
    v_embedding,
    v_position,
    v_qkv,
    v_out,
    v_up,
    v_down,
    v_norm,
    v_bias,
):
    low = jnp.bfloat16
    row_count = lax.axis_size("row")
    devices = HEADS * row_count
    planes = row_count // 2
    wire = Kernels(planes) if planes <= 4 else Plain(planes)
    head = lax.axis_index("head")
    row = lax.axis_index("row")
    core = row % 2
    device = head * row_count + row
    vocab_part, width = embedding.shape
    tokens = token_ids.shape[0] // HEADS
    inner = up_weight.shape[1] * devices

    share = width // devices
    share_inner = inner // devices

    labels_all = segment_ids.reshape(HEADS, tokens)
    slots = masked_pos.shape[1] // HEADS
    live = labels_at(segment_ids, masked_pos[0])
    target = jnp.where(live, masked_target[0], -1)
    small = jnp.concatenate([norm_params.reshape(-1), up_bias]).astype(low)
    small_rows = -(-small.shape[0] // 2048) * 16
    words = token_ids.shape[0] + target.shape[0]
    lines = -(-words // 1024) * 8
    numbers, small_all = wire.ids(
        padded(jnp.concatenate([token_ids, target]), lines, 128), padded(small, small_rows, 128)
    )
    numbers = numbers.reshape(row_count, lines * 128)
    small_all = jnp.moveaxis(small_all.reshape(2, HEADS, planes, -1), 0, 2).astype(jnp.float32)
    norms = small_all[..., : 8 * share].reshape(devices, 8, share)
    norms = norms.transpose(1, 0, 2).reshape(8, width)
    bias = small_all[..., 8 * share : 8 * share + share_inner]
    bias = bias.transpose(1, 0, 2, 3).reshape(planes, 1, -1)
    ramp = jnp.where(jnp.arange(inner) < OLD_FF, 1.0, STEP / RAMP).astype(jnp.float32)
    ramp = ramp.reshape(HEADS, planes, -1).transpose(1, 0, 2).reshape(planes, 1, -1)
    ids = numbers[:, : token_ids.shape[0]].reshape(planes, 2, HEADS, tokens)
    ids = ids.transpose(2, 0, 1, 3).reshape(HEADS * planes, 2 * tokens)
    targets = numbers[:, token_ids.shape[0] : words].reshape(row_count, HEADS, slots)
    targets = targets.transpose(1, 0, 2).reshape(-1)

    owner = ids // vocab_part
    counts = jnp.sum(owner[:, :, None] == jnp.arange(devices), axis=1)
    rounds = -(-jnp.max(counts) // ROOM)
    inside = owner == device
    order = jnp.arange(2 * tokens)
    before = (order[:, None] < order[None, :]).astype(low)
    rank = jnp.dot(inside.astype(low), before, preferred_element_type=jnp.float32).astype(jnp.int32)
    rank = jnp.where(inside, rank, -1)
    local = ids - device * vocab_part
    chip = head * planes + row // 2
    own_owner = lax.dynamic_index_in_dim(owner, chip, 0, keepdims=False)
    own_marks = own_owner[:, None] == jnp.arange(devices)
    own_before = contract(before, own_marks.astype(low), 0, 0).astype(jnp.int32)
    own_rank = jnp.sum(jnp.where(own_marks, own_before, 0), axis=1)
    own_owner = lax.dynamic_slice_in_dim(own_owner, core * tokens, tokens, 0)
    own_rank = lax.dynamic_slice_in_dim(own_rank, core * tokens, tokens, 0)
    own_home = (own_owner % 2) * (devices // 2) + own_owner // 2
    table = embedding.astype(low)

    def parcel_marks(turn):
        spot = jnp.arange(ROOM) + turn * ROOM
        hit = rank[:, None, :] == spot[None, :, None]
        which = jnp.sum(jnp.where(hit, local[:, None, :] + 1, 0), axis=2) - 1
        marks = which.reshape(-1)[:, None] == jnp.arange(vocab_part)[None, :]
        return marks.astype(low)

    def seats(turn):
        seat = own_rank - turn * ROOM
        return jnp.where((seat >= 0) & (seat < ROOM), own_home * ROOM + seat, -1)[:, None]

    def token_marks(turn):
        return (seats(turn) == jnp.arange(devices * ROOM)[None, :]).astype(low)

    def parcels_of(turn):
        picked = jnp.dot(parcel_marks(turn), table, preferred_element_type=jnp.float32)
        return picked.astype(low).reshape(HEADS, planes, ROOM, width)

    def opened(parcels, turn):
        return jnp.dot(
            token_marks(turn),
            parcels.reshape(devices * ROOM, width),
            preferred_element_type=jnp.float32,
        )

    def again(state):
        turn, so_far = state
        return turn + 1, so_far + opened(wire.deliver(parcels_of(turn)), turn)

    _, extra = lax.while_loop(
        lambda state: state[0] < rounds,
        again,
        (jnp.int32(1), jnp.zeros((tokens, width), jnp.float32)),
    )

    labels = lax.dynamic_index_in_dim(labels_all, head, 0, keepdims=False)
    chosen = lax.dynamic_slice_in_dim(masked_pos[0], head * slots, slots, 0) - head * tokens
    misc = jnp.concatenate(
        [out_weight.T, jnp.pad(position_table.T, ((0, 0), (0, width - SEQ)))], axis=0
    )
    gathered, saved = wire.forward(
        parcels_of(0),
        [misc.astype(low), qkv_weight.astype(low), up_weight.T.astype(low), down_weight.astype(low)],
        seats(0),
        extra,
        labels,
        norms,
        bias,
        ramp,
        chosen,
    )
    unit_zero, scale_zero, mixed, lse, heads_low, unit_one, scale_one = saved[:7]
    active, slope, unit_two, scale_two, picked = saved[7:]
    out_full = gathered[0][:, :, :, :share].reshape(width, width)
    qkv_full = gathered[1].reshape(HEADS, width, qkv_weight.shape[1])
    up_full, down_full = by_plane(gathered[2]), by_plane(gathered[3])
    normed_low = (unit_zero * norms[0] + norms[1]).astype(low)
    hidden_low = (unit_one * norms[2] + norms[3]).astype(low)
    query, keys, values = heads_of(mixed)
    heads = query.shape[1]
    summary = lse[:, :heads].T
    head_ramp = jnp.where(jnp.arange(heads) < OLD_HEADS, 1.0, STEP / RAMP).astype(jnp.float32)

    chosen_marks = chosen[:, None] == jnp.arange(tokens)[None, :]
    all_rows = wire.rows(picked).reshape(devices * slots, width)
    valid = (targets >= 0).astype(jnp.float32)
    logits = contract(all_rows, table, 1, 1)
    hits = jnp.arange(vocab_part)[None, :] == (targets - device * vocab_part)[:, None]
    top = jnp.max(logits, axis=1)
    part = top + jnp.log(jnp.sum(jnp.exp(logits - top[:, None]), axis=1))
    parts = wire.small(part.reshape(-1, 128), 5).reshape(devices, -1)
    peak = jnp.max(parts, axis=0)
    log_total = peak + jnp.log(jnp.sum(jnp.exp(parts - peak), axis=0))
    target_part = jnp.sum(jnp.where(hits, logits, 0.0))
    log_own = lax.dynamic_slice_in_dim(log_total * valid, device * slots, slots, 0)
    valid_own = lax.dynamic_slice_in_dim(valid, device * slots, slots, 0)
    loss_own = jnp.sum(log_own) - target_part
    count_own = jnp.sum(valid_own)
    grad_logits = (
        valid[:, None] * (jnp.exp(logits - log_total[:, None]) - hits.astype(jnp.float32))
    ).astype(low)
    grad_table = contract(grad_logits, all_rows, 0, 0)
    grad_rows = jnp.dot(grad_logits, table, preferred_element_type=jnp.float32).astype(low)
    grad_picked = wire.scatter_rows(grad_rows.reshape(HEADS, planes, 2, slots, width))

    grad_final = lax.dot_general(
        chosen_marks.astype(jnp.float32),
        grad_picked,
        (((0,), (0,)), ((), ())),
        precision=lax.Precision.HIGHEST,
    )
    grad_sum, gain_two = unit_back(grad_final, unit_two, scale_two, norms[4])
    grad_sum_low = grad_sum.astype(low)
    f32 = jnp.float32
    grad_down = jnp.einsum("ptu,td->pud", active, grad_sum_low, preferred_element_type=f32)
    grad_upper = jnp.einsum("td,pud->ptu", grad_sum_low, down_full, preferred_element_type=f32)
    grad_upper = grad_upper * slope.astype(f32)
    grad_upper_low = grad_upper.astype(low)
    grad_up = jnp.einsum("ptu,td->pud", grad_upper_low, hidden_low, preferred_element_type=f32)
    grad_hidden = grad_sum + jnp.einsum(
        "ptu,pud->td", grad_upper_low, up_full, preferred_element_type=f32
    )
    grad_res, gain_one = unit_back(grad_hidden, unit_one, scale_one, norms[2])
    grad_res_low = grad_res.astype(low)
    grad_out = contract(grad_res_low, heads_low, 0, 0)
    grad_heads = jnp.dot(grad_res_low, out_full, preferred_element_type=jnp.float32).astype(low)
    grad_attended = (
        grad_heads.reshape(tokens, heads, HD).astype(jnp.float32) * head_ramp[:, None]
    ).astype(low)
    grad_mixed = attend_back(query, keys, values, labels, summary, grad_attended)
    grad_mixed_low = grad_mixed.astype(low).reshape(tokens, HEADS, -1)
    grad_qkv = jnp.einsum(
        "td,thj->hdj", normed_low, grad_mixed_low, preferred_element_type=jnp.float32
    )
    grad_normed = grad_res + jnp.einsum(
        "thj,hdj->td", grad_mixed_low, qkv_full, preferred_element_type=jnp.float32
    )
    grad_start, gain_zero = unit_back(grad_normed, unit_zero, scale_zero, norms[0])
    grad_start_low = grad_start.astype(low)
    grad_norms = jnp.stack(
        [
            jnp.sum(gain_zero, axis=0),
            jnp.sum(grad_normed, axis=0),
            jnp.sum(gain_one, axis=0),
            jnp.sum(grad_hidden, axis=0),
            jnp.sum(gain_two, axis=0),
            jnp.sum(grad_final, axis=0),
            jnp.sum(grad_res, axis=0),
            jnp.sum(grad_sum, axis=0),
        ]
    )
    grad_bias = jnp.sum(grad_upper, axis=1).reshape(planes, HEADS, 2 * share_inner)

    def by_head(grad):
        grad = grad.reshape(planes, HEADS, 2, share_inner, width).astype(low)
        return grad.transpose(1, 0, 2, 3, 4)

    def parcels_back(turn):
        back = contract(token_marks(turn), grad_start_low, 0, 0).astype(low)
        return back.reshape(2, HEADS, planes, ROOM, width)

    def unpacked(parcels, turn):
        return contract(parcel_marks(turn), parcels.reshape(-1, width), 0, 0)

    flat = jnp.concatenate(
        [
            grad_norms.reshape(8, devices, share).transpose(1, 0, 2).reshape(devices, -1),
            grad_bias.transpose(1, 0, 2).reshape(devices, -1),
        ],
        axis=1,
    )
    more_rows = -(-flat.shape[1] // width)
    misc_rows = -(-(2 * share + more_rows) // 16) * 16
    flat = jnp.pad(flat, ((0, 0), (0, more_rows * width - flat.shape[1])))
    grad_misc = jnp.concatenate(
        [
            grad_out.reshape(devices, share, width),
            jnp.pad(grad_start.T, ((0, 0), (0, width - SEQ))).reshape(devices, share, width),
            flat.reshape(devices, more_rows, width),
            jnp.zeros((devices, misc_rows - more_rows - 2 * share, width), jnp.float32),
        ],
        axis=1,
    ).astype(low)
    parcels, summed = wire.give(
        parcels_back(0),
        [
            grad_misc.reshape(HEADS, planes, 2, misc_rows, width),
            grad_qkv.astype(low).reshape(HEADS, planes, 2, *qkv_weight.shape),
            by_head(grad_up),
            by_head(grad_down),
        ],
    )
    grad_table = grad_table + unpacked(parcels, 0)

    def again_back(state):
        turn, so_far = state
        return turn + 1, so_far + unpacked(wire.hand_back(parcels_back(turn)), turn)

    _, grad_table = lax.while_loop(
        lambda state: state[0] < rounds, again_back, (jnp.int32(1), grad_table)
    )
    flat = summed[0][2 * share : 2 * share + more_rows].reshape(-1)
    grads = (
        grad_table,
        summed[0][share : 2 * share, :SEQ].T,
        summed[1],
        summed[0][:share].T,
        summed[2].T,
        summed[3],
        flat[: 8 * share].reshape(8, share),
        flat[8 * share : 8 * share + share_inner],
    )
    squares = sum((jnp.sum(g * g) for g in grads))
    scalars = padded(jnp.stack([squares, loss_own, count_own]), 8, 128)
    scalars = jnp.sum(wire.small(scalars, 6).reshape(devices, 8, 128)[:, 0, :3], axis=0)
    squares, loss_sum, live_count = scalars[0], scalars[1], scalars[2]
    grad_norm = jnp.sqrt(squares) / live_count
    factor = jnp.minimum(1.0, CLIP / grad_norm) / live_count
    weights = (
        embedding,
        position_table,
        qkv_weight,
        out_weight,
        up_weight,
        down_weight,
        norm_params,
        up_bias,
    )
    firsts = (m_embedding, m_position, m_qkv, m_out, m_up, m_down, m_norm, m_bias)
    seconds = (v_embedding, v_position, v_qkv, v_out, v_up, v_down, v_norm, v_bias)
    decays = (DECAY,) * 6 + (0.0, 0.0)
    rates = (LEARN_RATE,) * 6 + (GAIN_RATE,) * 2
    results = [
        adamw(w, g * factor, m, v, d, r)
        for w, g, m, v, d, r in zip(weights, grads, firsts, seconds, decays, rates)
    ]
    return (
        *(r[0] for r in results),
        *(r[1] for r in results),
        *(r[2] for r in results),
        loss_sum,
        live_count,
        grad_norm,
    )


def labels_at(segment_ids, positions):
    at = positions[:, None] == jnp.arange(segment_ids.shape[0])[None, :]
    return jnp.sum(jnp.where(at, segment_ids[None, :], 0), axis=1) != SEQ - 1


def solution(mesh):
    vocab = P(("head", "row"), None)
    columns = P(None, ("head", "row"))
    flat = P(("head", "row"))
    weights = (vocab, columns, P("row", "head"), columns, columns, vocab, columns, flat)
    data = (P("row"), P("row"), P("row", None), P("row", None))
    return jax.shard_map(
        on_device,
        mesh=mesh,
        in_specs=(*data, *weights, *weights, *weights),
        out_specs=(*weights, *weights, *weights, P(), P(), P()),
        check_vma=False,
    )
```

```python
import functools

import jax
import jax.numpy as jnp
from jax import lax
from jax.experimental import pallas as pl
from jax.experimental.pallas import tpu as pltpu
from jax.sharding import PartitionSpec as P

HD = 64
SEQ = 512
STEP = 5
RAMP = 10
OLD_HEADS = 8
OLD_FF = 2048


EPSILON = 1e-05
LEARN_RATE = 0.03
GAIN_RATE = 0.5
BETA_ONE = 0.9
BETA_TWO = 0.999
ADAM_EPSILON = 1e-08
DECAY = 0.01
CLIP = 0.02

ROOM = 64
HEADS = 4
MESH = pl.DeviceIdType.MESH
ANY = pl.BlockSpec(memory_space=pl.ANY)
VMEM = pl.BlockSpec(memory_space=pltpu.VMEM)


def place():
    h = lax.axis_index("head")
    r = lax.axis_index("row")
    return h, lax.div(r, 2), lax.rem(r, 2)


def across(h, q):
    if q == 0:
        return h
    if q == 1:
        return h + 1 - 2 * lax.rem(h, 2)
    if q == 2:
        return lax.rem(h + 2, 4)
    return 3 - h


class Wires:
    def __init__(self, send, recv):
        self.send, self.recv, self.used, self.made = send, recv, 0, []

    def copy(self, src, dst, to):
        i = self.used
        self.used += 1
        one = pltpu.make_async_remote_copy(
            src_ref=src,
            dst_ref=dst,
            send_sem=self.send.at[i],
            recv_sem=self.recv.at[i],
            device_id=to,
            device_id_type=MESH,
        )
        one.start()
        self.made.append(one)
        return one

    def sent(self):
        for one in self.made:
            one.wait_send()


def greet(peers):
    barrier = pltpu.get_barrier_semaphore()
    for to in peers:
        pl.semaphore_signal(barrier, inc=1, device_id=to, device_id_type=MESH)
    pl.semaphore_wait(barrier, len(peers))


def near(planes):
    h, z, c = place()
    peers = [(h, 2 * z + 1 - c), (across(h, 1), 2 * z + c), (across(h, 2), 2 * z + c)]
    peers += [(h, 2 * lax.rem(z + s, planes) + c) for s in range(1, planes)]
    return peers


def every_chip(planes):
    h, z, c = place()
    peers = [(h, 2 * z + 1 - c)]
    for q in range(4):
        for s in range(planes):
            if q or s:
                peers.append((across(h, q), 2 * lax.rem(z + s, planes) + c))
    return peers


def split(rows):
    first = -(-rows // 32) * 16
    return pl.ds(0, first), pl.ds(first, rows - first)


def gather_steps(wires, local, planes, pairs):
    h, z, c = place()
    row = 2 * z + c
    sib = (h, 2 * z + 1 - c)
    hx, hy, hd = across(h, 1), across(h, 2), across(h, 3)
    xn, yn = (hx, row), (hy, row)
    zs = [lax.rem(z - s + planes, planes) for s in range(planes)]
    count = len(pairs)
    here = []
    for k, (x, out) in enumerate(pairs):
        one = pltpu.make_async_copy(x, out.at[h, z, c], local.at[k])
        one.start()
        here.append(one)
    from_z = {}
    for k, (x, out) in enumerate(pairs):
        for s in range(1, planes):
            from_z[k, s] = wires.copy(x, out.at[h, z, c], (h, 2 * lax.rem(z + s, planes) + c))
    from_x, from_y, from_xd, from_yd, from_sib = {}, {}, {}, {}, []

    def launch(k, s):
        x, out = pairs[k]
        src = x if s == 0 else out.at[h, zs[s], c]
        if s:
            from_z[k, s].wait_recv()
        dst = out.at[h, zs[s], c]
        from_x[k, s] = wires.copy(src, dst, xn)
        from_y[k, s] = wires.copy(src, dst, yn)
        from_sib.append(wires.copy(src, dst, sib))

    def relay(k, s):
        _, out = pairs[k]
        first, second = split(out.shape[3])
        from_x[k, s].wait_recv()
        got = out.at[hx, zs[s], c]
        from_yd[k, s] = wires.copy(got.at[second], got.at[second], yn)
        from_sib.append(wires.copy(got, got, sib))
        from_y[k, s].wait_recv()
        got = out.at[hy, zs[s], c]
        from_xd[k, s] = wires.copy(got.at[first], got.at[first], xn)
        from_sib.append(wires.copy(got, got, sib))

    def finish(k, s):
        _, out = pairs[k]
        from_yd[k, s].wait_recv()
        from_xd[k, s].wait_recv()
        got = out.at[hd, zs[s], c]
        from_sib.append(wires.copy(got, got, sib))

    order = [(k, s) for k in range(count) for s in range(planes)]
    for i in range(len(order) + 2):
        if i < len(order):
            launch(*order[i])
        if 1 <= i <= len(order):
            relay(*order[i - 1])
        if i >= 2:
            finish(*order[i - 2])
    for one in from_sib:
        one.wait_recv()
    for one in here:
        one.wait()


def spread_start(wires, local, planes, parcels, out):
    h, z, c = place()
    sib = (h, 2 * z + 1 - c)
    got = {}
    for q in range(4):
        for s in range(planes):
            if q or s:
                th, tz = across(h, q), lax.rem(z + s, planes)
                got[q, s] = wires.copy(parcels(th, tz), out.at[c, h, z], (th, 2 * tz + c))
    mine = pltpu.make_async_copy(parcels(h, z), out.at[c, h, z], local)
    mine.start()
    passed = [wires.copy(parcels(h, z), out.at[c, h, z], sib)]
    return got, mine, passed


def spread_finish(wires, planes, out, state):
    h, z, c = place()
    sib = (h, 2 * z + 1 - c)
    got, mine, passed = state
    for (q, s), one in got.items():
        one.wait_recv()
        there = out.at[c, across(h, q), lax.rem(z - s + planes, planes)]
        passed.append(wires.copy(there, there, sib))
    for one in passed:
        one.wait_recv()
    mine.wait()


def small_kernel(planes, x, out, send, recv, local):
    greet(every_chip(planes))
    wires = Wires(send, recv)
    state = spread_start(wires, local, planes, lambda h, z: x, out)
    spread_finish(wires, planes, out, state)
    wires.sent()


def gather_kernel(planes, count, *refs):
    xs, outs = refs[:count], refs[count : 2 * count]
    send, recv, local = refs[2 * count :]
    greet(near(planes))
    wires = Wires(send, recv)
    gather_steps(wires, local, planes, list(zip(xs, outs)))
    wires.sent()


def deliver_kernel(planes, parcels, out, send, recv, local):
    greet(every_chip(planes))
    wires = Wires(send, recv)
    state = spread_start(wires, local, planes, lambda h, z: parcels.at[h, z], out)
    spread_finish(wires, planes, out, state)
    wires.sent()


def add_rows(target, others, rows):
    @pl.loop(0, rows // 16)
    def _(i):
        at = pl.ds(pl.multiple_of(i * 16, 16), 16)
        total = target[at, :].astype(jnp.float32)
        for other in others:
            total = total + other[at, :].astype(jnp.float32)
        target[at, :] = total.astype(target.dtype)


def scatter_steps(wires, local, planes, groups):
    h, z, c = place()
    row = 2 * z + c
    sib = (h, 2 * z + 1 - c)
    hx, hy, hd = across(h, 1), across(h, 2), across(h, 3)
    xn, yn = (hx, row), (hy, row)
    zs = [lax.rem(z + 1 + s, planes) for s in range(planes)]
    order = [(k, s) for k in range(len(groups)) for s in range(planes)]
    from_sib, loads = {}, {}
    for i, (k, s) in enumerate(order):
        grads, out, own, sibs, px, pz = groups[k]
        for q in (3, 1, 2, 0):
            th = across(h, q)
            from_sib[k, s, q] = wires.copy(grads.at[th, zs[s], 1 - c], sibs.at[th, zs[s]], sib)
        loads[k, s] = pltpu.make_async_copy(grads.at[:, zs[s], c], own.at[:, zs[s]], local.at[i])
        loads[k, s].start()
    first, second, from_z = {}, {}, {}

    def pair(k, s):
        grads, out, own, sibs, px, pz = groups[k]
        a, b = split(own.shape[2])
        loads[k, s].wait()
        for q in (3, 1, 2, 0):
            from_sib[k, s, q].wait_recv()
            th = across(h, q)
            add_rows(own.at[th, zs[s]], [sibs.at[th, zs[s]]], own.shape[2])
            if q == 3:
                first[k, s, "xd"] = wires.copy(
                    own.at[hd, zs[s]].at[a], px.at[zs[s], 0].at[a], xn
                )
                first[k, s, "yd"] = wires.copy(
                    own.at[hd, zs[s]].at[b], px.at[zs[s], 0].at[b], yn
                )
            if q == 1:
                first[k, s, "x"] = wires.copy(own.at[hx, zs[s]].at[a], px.at[zs[s], 1].at[a], xn)
            if q == 2:
                first[k, s, "y"] = wires.copy(own.at[hy, zs[s]].at[b], px.at[zs[s], 1].at[b], yn)

    def plane(k, s):
        grads, out, own, sibs, px, pz = groups[k]
        a, b = split(own.shape[2])
        first[k, s, "xd"].wait_recv()
        add_rows(own.at[hy, zs[s]].at[a], [px.at[zs[s], 0].at[a]], a.size)
        second[k, s, "y"] = wires.copy(own.at[hy, zs[s]].at[a], px.at[zs[s], 2].at[a], yn)
        first[k, s, "yd"].wait_recv()
        add_rows(own.at[hx, zs[s]].at[b], [px.at[zs[s], 0].at[b]], b.size)
        second[k, s, "x"] = wires.copy(own.at[hx, zs[s]].at[b], px.at[zs[s], 2].at[b], xn)

    def line(k, s):
        grads, out, own, sibs, px, pz = groups[k]
        for part in ("x", "y"):
            first[k, s, part].wait_recv()
            second[k, s, part].wait_recv()
        add_rows(own.at[h, zs[s]], [px.at[zs[s], 1], px.at[zs[s], 2]], own.shape[2])
        if s < planes - 1:
            from_z[k, s] = wires.copy(own.at[h, zs[s]], pz.at[s], (h, 2 * zs[s] + c))

    def total(k):
        grads, out, own, sibs, px, pz = groups[k]
        for s in range(planes - 1):
            from_z[k, s].wait_recv()

        @pl.loop(0, out.shape[0] // 16)
        def _(i):
            at = pl.ds(pl.multiple_of(i * 16, 16), 16)
            value = own[h, z, at, :].astype(jnp.float32)
            for s in range(planes - 1):
                value = value + pz[s, at, :].astype(jnp.float32)
            out[at, :] = value

    for i in range(len(order) + 2):
        if i < len(order):
            pair(*order[i])
        if 1 <= i <= len(order):
            plane(*order[i - 1])
        if i >= 2:
            line(*order[i - 2])
    for k in range(len(groups)):
        total(k)


def scatter_kernel(planes, count, *refs):
    grads, outs = refs[:count], refs[count : 2 * count]
    held = refs[2 * count : 2 * count + 4 * count]
    send, recv, local = refs[6 * count :]
    greet(near(planes))
    wires = Wires(send, recv)
    groups = [(grads[k], outs[k], *held[4 * k : 4 * k + 4]) for k in range(count)]
    scatter_steps(wires, local, planes, groups)
    wires.sent()


class Scatter:
    def __init__(self, wires, planes, groups):
        self.wires, self.planes, self.groups = wires, planes, groups
        h, z, c = place()
        self.h, self.z, self.c = h, z, c
        row = 2 * z + c
        self.sib = (h, 2 * z + 1 - c)
        self.hx, self.hy, self.hd = across(h, 1), across(h, 2), across(h, 3)
        self.xn, self.yn = (self.hx, row), (self.hy, row)
        self.to = [lax.rem(z + 1 + s, planes) for s in range(planes)]
        self.got = {}

    def post(self, k, s):
        grads, out, sibs, px, pz = self.groups[k]
        t = self.to[s]
        for q in (3, 1, 2, 0):
            th = across(self.h, q)
            self.got[k, s, q] = self.wires.copy(
                grads.at[th, t, 1 - self.c], sibs.at[th, t], self.sib
            )

    def pair(self, k, s):
        grads, out, sibs, px, pz = self.groups[k]
        t, rows = self.to[s], sibs.shape[2]
        a, b = split(rows)
        copy, got = self.wires.copy, self.got
        for q in (3, 1, 2, 0):
            got[k, s, q].wait_recv()
            th = across(self.h, q)
            own = grads.at[th, t, self.c]
            add_rows(own, [sibs.at[th, t]], rows)
            if q == 3:
                got[k, s, "xd"] = copy(own.at[a], px.at[t, 0].at[a], self.xn)
                got[k, s, "yd"] = copy(own.at[b], px.at[t, 0].at[b], self.yn)
            if q == 1:
                got[k, s, "x"] = copy(own.at[a], px.at[t, 1].at[a], self.xn)
            if q == 2:
                got[k, s, "y"] = copy(own.at[b], px.at[t, 1].at[b], self.yn)

    def plane(self, k, s):
        grads, out, sibs, px, pz = self.groups[k]
        t, rows = self.to[s], sibs.shape[2]
        a, b = split(rows)
        copy, got = self.wires.copy, self.got
        got[k, s, "xd"].wait_recv()
        own = grads.at[self.hy, t, self.c].at[a]
        add_rows(own, [px.at[t, 0].at[a]], a.size)
        got[k, s, "y2"] = copy(own, px.at[t, 2].at[a], self.yn)
        got[k, s, "yd"].wait_recv()
        own = grads.at[self.hx, t, self.c].at[b]
        add_rows(own, [px.at[t, 0].at[b]], b.size)
        got[k, s, "x2"] = copy(own, px.at[t, 2].at[b], self.xn)

    def line(self, k, s):
        grads, out, sibs, px, pz = self.groups[k]
        t = self.to[s]
        for part in ("x", "y2", "y", "x2"):
            self.got[k, s, part].wait_recv()
        own = grads.at[self.h, t, self.c]
        add_rows(own, [px.at[t, 1], px.at[t, 2]], sibs.shape[2])
        if s < self.planes - 1:
            self.got[k, s, "z"] = self.wires.copy(own, pz.at[s], (self.h, 2 * t + self.c))

    def total(self, k):
        grads, out, sibs, px, pz = self.groups[k]
        h, z, c = self.h, self.z, self.c
        for s in range(self.planes - 1):
            self.got[k, s, "z"].wait_recv()

        @pl.loop(0, out.shape[0] // 16)
        def _(i):
            at = pl.ds(pl.multiple_of(i * 16, 16), 16)
            value = grads[h, z, c, at, :].astype(jnp.float32)
            for s in range(self.planes - 1):
                value = value + pz[s, at, :].astype(jnp.float32)
            out[at, :] = value


def give_steps(wires, planes, parcels, out, other, keep):
    h, z, c = place()
    sib = (h, 2 * z + 1 - c)
    passed = wires.copy(parcels.at[1 - c], other, sib)
    passed.wait_recv()
    given = []
    for q in (3, 1, 2, 0):
        for s in range(planes - 1, -1, -1):
            th, tz = across(h, q), lax.rem(z + s, planes)
            mine = parcels.at[c, th, tz]
            add_rows(mine, [other.at[th, tz]], other.shape[2])
            if q or s:
                given.append(wires.copy(mine, out.at[h, z], (th, 2 * tz + c)))
    stay = pltpu.make_async_copy(parcels.at[c, h, z], out.at[h, z], keep)
    stay.start()
    return given, stay


def return_kernel(planes, parcels, out, other, send, recv, keep):
    greet(every_chip(planes))
    wires = Wires(send, recv)
    given, stay = give_steps(wires, planes, parcels, out, other, keep)
    for one in given:
        one.wait_recv()
    stay.wait()
    wires.sent()


def guarded(ok, act):
    if ok is None:
        act()
    else:
        pl.when(ok)(act)


class Lines:
    def __init__(self, send, recv):
        self.send, self.recv, self.used, self.made = send, recv, 0, []

    def make(self, src, dst, to, ok):
        i = self.used
        self.used += 1
        one = pltpu.make_async_remote_copy(
            src_ref=src,
            dst_ref=dst,
            send_sem=self.send.at[i],
            recv_sem=self.recv.at[i],
            device_id=to,
            device_id_type=MESH,
        )
        self.made.append((one, ok))
        return one

    def sent(self):
        for one, ok in self.made:
            guarded(ok, one.wait_send)


def line_steps(planes):
    return [0] + [d * s for s in range(1, planes) for d in (1, -1)]


class Gather:
    def __init__(self, wires, local, planes, pairs):
        self.wires, self.planes, self.pairs = wires, planes, pairs
        h, z, c = place()
        self.h, self.z, self.c = h, z, c
        row = 2 * z + c
        self.sib = (h, 2 * z + 1 - c)
        self.hx, self.hy, self.hd = across(h, 1), across(h, 2), across(h, 3)
        self.xn, self.yn = (self.hx, row), (self.hy, row)
        self.at, self.have, self.on = {0: z}, {0: None}, {}
        for s in line_steps(planes)[1:]:
            t = z - s
            self.have[s] = (t >= 0) & (t < planes)
            self.at[s] = jnp.clip(t, 0, planes - 1)
        for s in range(planes - 1):
            for d in (1, -1):
                u = z + d
                ok = (u >= 0) & (u < planes)
                self.on[d, s] = (ok & self.have[d * s]) if s else ok
        self.here = []
        for k, (x, out) in enumerate(pairs):
            one = pltpu.make_async_copy(x, out.at[h, z, c], local.at[k])
            one.start()
            self.here.append(one)
        self.line, self.copies = {}, {}

    def onward(self, k, d, s):
        x, out = self.pairs[k]
        t = self.at[d * s]
        ref = x if s == 0 else out.at[self.h, t, self.c]
        u = jnp.clip(self.z + d, 0, self.planes - 1)
        ok = self.on[d, s]
        one = self.wires.make(ref, out.at[self.h, t, self.c], (self.h, 2 * u + self.c), ok)
        self.line[k, d, s] = one
        guarded(ok, one.start)

    def launch(self, k, s):
        x, out = self.pairs[k]
        t, ok = self.at[s], self.have[s]
        here = out.at[self.h, t, self.c]
        ref = x if s == 0 else here
        if s == 0:
            self.onward(k, 1, 0)
            self.onward(k, -1, 0)
        else:
            d, a = (1, s) if s > 0 else (-1, -s)
            guarded(ok, self.line[k, d, a - 1].wait_recv)
            if a < self.planes - 1:
                self.onward(k, d, a)
        make = self.wires.make
        ones = [make(ref, here, to, ok) for to in (self.xn, self.yn, self.sib)]
        self.copies[k, s, "x"], self.copies[k, s, "y"], self.copies[k, s, "s"] = ones

        def act():
            for one in ones:
                one.start()

        guarded(ok, act)

    def relay(self, k, s):
        out = self.pairs[k][1]
        t, ok = self.at[s], self.have[s]
        first, second = split(out.shape[3])
        make, got = self.wires.make, self.copies
        gx, gy = out.at[self.hx, t, self.c], out.at[self.hy, t, self.c]
        got[k, s, "yd"] = make(gx.at[second], gx.at[second], self.yn, ok)
        got[k, s, "sx"] = make(gx, gx, self.sib, ok)
        got[k, s, "xd"] = make(gy.at[first], gy.at[first], self.xn, ok)
        got[k, s, "sy"] = make(gy, gy, self.sib, ok)

        def act():
            got[k, s, "x"].wait_recv()
            got[k, s, "yd"].start()
            got[k, s, "sx"].start()
            got[k, s, "y"].wait_recv()
            got[k, s, "xd"].start()
            got[k, s, "sy"].start()

        guarded(ok, act)

    def finish(self, k, s):
        out = self.pairs[k][1]
        t, ok = self.at[s], self.have[s]
        got = self.copies
        gd = out.at[self.hd, t, self.c]
        got[k, s, "sd"] = self.wires.make(gd, gd, self.sib, ok)

        def act():
            got[k, s, "yd"].wait_recv()
            got[k, s, "xd"].wait_recv()
            got[k, s, "sd"].start()

        guarded(ok, act)

    def done(self, k, s):
        if s == 0:
            self.here[k].wait()

        def act():
            for part in ("s", "sx", "sy", "sd"):
                self.copies[k, s, part].wait_recv()

        guarded(self.have[s], act)


def line_wires(planes, count):
    return count * (2 * planes - 1) * 9


def iota(shape, dim):
    return lax.broadcasted_iota(jnp.int32, shape, dim)


def ones_where(marks):
    return marks.astype(jnp.float32).astype(jnp.bfloat16)


def column(lines):
    turned = lines.T
    return jnp.concatenate([turned[:, i : i + 1] for i in range(lines.shape[0])], axis=0)


def prepare_kernel(planes, room, *refs):
    (tokens, picks, goals, segments, norms_in, bias_in, table) = refs[:7]
    (out_w, places_w, qkv_w, up_w) = refs[7:11]
    (numbers, small_all, home, rank_out, which_out, rounds, box) = refs[11:18]
    (misc_all, wq_all, wu_all) = refs[18:21]
    (block, small, misc, wq, wu, parcels, send, recv, send2, recv2, local) = refs[21:]
    low, f32 = jnp.bfloat16, jnp.float32
    h, z, c = place()
    row = 2 * z + c
    rows = 2 * planes
    device = h * rows + row
    part = table.shape[0]
    lines = tokens.shape[0]
    each = lines // 4
    peers = [(s, e) for s in range(planes) for e in range(2) if s or e]
    peers = [(h, 2 * lax.rem(z + s, planes) + lax.rem(c + e, 2)) for s, e in peers]
    chips = [
        (across(h, q), 2 * lax.rem(z + s, planes) + c) for q in (1, 2, 3) for s in range(planes)
    ]
    padding = ones_where(segments[...] == SEQ - 1)
    at = iota((128, picks.shape[1]), 0) == lax.rem(picks[...], 128)
    padded_at = mul(padding, ones_where(at))
    line = iota((lines, picks.shape[1]), 0) == lax.div(picks[...], 128)
    padded_at = jnp.sum(jnp.where(line, padded_at, 0.0), axis=0, keepdims=True)
    goal = jnp.where(padded_at == 0.0, goals[...], -1)
    block[...] = jnp.zeros_like(block)
    block[0:lines, :] = tokens[...]
    for i in range(goal.shape[1] // 128):
        block[lines + i : lines + i + 1, :] = goal[:, 128 * i : 128 * (i + 1)]
    share, width = norms_in.shape[1], table.shape[1]
    small[...] = jnp.zeros_like(small)
    small[0:8, 0:share] = norms_in[...].astype(low).astype(f32)
    small[8:9, 0 : bias_in.shape[1]] = bias_in[...].astype(low).astype(f32)
    greet(peers + chips)
    posts = Wires(send2, recv2)
    mine = pltpu.make_async_copy(block, numbers.at[row], local.at[0])
    mine.start()
    ids = [posts.copy(block, numbers.at[row], to) for to in peers]
    spread = spread_start(posts, local.at[1], planes, lambda th, tz: small, small_all)
    wq[...] = qkv_w[...].astype(low)
    wu[...] = up_w[...].astype(low)
    places_row = jnp.concatenate([places_w[...], jnp.zeros((share, width - SEQ), f32)], axis=1)
    misc[...] = jnp.concatenate([out_w[...], places_row], axis=0).astype(low)
    lines_of = Lines(send, recv)
    pairs = [(misc, misc_all), (wq, wq_all), (wu, wu_all)]
    gather = Gather(lines_of, local.at[pl.ds(2, 3)], planes, pairs)
    for k in range(3):
        gather.launch(k, 0)
    for one in ids:
        one.wait_recv()
    mine.wait()

    everyone = numbers[...][:, :lines, :].reshape(rows * lines, 128)
    total = rows * lines
    by_row, by_col = iota((total, total), 0), iota((total, total), 1)

    def parts(n):
        return n // (2 * lines), (n // lines) % 2, (n // each) % 4, n % each

    def parts_of(n):
        plane = lax.div(n, 2 * lines)
        core = lax.rem(lax.div(n, lines), 2)
        head = lax.rem(lax.div(n, each), 4)
        return plane, core, head, lax.rem(n, each)

    pr, cr, hr, ir = parts_of(by_row)
    pc, cc, hc, ic = parts_of(by_col)
    same = (pr == pc) & (hr == hc)
    earlier = same & (cc * each + ic < cr * each + ir)
    earlier = ones_where(earlier)
    before = ones_where(iota((128, 128), 0) < iota((128, 128), 1))
    ones = jnp.ones((128, 128), low)

    near_id = everyone - device * part
    inside = (near_id >= 0) & (near_id < part)
    marks = ones_where(inside)
    in_row = mul(marks, ones).astype(low)
    rank = (mul(marks, before) + mul(earlier, in_row)).astype(jnp.int32)
    rank = jnp.where(inside, rank, -1)

    counts = jnp.zeros((total, 128), f32)
    for d in range(4 * rows):
        owned = ones_where((everyone >= d * part) & (everyone < (d + 1) * part))
        counts = counts + mul(owned, ones_where(iota((128, 128), 1) == d))
    fullest = jnp.max(mul(ones_where(same), counts.astype(low)))
    rounds[...] = jnp.full(rounds.shape, fullest.astype(jnp.int32))

    slot = iota((room, 128), 0)
    low_table = table[...].astype(low)
    vocab = iota((room, part), 1)
    for th in range(4):
        for tz in range(planes):
            found = jnp.zeros((room, 128), jnp.int32)
            for core in range(2):
                for i in range(each):
                    n = (tz * 2 + core) * lines + th * each + i
                    hit = rank[n : n + 1, :] == slot
                    found = found + jnp.where(hit, near_id[n : n + 1, :] + 1, 0)
            which = jnp.sum(found.astype(f32), axis=1, keepdims=True).astype(jnp.int32) - 1
            at = (th * planes + tz) * room
            which_out[at : at + room, :] = which
            parcels[th, tz] = mul(ones_where(which == vocab), low_table).astype(low)
    post = spread_start(posts, local.at[5], planes, lambda th, tz: parcels.at[th, tz], box)

    for k in range(3):
        gather.launch(k, 1)
        gather.launch(k, -1)
    for k in range(3):
        gather.relay(k, 0)

    ids_here = [
        numbers[2 * z + core, pl.ds(each * h, each), :].astype(f32) for core in range(2)
    ]
    own = column(numbers[row, pl.ds(each * h, each), :].astype(f32))
    count = each * 128

    def owners(values):
        owner = jnp.zeros(values.shape, f32)
        for d in range(1, 4 * rows):
            owner = owner + jnp.where(values >= float(d * part), 1.0, 0.0)
        return owner

    own_owner = owners(own)
    own_spot = iota((count, 128), 0) + c * count
    ahead = jnp.zeros((count, 128), f32)
    for core in range(2):
        them = owners(ids_here[core])
        for i in range(each):
            spot = core * count + 128 * i + iota((count, 128), 1)
            hit = (own_owner == them[i : i + 1, :]) & (spot < own_spot)
            ahead = ahead + jnp.where(hit, 1.0, 0.0)
    rank_out[...] = jnp.sum(ahead, axis=1, keepdims=True).astype(jnp.int32)
    owner = own_owner.astype(jnp.int32)
    home[...] = lax.rem(owner, 2) * (2 * rows) + lax.div(owner, 2)

    order = [(k, s) for k in range(3) for s in (1, -1)]
    order += [(k, s) for a in range(2, planes) for k in range(3) for s in (a, -a)]
    for k in range(3):
        gather.finish(k, 0)
    lag = 3
    for i in range(len(order) + 2 * lag):
        if 6 <= i < len(order):
            gather.launch(*order[i])
        if lag <= i < len(order) + lag:
            gather.relay(*order[i - lag])
        if i >= 2 * lag:
            gather.finish(*order[i - 2 * lag])
    spread_finish(posts, planes, small_all, spread)
    spread_finish(posts, planes, box, post)
    for k in range(3):
        for s in line_steps(planes):
            gather.done(k, s)
    posts.sent()
    lines_of.sent()


def mul(left, right, left_dim=1, right_dim=0):
    return lax.dot_general(
        left, right, (((left_dim,), (right_dim,)), ((), ())), preferred_element_type=jnp.float32
    )


def unit_of(values):
    center = values - jnp.mean(values, axis=-1, keepdims=True)
    scale = lax.rsqrt(jnp.mean(center * center, axis=-1, keepdims=True) + EPSILON)
    return center * scale, scale


ERF_TOP = (
    -2.72614225801306e-10,
    2.77068142495902e-08,
    -2.10102402082508e-06,
    -5.69250639462346e-05,
    -7.34990630326855e-04,
    -2.95459980854025e-03,
    -1.60960333262415e-02,
)
ERF_LOW = (
    -1.45660718464996e-05,
    -2.13374055278905e-04,
    -1.68282697438203e-03,
    -7.37332916720468e-03,
    -1.42647390514189e-02,
)


def erf(x):
    x = jnp.clip(x, -4.0, 4.0)
    square = x * x
    top = jnp.full_like(x, ERF_TOP[0])
    for c in ERF_TOP[1:]:
        top = top * square + c
    bottom = jnp.full_like(x, ERF_LOW[0])
    for c in ERF_LOW[1:]:
        bottom = bottom * square + c
    return x * top / bottom


def gelu_parts(u, ramp):
    cdf = 0.5 + 0.5 * erf(u * (0.5**0.5))
    density = jnp.exp(-0.5 * u * u) * 0.3989422804014327
    return u * cdf * ramp, (cdf + u * density) * ramp


def head_slice(ref, head, part):
    group, i = head // 3, head % 3
    start = (3 * i + part) * HD
    return ref[group, :, start : start + HD]


def masked_scores(q, k, labels_col, labels_row):
    s = mul(q, k, 1, 1) * HD**-0.5
    return jnp.where(labels_col == labels_row, s, -1000000000.0)


def forward_kernel(planes, room, *refs):
    (box, misc_all, wq_all, wu_all, wd, home, ranks, extra) = refs[:8]
    (lab_col, lab_row, norms, bias, ramp, chosen) = refs[8:14]
    wd_all = refs[14]
    (unit0, scale0, mixed, lse, heads, unit1, scale1, active, slope, unit2, scale2, picked) = refs[
        15:27
    ]
    (misc_v, wq_v, wu_v, wd_v, hidden, total, lab_one) = refs[27:34]
    send, recv, local, loads = refs[34:]
    low = jnp.bfloat16
    h, z, c = place()
    greet(near(planes))
    lines = Lines(send, recv)
    pairs = [(wd, wd_all)]
    gather = Gather(lines, local, planes, pairs)
    tokens, width = unit0.shape

    def load(i, src, dst):
        one = pltpu.make_async_copy(src, dst, loads.at[i])
        one.start()
        return one

    ready_misc = load(0, misc_all, misc_v)
    ready_q = load(1, wq_all, wq_v)

    def start_norm():
        lab_one[...] = column(lab_col[...].astype(jnp.float32)).astype(jnp.int32)
        ready_misc.wait()
        spots = iota((tokens, box.shape[3] * 8 * planes), 1)
        seat = jnp.where(ranks[...] < room, home[...] * room + ranks[...], -1)
        rows = box[...].reshape(-1, width)
        looked = mul(ones_where(seat == spots), rows) + extra[...]
        pieces = misc_v[...].astype(jnp.float32)
        share = misc_v.shape[3] // 2
        places = pieces[:, :, :, share:, :SEQ].reshape(width, SEQ).T
        unit, scale = unit_of(looked + places)
        unit0[...] = unit
        scale0[...] = scale
        hidden[...] = unit * norms[0:1, :] + norms[1:2, :]

    def project(group):
        weight = wq_v[group].reshape(width, wq_v.shape[4])
        mixed[group] = mul(hidden[...].astype(low), weight).astype(low)

    def attend(pair):
        outs = []
        for head in (2 * pair, 2 * pair + 1):
            q, k, v = (head_slice(mixed, head, j) for j in range(3))
            s = masked_scores(q, k, lab_one[...], lab_row[...])
            top = jnp.max(s, axis=1, keepdims=True)
            e = jnp.exp(s - top)
            sums = jnp.sum(e, axis=1, keepdims=True)
            lse[:, head : head + 1] = top + jnp.log(sums)
            p = (e / sums).astype(low)
            scale = 1.0 if head < OLD_HEADS else STEP / RAMP
            outs.append((mul(p, v) * scale).astype(low))
        heads[:, 2 * HD * pair : 2 * HD * (pair + 1)] = jnp.concatenate(outs, axis=1)

    def middle():
        share = misc_v.shape[3] // 2
        weight = misc_v[...].astype(jnp.float32)[:, :, :, :share].reshape(width, width).astype(low)
        value = hidden[...] + mul(heads[...], weight, 1, 1) + norms[6:7, :]
        unit, scale = unit_of(value)
        unit1[...] = unit
        scale1[...] = scale
        hidden[...] = unit * norms[2:3, :] + norms[3:4, :]
        total[...] = hidden[...] + norms[7:8, :]

    def chunk(t):
        one = load(2, wu_all.at[:, t], wu_v.at[0])
        two = load(3, wd_all.at[:, t], wd_v.at[0])
        one.wait()
        units = wu_v.shape[1] * 2 * wu_v.shape[3]
        u = mul(hidden[...].astype(low), wu_v[0].reshape(units, width), 1, 1) + bias[t]
        value, rise = gelu_parts(u, ramp[t])
        value = value.astype(low)
        active[t] = value
        slope[t] = rise.astype(low)
        two.wait()
        total[...] += mul(value, wd_v[0].reshape(units, width))

    def last():
        unit, scale = unit_of(total[...])
        unit2[...] = unit
        scale2[...] = scale
        final = (unit * norms[4:5, :] + norms[5:6, :]).astype(low)
        marks = ones_where(iota((tokens, chosen.shape[1]), 0) == chosen[...])
        picked[...] = mul(marks, final, 0, 0).astype(low)

    near_first = []
    for j in range(planes):
        spot = jnp.int32(0)
        for zz in range(planes):
            ranked = sorted(range(planes), key=lambda t: (abs(t - zz), t))
            spot = jnp.where(z == zz, ranked[j], spot)
        near_first.append(spot)

    lag = 3
    whole = [(0, s) for s in line_steps(planes)]
    events = []
    for i in range(len(whole) + 2 * lag):
        if i < len(whole):
            events.append((gather.launch, *whole[i]))
        if lag <= i < len(whole) + lag:
            events.append((gather.relay, *whole[i - lag]))
        if i >= 2 * lag:
            events.append((gather.finish, *whole[i - 2 * lag]))

    def settle(a):
        for s in (a, -a) if a else (0,):
            gather.done(0, s)

    def take(upto):
        while events and (upto is None or upto > 0):
            event, k, s = events.pop(0)
            event(k, s)
            if upto is not None:
                upto -= 1

    take(3)
    work = [start_norm, lambda: (ready_q.wait(), project(0))]
    work += [functools.partial(project, g) for g in range(1, 4)]
    work += [functools.partial(attend, p) for p in range(6)]
    work += [middle]
    stop = len(events)
    count = len(work)
    shares = [stop * (i + 1) // count - stop * i // count for i in range(count)]
    for act, some in zip(work, shares):
        act()
        take(some)
    for a in range(planes):
        settle(a)
        chunk(near_first[a])
    last()
    lines.sent()


def unit_back(grad, unit, scale, gain):
    inner = grad * gain
    back = scale * (
        inner
        - jnp.mean(inner, axis=-1, keepdims=True)
        - unit * jnp.mean(inner * unit, axis=-1, keepdims=True)
    )
    return (back, grad * unit)


def backward_kernel(planes, room, *refs):
    (picked, chosen, norms, lab_lines, lab_row, home, ranks) = refs[:7]
    (scale0, scale1, scale2, lse) = refs[7:11]
    (unit0, unit1, unit2, mixed, heads, active, slope) = refs[11:18]
    (misc_all, wq_all, wu_all, wd_all) = refs[18:22]
    (back, up_sum, down_sum, q_sum, misc_sum, grad_low) = refs[22:28]
    (ups, downs, qs, miscs) = (refs[28 + 4 * k : 32 + 4 * k] for k in range(4))
    (parcels, other, unit_v, grad, extra, act_low, heads_v) = refs[44:51]
    (wu_v, wd_v, active_v, slope_v, wq_v, mixed_v, norm_sums, lab_one) = refs[51:59]
    send, recv, local = refs[59:]
    low, f32 = jnp.bfloat16, jnp.float32
    h, z, c = place()
    tokens, width = unit_v.shape
    units = active_v.shape[1]
    share = wu_v.shape[2]
    lanes = mixed_v.shape[1]
    up_g, down_g, q_g, misc_g = ups[0], downs[0], qs[0], miscs[0]
    loads = {}

    def load(i, src, dst):
        one = pltpu.make_async_copy(src, dst, local.at[i])
        one.start()
        loads[i] = one

    def ready(*which):
        for i in which:
            loads.pop(i).wait()

    greet(every_chip(planes))
    wires = Wires(send, recv)
    sums = [up_sum, down_sum, q_sum, misc_sum]
    groups = [(g[0], out, *g[1:]) for g, out in zip((ups, downs, qs, miscs), sums)]
    scatter = Scatter(wires, planes, groups)
    order = scatter.to
    load(0, unit2, unit_v)
    load(1, wd_all.at[:, order[0]], wd_v)
    load(2, active.at[order[0]], active_v)
    load(3, slope.at[order[0]], slope_v)
    load(4, wu_all.at[:, order[0]], wu_v)
    load(5, heads, heads_v)
    load(6, misc_all, misc_g)

    def row_sum(i, values):
        norm_sums[i : i + 1, :] = jnp.sum(values, axis=0, keepdims=True)

    def start():
        lab_one[...] = column(lab_lines[...].astype(f32)).astype(jnp.int32)
        marks = (iota((tokens, chosen.shape[1]), 0) == chosen[...]).astype(f32)
        final = lax.dot_general(
            marks,
            picked[...],
            (((1,), (0,)), ((), ())),
            precision=lax.Precision.HIGHEST,
            preferred_element_type=f32,
        )
        ready(0)
        value, gains = unit_back(final, unit_v[...], scale2[...], norms[4:5, :])
        row_sum(4, gains)
        row_sum(5, final)
        row_sum(7, value)
        grad[...] = value
        grad_low[...] = value.astype(low)
        load(0, unit1, unit_v)
        ready(0)
        act_low[...] = (unit_v[...] * norms[2:3, :] + norms[3:4, :]).astype(low)
        extra[0:tokens, :] = jnp.zeros((tokens, width), f32)

    def spread_out(ref, t, value):
        parts = value.reshape(4, 2, value.shape[0] // 8, value.shape[1])
        for th in range(4):
            ref[th, t] = parts[th]

    def chunk(s):
        t = order[s]
        ahead = order[s + 1] if s + 1 < planes else None
        ready(1, 2, 3, 4)
        pulled = mul(grad_low[...], wd_v[...].reshape(units, width), 1, 1)
        if ahead is not None:
            load(1, wd_all.at[:, ahead], wd_v)
        spread_out(down_g, t, mul(active_v[...], grad_low[...], 0, 0).astype(low))
        if ahead is not None:
            load(2, active.at[ahead], active_v)
        pulled = pulled * slope_v[...].astype(f32)
        if ahead is not None:
            load(3, slope.at[ahead], slope_v)
        sums_row = jnp.sum(pulled, axis=0, keepdims=True)
        col = jnp.broadcast_to(sums_row, (8, units)).T[:, 0:1]
        first = iota((units, q_g.shape[4] - lanes), 1) == 0
        bias = jnp.where(first, col, 0.0).astype(low).reshape(4, 2, share, -1)
        for th in range(4):
            q_g[th, t, :, :, lanes:] = bias[th]
        pulled = pulled.astype(low)
        spread_out(up_g, t, mul(pulled, act_low[...], 0, 0).astype(low))
        extra[0:tokens, :] += mul(pulled, wu_v[...].reshape(units, width))
        if ahead is not None:
            load(4, wu_all.at[:, ahead], wu_v)

    def middle():
        total = grad[...] + extra[0:tokens, :]
        value, gains = unit_back(total, unit_v[...], scale1[...], norms[2:3, :])
        row_sum(2, gains)
        row_sum(3, total)
        row_sum(6, value)
        load(0, unit0, unit_v)
        load(7, wq_all.at[0], wq_v)
        load(8, mixed.at[0], mixed_v)
        grad[...] = value
        value = value.astype(low)
        ready(5, 6)
        extra[...] = mul(value, heads_v[...], 0, 0)
        weight = misc_g[...].astype(f32)[:, :, :, : misc_g.shape[3] // 2]
        weight = weight.reshape(width, width).astype(low)
        heads_v[...] = mul(value, weight).astype(low)
        ready(0)
        act_low[...] = (unit_v[...] * norms[0:1, :] + norms[1:2, :]).astype(low)

    def attend(group):
        ready(7, 8)
        parts = []
        for i in range(3):
            head = 3 * group + i
            q, k, v = (mixed_v[:, (3 * i + j) * HD : (3 * i + j + 1) * HD] for j in range(3))
            pull = heads_v[:, head * HD : (head + 1) * HD]
            if head >= OLD_HEADS:
                pull = (pull.astype(f32) * (STEP / RAMP)).astype(low)
            s = masked_scores(q, k, lab_one[...], lab_row[...])
            p = jnp.exp(s - lse[:, head : head + 1])
            of_v = mul(p.astype(low), pull, 0, 0)
            of_p = mul(pull, v, 1, 1)
            ds = (p * (of_p - jnp.sum(of_p * p, axis=1, keepdims=True))).astype(low)
            of_q = mul(ds, k) * HD**-0.5
            of_k = mul(ds, q, 0, 0) * HD**-0.5
            parts += [of_q, of_k, of_v]
        pulled = jnp.concatenate(parts, axis=1).astype(low)
        if group < 3:
            load(8, mixed.at[group + 1], mixed_v)
        grad[...] += mul(pulled, wq_v[...].reshape(width, lanes), 1, 1)
        if group < 3:
            load(7, wq_all.at[group + 1], wq_v)
        value = mul(act_low[...], pulled, 0, 0).astype(low)
        q_g[group, :, :, :, 0:lanes] = value.reshape(planes, 2, width // (2 * planes), lanes)

    def finish():
        total = grad[...]
        value, gains = unit_back(total, unit_v[...], scale0[...], norms[0:1, :])
        row_sum(0, gains)
        row_sum(1, total)
        seat = jnp.where(ranks[...] < room, home[...] * room + ranks[...], -1)
        marks = ones_where(seat == iota((tokens, parcels.shape[3] * 8 * planes), 1))
        grad_low[...] = value.astype(low)
        parcels[...] = mul(marks, grad_low[...], 0, 0).astype(low).reshape(parcels.shape)
        rest = jnp.zeros((width, width - tokens - 8), f32)
        rows = jnp.concatenate([value.T, norm_sums[...].T, rest], axis=1)
        split_rows = misc_g.shape[3] // 2
        shape = (4, planes, 2, split_rows, width)
        both = jnp.concatenate([extra[...].reshape(shape), rows.reshape(shape)], axis=3)
        misc_g[...] = both.astype(low)

    last = planes - 1
    start()
    for s in range(planes):
        chunk(s)
        for k in (0, 1):
            scatter.post(k, s)
        for k in (0, 1):
            if s >= 1:
                scatter.pair(k, s - 1)
        if s == last:
            for k in (0, 1):
                scatter.plane(k, 0)
    middle()
    for k in (0, 1):
        scatter.pair(k, last)
    for k in (0, 1):
        scatter.line(k, 0)
    ahead = [(f, k, s) for s in range(1, planes) for f in (scatter.plane, scatter.line) for k in (0, 1)]
    cuts = [len(ahead) * i // 5 for i in range(6)]
    for group in range(4):
        attend(group)
        for f, k, s in ahead[cuts[group] : cuts[group + 1]]:
            f(k, s)
    for s in range(planes):
        scatter.post(2, s)
    finish()
    given, stay = give_steps(wires, planes, parcels, back, other, local.at[9])
    for s in range(planes):
        scatter.post(3, s)
    for f, k, s in ahead[cuts[4] :]:
        f(k, s)
    rest = [(k, s) for k in (2, 3) for s in range(planes)]
    for i in range(len(rest) + 4):
        if i < len(rest):
            scatter.pair(*rest[i])
        if 2 <= i < len(rest) + 2:
            scatter.plane(*rest[i - 2])
        if i >= 4:
            scatter.line(*rest[i - 4])
    for k in range(4):
        scatter.total(k)
    for one in given:
        one.wait_recv()
    stay.wait()
    wires.sent()


def params(number):
    return pltpu.CompilerParams(
        collective_id=number, has_side_effects=True, vmem_limit_bytes=56 << 20
    )


def dma(count):
    return pltpu.SemaphoreType.DMA((count,))


def gather_wires(planes, count):
    return count * (planes - 1 + planes * 8)


def spread_wires(planes):
    return 2 * 4 * planes


def scatter_wires(planes, count):
    return count * planes * 11


def held_scratch(planes, shape):
    rows, lanes = shape
    return [
        pltpu.VMEM((4, planes, rows, lanes), jnp.bfloat16),
        pltpu.VMEM((4, planes, rows, lanes), jnp.bfloat16),
        pltpu.VMEM((planes, 3, rows, lanes), jnp.bfloat16),
        pltpu.VMEM((planes - 1, rows, lanes), jnp.bfloat16),
    ]


class Kernels:
    def __init__(self, planes):
        self.planes = planes

    def prepare(self, token_ids, masked_pos, masked_target, segment_ids, norms, bias, table, rest):
        planes = self.planes
        low, f32, i32 = jnp.bfloat16, jnp.float32, jnp.int32
        out_w, places_w, qkv_w, up_w = rest
        part, width = table.shape
        lines = token_ids.shape[0] // 128
        block = (-(-(lines + masked_pos.shape[1] // 128) // 8) * 8, 128)
        small = (16, 128)
        seq = token_ids.shape[0] // 4
        misc = (2 * norms.shape[1], width)
        shape = jax.ShapeDtypeStruct
        count = line_wires(planes, 3)
        posts = 2 * planes - 1 + 2 * spread_wires(planes)
        return pl.pallas_call(
            functools.partial(prepare_kernel, planes, ROOM),
            out_shape=[
                shape((2 * planes, *block), i32),
                shape((2, 4, planes, *small), f32),
                shape((seq, 1), i32),
                shape((seq, 1), i32),
                shape((4 * planes * ROOM, 1), i32),
                shape((8, 128), i32),
                shape((2, 4, planes, ROOM, width), low),
                shape((4, planes, 2, *misc), low),
                shape((4, planes, 2, *qkv_w.shape), low),
                shape((4, planes, 2, *up_w.shape), low),
            ],
            in_specs=[VMEM] * 11,
            out_specs=[VMEM] * 6 + [ANY] * 4,
            scratch_shapes=[
                pltpu.VMEM(block, i32),
                pltpu.VMEM(small, f32),
                pltpu.VMEM(misc, low),
                pltpu.VMEM(qkv_w.shape, low),
                pltpu.VMEM(up_w.shape, low),
                pltpu.VMEM((4, planes, ROOM, width), low),
                dma(count),
                dma(count),
                dma(posts),
                dma(posts),
                dma(6),
            ],
            compiler_params=params(1),
            name="prepare",
        )(
            token_ids.reshape(lines, 128),
            masked_pos,
            masked_target,
            segment_ids.reshape(lines, 128),
            norms,
            bias.reshape(1, -1),
            table,
            out_w,
            places_w,
            qkv_w,
            up_w,
        )

    def forward(self, box, gathered, blocks, home, ranks, extra, labels, norms, bias, ramp, chosen):
        planes = self.planes
        low, f32 = jnp.bfloat16, jnp.float32
        tokens, width = extra.shape
        units = bias.shape[2]
        whole = [jax.ShapeDtypeStruct((4, planes, 2, *b.shape), b.dtype) for b in blocks]
        saved = [
            ((tokens, width), f32),
            ((tokens, 1), f32),
            ((4, tokens, gathered[1].shape[4]), low),
            ((tokens, 128), f32),
            ((tokens, width), low),
            ((tokens, width), f32),
            ((tokens, 1), f32),
            ((planes, tokens, units), low),
            ((planes, tokens, units), low),
            ((tokens, width), f32),
            ((tokens, 1), f32),
            ((chosen.shape[0], width), low),
        ]
        count = line_wires(planes, 1)
        share = blocks[0].shape[0]
        result = pl.pallas_call(
            functools.partial(forward_kernel, planes, ROOM),
            out_shape=whole + [jax.ShapeDtypeStruct(s, t) for s, t in saved],
            in_specs=[VMEM] + [ANY] * 4 + [VMEM] * 9,
            out_specs=[ANY] + [VMEM] * len(saved),
            scratch_shapes=[
                pltpu.VMEM(gathered[0].shape, low),
                pltpu.VMEM(gathered[1].shape, low),
                pltpu.VMEM((1, 4, 2, share, width), low),
                pltpu.VMEM((1, 4, 2, share, width), low),
                pltpu.VMEM((tokens, width), f32),
                pltpu.VMEM((tokens, width), f32),
                pltpu.VMEM((tokens, 1), jnp.int32),
                dma(count),
                dma(count),
                dma(1),
                dma(4),
            ],
            compiler_params=params(2),
            name="forward",
        )(
            box,
            *gathered,
            *blocks,
            home,
            ranks,
            extra,
            labels.reshape(-1, 128),
            labels.reshape(1, -1),
            norms,
            bias,
            ramp,
            chosen.reshape(1, -1),
        )
        return result[:1], result[1:]

    def deliver(self, parcels):
        planes = self.planes
        wires = spread_wires(planes)
        return pl.pallas_call(
            functools.partial(deliver_kernel, planes),
            out_shape=jax.ShapeDtypeStruct((2, *parcels.shape), parcels.dtype),
            in_specs=[ANY],
            out_specs=ANY,
            scratch_shapes=[dma(wires), dma(wires), pltpu.SemaphoreType.DMA],
            compiler_params=params(3),
            name="deliver",
        )(parcels)

    def rows(self, block):
        planes = self.planes
        wires = gather_wires(planes, 1)
        return pl.pallas_call(
            functools.partial(gather_kernel, planes, 1),
            out_shape=jax.ShapeDtypeStruct((4, planes, 2, *block.shape), block.dtype),
            in_specs=[ANY],
            out_specs=ANY,
            scratch_shapes=[dma(wires), dma(wires), dma(1)],
            compiler_params=params(4),
            name="rows",
        )(block)

    def small(self, block, number):
        planes = self.planes
        wires = spread_wires(planes)
        return pl.pallas_call(
            functools.partial(small_kernel, planes),
            out_shape=jax.ShapeDtypeStruct((2, 4, planes, *block.shape), block.dtype),
            in_specs=[VMEM],
            out_specs=VMEM,
            scratch_shapes=[dma(wires), dma(wires), pltpu.SemaphoreType.DMA],
            compiler_params=params(number),
            name="small",
        )(block)

    def scatter_rows(self, grads):
        planes = self.planes
        shape = grads.shape[3:]
        wires = scatter_wires(planes, 1)
        return pl.pallas_call(
            functools.partial(scatter_kernel, planes, 1),
            out_shape=jax.ShapeDtypeStruct(shape, jnp.float32),
            in_specs=[ANY],
            out_specs=VMEM,
            scratch_shapes=held_scratch(planes, shape) + [dma(wires), dma(wires), dma(planes)],
            compiler_params=params(7),
            name="scatter_rows",
        )(grads)

    def hand_back(self, parcels):
        planes = self.planes
        layer = parcels.shape[1:]
        wires = spread_wires(planes)
        return pl.pallas_call(
            functools.partial(return_kernel, planes),
            out_shape=jax.ShapeDtypeStruct(layer, parcels.dtype),
            in_specs=[VMEM],
            out_specs=ANY,
            scratch_shapes=[pltpu.VMEM(layer, parcels.dtype)]
            + [dma(wires), dma(wires), pltpu.SemaphoreType.DMA],
            compiler_params=params(9),
            name="hand_back",
        )(parcels)

    def backward(self, grad_picked, chosen, norms, labels, home, ranks, saved, gathered):
        planes = self.planes
        low, f32 = jnp.bfloat16, jnp.float32
        unit0, scale0, mixed, lse, heads, unit1, scale1, active, slope, unit2, scale2 = saved
        misc_all, wq_all, wu_all, wd_all = gathered
        tokens, width = unit0.shape
        share = wu_all.shape[3]
        rows, lanes = wq_all.shape[3:]
        wide = -(-(lanes + 1) // 128) * 128
        blocks = [(share, width), (share, width), (rows, wide), misc_all.shape[3:]]
        count = scatter_wires(planes, 4) + spread_wires(planes)

        def held(shape):
            n, m = shape
            return [
                pltpu.VMEM((4, planes, 2, n, m), low),
                pltpu.VMEM((4, planes, n, m), low),
                pltpu.VMEM((planes, 3, n, m), low),
                pltpu.VMEM((planes - 1, n, m), low),
            ]

        units = active.shape[2]
        out = pl.pallas_call(
            functools.partial(backward_kernel, planes, ROOM),
            out_shape=[jax.ShapeDtypeStruct((4, planes, ROOM, width), low)]
            + [jax.ShapeDtypeStruct(b, f32) for b in blocks]
            + [jax.ShapeDtypeStruct((tokens, width), low)],
            in_specs=[VMEM] * 11 + [ANY] * 11,
            out_specs=[ANY] + [VMEM] * 5,
            scratch_shapes=[x for b in blocks for x in held(b)]
            + [
                pltpu.VMEM((2, 4, planes, ROOM, width), low),
                pltpu.VMEM((4, planes, ROOM, width), low),
                pltpu.VMEM((tokens, width), f32),
                pltpu.VMEM((tokens, width), f32),
                pltpu.VMEM((width, width), f32),
                pltpu.VMEM((tokens, width), low),
                pltpu.VMEM((tokens, width), low),
                pltpu.VMEM((4, 2, share, width), low),
                pltpu.VMEM((4, 2, share, width), low),
                pltpu.VMEM((tokens, units), low),
                pltpu.VMEM((tokens, units), low),
                pltpu.VMEM((planes, 2, rows, lanes), low),
                pltpu.VMEM((tokens, lanes), low),
                pltpu.VMEM((8, width), f32),
                pltpu.VMEM((tokens, 1), jnp.int32),
                dma(count),
                dma(count),
                dma(12),
            ],
            compiler_params=pltpu.CompilerParams(
                collective_id=8, has_side_effects=True, vmem_limit_bytes=62 << 20
            ),
            name="backward",
        )(
            grad_picked,
            chosen.reshape(1, -1),
            norms,
            labels.reshape(-1, 128),
            labels.reshape(1, -1),
            home,
            ranks,
            scale0,
            scale1,
            scale2,
            lse,
            unit0,
            unit1,
            unit2,
            mixed,
            heads,
            active,
            slope,
            misc_all,
            wq_all,
            wu_all,
            wd_all,
        )
        back, up, down, q, misc, of_start = out
        return back, up, down, q[:, :lanes], q[:, lanes], misc, of_start


class Plain:
    def __init__(self, planes):
        self.planes = planes

    def prepare(self, token_ids, masked_pos, masked_target, segment_ids, norms, bias, table, rest):
        return prepare_plain(
            self, token_ids, masked_pos, masked_target, segment_ids, norms, bias, table, rest
        )

    def gather(self, block):
        whole = lax.all_gather(block, ("head", "row"))
        return whole.reshape(4, self.planes, 2, *block.shape)

    def forward(self, box, gathered, blocks, home, ranks, extra, labels, norms, bias, ramp, chosen):
        whole = [self.gather(b) for b in blocks]
        seat = jnp.where(ranks < ROOM, home * ROOM + ranks, -1)
        saved = forward_plain(
            box, [*gathered, *whole], seat, extra, labels, norms, bias, ramp, chosen
        )
        return whole, saved

    def deliver(self, parcels):
        shape = parcels.shape
        both = jnp.broadcast_to(parcels[:, :, None], (*shape[:2], 2, *shape[2:]))
        flat = both.reshape(8 * self.planes, *shape[2:])
        got = lax.all_to_all(flat, ("head", "row"), split_axis=0, concat_axis=0, tiled=True)
        return jnp.moveaxis(got.reshape(4, self.planes, 2, *shape[2:]), 2, 0)

    def rows(self, block):
        return self.gather(block)

    def small(self, block, number):
        return jnp.moveaxis(self.gather(block), 2, 0)

    def scatter_rows(self, grads):
        flat = grads.reshape(-1, grads.shape[-1]).astype(jnp.float32)
        return lax.psum_scatter(flat, ("head", "row"), scatter_dimension=0, tiled=True)

    def backward(self, grad_picked, chosen, norms, labels, home, ranks, saved, gathered):
        return backward_plain(
            self, grad_picked, chosen, norms, labels, home, ranks, saved, gathered
        )

    def hand_back(self, parcels):
        shape = parcels.shape
        flat = jnp.moveaxis(parcels, 0, 2).reshape(8 * self.planes, *shape[3:])
        got = lax.all_to_all(flat, ("head", "row"), split_axis=0, concat_axis=0, tiled=True)
        got = got.reshape(4, self.planes, 2, *shape[3:]).astype(jnp.float32)
        return jnp.sum(got, axis=2).astype(parcels.dtype)


def contract(left, right, left_dim, right_dim):
    return lax.dot_general(
        left, right, (((left_dim,), (right_dim,)), ((), ())), preferred_element_type=jnp.float32
    )


def by_plane(blocks):
    planes, lanes = blocks.shape[1], blocks.shape[4]
    return blocks.transpose(1, 0, 2, 3, 4).reshape(planes, -1, lanes)


def heads_of(mixed):
    tokens = mixed.shape[1]
    parts = mixed.reshape(4, tokens, -1, 3, HD).transpose(3, 1, 0, 2, 4)
    parts = parts.reshape(3, tokens, -1, HD)
    return parts[0], parts[1], parts[2]


def prepare_plain(
    wire, token_ids, masked_pos, masked_target, segment_ids, norms, bias, table, rest
):
    low, f32 = jnp.bfloat16, jnp.float32
    out_w, places_w, qkv_w, up_w = rest
    planes = wire.planes
    rows = 2 * planes
    device = lax.axis_index("head") * rows + lax.axis_index("row")
    chip = lax.axis_index("head") * planes + lax.axis_index("row") // 2
    part, width = table.shape
    share = norms.shape[1]
    lines = token_ids.shape[0] // 128
    at = masked_pos[0][:, None] == jnp.arange(segment_ids.shape[0])[None, :]
    labels = jnp.sum(jnp.where(at, segment_ids[None, :], 0), axis=1)
    target = jnp.where(labels != SEQ - 1, masked_target[0], -1)
    block = jnp.concatenate([token_ids, target])
    block_rows = -(-block.shape[0] // 1024) * 8
    numbers = lax.all_gather(padded(block, block_rows, 128), "row")
    small = jnp.zeros((16, 128), f32).at[:8, :share].set(norms).at[8, : bias.shape[0]].set(bias)
    small_all = wire.small(small.astype(low), 0)
    tokens = token_ids.shape[0] // HEADS
    ids = numbers[:, :lines].reshape(planes, 2, HEADS, tokens)
    ids = ids.transpose(2, 0, 1, 3).reshape(HEADS * planes, 2 * tokens)
    owner = ids // part
    devices = HEADS * rows
    counts = jnp.sum(owner[:, :, None] == jnp.arange(devices), axis=1)
    order = jnp.arange(2 * tokens)
    before = (order[:, None] < order[None, :]).astype(low)
    inside = owner == device
    rank = jnp.dot(inside.astype(low), before, preferred_element_type=f32).astype(jnp.int32)
    hit = jnp.where(inside, rank, -1)[:, None, :] == jnp.arange(ROOM)[None, :, None]
    which = jnp.sum(jnp.where(hit, ids[:, None, :] - device * part + 1, 0), axis=2) - 1
    marks = (which.reshape(-1, 1) == jnp.arange(part)[None, :]).astype(low)
    parcels = jnp.dot(marks, table.astype(low), preferred_element_type=f32).astype(low)
    box = wire.deliver(parcels.reshape(HEADS, planes, ROOM, width))
    own = lax.dynamic_index_in_dim(owner, chip, 0, keepdims=False)
    own_marks = own[:, None] == jnp.arange(devices)
    own_before = contract(before, own_marks.astype(low), 0, 0).astype(jnp.int32)
    own_rank = jnp.sum(jnp.where(own_marks, own_before, 0), axis=1)
    core = lax.axis_index("row") % 2
    own = lax.dynamic_slice_in_dim(own, core * tokens, tokens, 0)
    own_rank = lax.dynamic_slice_in_dim(own_rank, core * tokens, tokens, 0)
    home = (own % 2) * (devices // 2) + own // 2
    misc = jnp.concatenate(
        [out_w, jnp.pad(places_w, ((0, 0), (0, width - SEQ)))], axis=0
    ).astype(low)
    return (
        numbers,
        small_all,
        home[:, None],
        own_rank[:, None],
        which.reshape(-1, 1),
        jnp.max(counts).reshape(1, 1),
        box,
        wire.gather(misc),
        wire.gather(qkv_w.astype(low)),
        wire.gather(up_w.astype(low)),
    )


def forward_plain(parcels, gathered, home, extra, labels, norms, bias, ramp, chosen):
    low = jnp.bfloat16
    misc, wq, wu, wd = gathered
    tokens, width = extra.shape
    share = misc.shape[3] // 2
    rows = parcels.reshape(-1, width)
    looked = jnp.dot(
        (home == jnp.arange(rows.shape[0])[None, :]).astype(low),
        rows,
        preferred_element_type=jnp.float32,
    )
    places = misc[:, :, :, share:, :SEQ].reshape(width, SEQ).T.astype(jnp.float32)
    unit0, scale0 = unit_of(looked + extra + places)
    normed = unit0 * norms[0] + norms[1]
    weight = wq.reshape(4, width, wq.shape[4])
    mixed = jnp.einsum("td,hdj->htj", normed.astype(low), weight, preferred_element_type=jnp.float32)
    mixed = mixed.astype(low)
    query, keys, values = heads_of(mixed)
    attended, summary = attend_fwd(query, keys, values, labels)
    head_ramp = jnp.where(jnp.arange(query.shape[1]) < OLD_HEADS, 1.0, STEP / RAMP)
    heads = (attended * head_ramp[:, None]).astype(low).reshape(tokens, width)
    lse = jnp.pad(summary.T, ((0, 0), (0, 128 - summary.shape[0])))
    weight = misc[:, :, :, :share].reshape(width, width)
    unit1, scale1 = unit_of(normed + contract(heads, weight, 1, 1) + norms[6])
    hidden = unit1 * norms[2] + norms[3]
    u = jnp.einsum(
        "td,pud->ptu", hidden.astype(low), by_plane(wu), preferred_element_type=jnp.float32
    )
    value, rise = gelu_parts(u + bias, ramp)
    active = value.astype(low)
    down = jnp.einsum("ptu,pud->td", active, by_plane(wd), preferred_element_type=jnp.float32)
    unit2, scale2 = unit_of(hidden + down + norms[7])
    final = (unit2 * norms[4] + norms[5]).astype(low)
    marks = (chosen[:, None] == jnp.arange(tokens)[None, :]).astype(low)
    picked = jnp.dot(marks, final, preferred_element_type=jnp.float32).astype(low)
    slope = rise.astype(low)
    return (unit0, scale0, mixed, lse, heads, unit1, scale1, active, slope, unit2, scale2, picked)


def score_block(query, keys, labels):
    scores = jnp.einsum("qhe,khe->hqk", query, keys, preferred_element_type=jnp.float32) * HD ** (
        -0.5
    )
    allowed = labels[:, None] == labels[None, :]
    return jnp.where(allowed[None], scores, -1000000000.0)


def attend_fwd(query, keys, values, labels):
    scores = score_block(query, keys, labels)
    top = jnp.max(scores, axis=-1, keepdims=True)
    weights = jnp.exp(scores - top)
    total = jnp.sum(weights, axis=-1, keepdims=True)
    probs = weights / total
    output = jnp.einsum(
        "hqk,khe->qhe", probs.astype(jnp.bfloat16), values, preferred_element_type=jnp.float32
    )
    return (output, (top + jnp.log(total))[..., 0])


def attend_back(query, keys, values, labels, summary, grad_out):
    scores = score_block(query, keys, labels)
    probs = jnp.exp(scores - summary[..., None])
    grad_values = jnp.einsum(
        "hqk,qhe->khe", probs.astype(jnp.bfloat16), grad_out, preferred_element_type=jnp.float32
    )
    grad_probs = jnp.einsum("qhe,khe->hqk", grad_out, values, preferred_element_type=jnp.float32)
    grad_scores = probs * (grad_probs - jnp.sum(grad_probs * probs, axis=-1, keepdims=True))
    grad_low = grad_scores.astype(jnp.bfloat16)
    grad_query = jnp.einsum(
        "hqk,khe->qhe", grad_low, keys, preferred_element_type=jnp.float32
    ) * HD ** (-0.5)
    grad_keys = jnp.einsum(
        "hqk,qhe->khe", grad_low, query, preferred_element_type=jnp.float32
    ) * HD ** (-0.5)
    return jnp.stack([grad_query, grad_keys, grad_values], axis=2)


def backward_plain(wire, grad_picked, chosen, norms, labels, home, ranks, saved, gathered):
    low, f32 = jnp.bfloat16, jnp.float32
    unit_zero, scale_zero, mixed, lse, heads_low, unit_one, scale_one = saved[:7]
    active, slope, unit_two, scale_two = saved[7:]
    planes = wire.planes
    devices = 8 * planes
    tokens, width = unit_zero.shape
    share, share_inner = width // devices, gathered[2].shape[3]
    out_full = gathered[0][:, :, :, :share].reshape(width, width)
    qkv_full = gathered[1].reshape(HEADS, width, -1)
    up_full, down_full = by_plane(gathered[2]), by_plane(gathered[3])
    normed_low = (unit_zero * norms[0] + norms[1]).astype(low)
    hidden_low = (unit_one * norms[2] + norms[3]).astype(low)
    query, keys, values = heads_of(mixed)
    heads = query.shape[1]
    summary = lse[:, :heads].T
    head_ramp = jnp.where(jnp.arange(heads) < OLD_HEADS, 1.0, STEP / RAMP).astype(f32)
    chosen_marks = chosen[:, None] == jnp.arange(tokens)[None, :]
    grad_final = lax.dot_general(
        chosen_marks.astype(jnp.float32),
        grad_picked,
        (((0,), (0,)), ((), ())),
        precision=lax.Precision.HIGHEST,
    )
    grad_sum, gain_two = unit_back(grad_final, unit_two, scale_two, norms[4])
    grad_sum_low = grad_sum.astype(low)
    grad_down = jnp.einsum("ptu,td->pud", active, grad_sum_low, preferred_element_type=f32)
    grad_upper = jnp.einsum("td,pud->ptu", grad_sum_low, down_full, preferred_element_type=f32)
    grad_upper = grad_upper * slope.astype(f32)
    grad_upper_low = grad_upper.astype(low)
    grad_up = jnp.einsum("ptu,td->pud", grad_upper_low, hidden_low, preferred_element_type=f32)
    grad_hidden = grad_sum + jnp.einsum(
        "ptu,pud->td", grad_upper_low, up_full, preferred_element_type=f32
    )
    grad_res, gain_one = unit_back(grad_hidden, unit_one, scale_one, norms[2])
    grad_res_low = grad_res.astype(low)
    grad_out = contract(grad_res_low, heads_low, 0, 0)
    grad_heads = jnp.dot(grad_res_low, out_full, preferred_element_type=jnp.float32).astype(low)
    grad_attended = (
        grad_heads.reshape(tokens, heads, HD).astype(jnp.float32) * head_ramp[:, None]
    ).astype(low)
    grad_mixed = attend_back(query, keys, values, labels, summary, grad_attended)
    grad_mixed_low = grad_mixed.astype(low).reshape(tokens, HEADS, -1)
    grad_qkv = jnp.einsum(
        "td,thj->hdj", normed_low, grad_mixed_low, preferred_element_type=jnp.float32
    )
    grad_normed = grad_res + jnp.einsum(
        "thj,hdj->td", grad_mixed_low, qkv_full, preferred_element_type=jnp.float32
    )
    grad_start, gain_zero = unit_back(grad_normed, unit_zero, scale_zero, norms[0])
    grad_start_low = grad_start.astype(low)
    grad_norms = jnp.stack(
        [
            jnp.sum(gain_zero, axis=0),
            jnp.sum(grad_normed, axis=0),
            jnp.sum(gain_one, axis=0),
            jnp.sum(grad_hidden, axis=0),
            jnp.sum(gain_two, axis=0),
            jnp.sum(grad_final, axis=0),
            jnp.sum(grad_res, axis=0),
            jnp.sum(grad_sum, axis=0),
        ]
    )
    grad_bias = jnp.sum(grad_upper, axis=1).reshape(planes, HEADS, 2, share_inner)
    seat = jnp.where(ranks < ROOM, home * ROOM + ranks, -1)
    marks = (seat == jnp.arange(devices * ROOM)[None, :]).astype(low)
    back = contract(marks, grad_start_low, 0, 0).astype(low)
    back = wire.hand_back(back.reshape(2, HEADS, planes, ROOM, width))

    def by_head(grad):
        grad = grad.reshape(planes, HEADS, 2, share_inner, width).astype(low)
        return grad.transpose(1, 0, 2, 3, 4)

    rows = jnp.concatenate(
        [grad_start.T, grad_norms.T, jnp.zeros((width, width - tokens - 8), f32)], axis=1
    )
    misc = jnp.concatenate(
        [grad_out.reshape(devices, share, width), rows.reshape(devices, share, width)], axis=1
    )
    bias = grad_bias.transpose(1, 0, 2, 3).reshape(devices, 1, share_inner)
    return (
        back,
        wire.scatter_rows(by_head(grad_up)),
        wire.scatter_rows(by_head(grad_down)),
        wire.scatter_rows(grad_qkv.astype(low).reshape(devices, -1, qkv_full.shape[2])),
        wire.scatter_rows(bias)[0],
        wire.scatter_rows(misc.astype(low)),
        grad_start_low,
    )


def adamw(weight, grad, first, second, decay, rate):
    first = BETA_ONE * first + (1 - BETA_ONE) * grad
    second = BETA_TWO * second + (1 - BETA_TWO) * grad * grad
    moved = first / (1 - BETA_ONE**STEP) / (jnp.sqrt(second / (1 - BETA_TWO**STEP)) + ADAM_EPSILON)
    return (weight - rate * (moved + decay * weight), first, second)


def padded(flat, rows, lanes):
    return jnp.pad(flat, (0, rows * lanes - flat.shape[0])).reshape(rows, lanes)


def on_device(
    token_ids,
    segment_ids,
    masked_pos,
    masked_target,
    embedding,
    position_table,
    qkv_weight,
    out_weight,
    up_weight,
    down_weight,
    norm_params,
    up_bias,
    m_embedding,
    m_position,
    m_qkv,
    m_out,
    m_up,
    m_down,
    m_norm,
    m_bias,
    v_embedding,
    v_position,
    v_qkv,
    v_out,
    v_up,
    v_down,
    v_norm,
    v_bias,
):
    low = jnp.bfloat16
    row_count = lax.axis_size("row")
    devices = HEADS * row_count
    planes = row_count // 2
    wire = Kernels(planes) if planes <= 4 else Plain(planes)
    head = lax.axis_index("head")
    row = lax.axis_index("row")
    core = row % 2
    device = head * row_count + row
    vocab_part, width = embedding.shape
    tokens = token_ids.shape[0] // HEADS
    inner = up_weight.shape[1] * devices

    share = width // devices
    share_inner = inner // devices

    labels_all = segment_ids.reshape(HEADS, tokens)
    slots = masked_pos.shape[1] // HEADS
    numbers, small_all, home, ranks, which, fullest, box, *first = wire.prepare(
        token_ids,
        masked_pos,
        masked_target,
        segment_ids,
        norm_params,
        up_bias,
        embedding,
        (out_weight.T, position_table.T, qkv_weight, up_weight.T),
    )
    rounds = -(-fullest[0, 0] // ROOM)
    lines = token_ids.shape[0] // 128
    numbers = numbers.reshape(row_count, -1)
    targets = numbers[:, lines * 128 : lines * 128 + masked_pos.shape[1]]
    targets = targets.reshape(row_count, HEADS, slots).transpose(1, 0, 2).reshape(-1)
    small_all = jnp.moveaxis(small_all, 0, 2).astype(jnp.float32)
    norms = small_all[..., :8, :share].transpose(3, 0, 1, 2, 4).reshape(8, width)
    bias = small_all[..., 8, :share_inner].transpose(1, 0, 2, 3).reshape(planes, 1, -1)
    ramp = jnp.where(jnp.arange(inner) < OLD_FF, 1.0, STEP / RAMP).astype(jnp.float32)
    ramp = ramp.reshape(HEADS, planes, -1).transpose(1, 0, 2).reshape(planes, 1, -1)
    table = embedding.astype(low)

    def which_in(turn):
        ids = numbers[:, : lines * 128].reshape(planes, 2, HEADS, tokens)
        ids = ids.transpose(2, 0, 1, 3).reshape(HEADS * planes, 2 * tokens) - device * vocab_part
        inside = (ids >= 0) & (ids < vocab_part)
        order = jnp.arange(2 * tokens)
        before = (order[:, None] < order[None, :]).astype(low)
        rank = jnp.dot(inside.astype(low), before, preferred_element_type=jnp.float32)
        rank = jnp.where(inside, rank.astype(jnp.int32), -1)
        spot = jnp.arange(ROOM) + turn * ROOM
        hit = rank[:, None, :] == spot[None, :, None]
        return (jnp.sum(jnp.where(hit, ids[:, None, :] + 1, 0), axis=2) - 1).reshape(-1, 1)

    def parcel_marks(which):
        return (which == jnp.arange(vocab_part)[None, :]).astype(low)

    def token_marks(turn):
        seat = ranks - turn * ROOM
        seat = jnp.where((seat >= 0) & (seat < ROOM), home * ROOM + seat, -1)
        return (seat == jnp.arange(devices * ROOM)[None, :]).astype(low)

    def again(state):
        turn, so_far = state
        parcels = jnp.dot(parcel_marks(which_in(turn)), table, preferred_element_type=jnp.float32)
        more = wire.deliver(parcels.astype(low).reshape(HEADS, planes, ROOM, width))
        more = jnp.dot(
            token_marks(turn),
            more.reshape(devices * ROOM, width),
            preferred_element_type=jnp.float32,
        )
        return turn + 1, so_far + more

    _, extra = lax.while_loop(
        lambda state: state[0] < rounds,
        again,
        (jnp.int32(1), jnp.zeros((tokens, width), jnp.float32)),
    )

    labels = lax.dynamic_index_in_dim(labels_all, head, 0, keepdims=False)
    chosen = lax.dynamic_slice_in_dim(masked_pos[0], head * slots, slots, 0) - head * tokens
    second, saved = wire.forward(
        box,
        first,
        [down_weight.astype(low)],
        home,
        ranks,
        extra,
        labels,
        norms,
        bias,
        ramp,
        chosen,
    )
    gathered = [*first, *second]
    *saved, picked = saved

    all_rows = wire.rows(picked).reshape(devices * slots, width)
    valid = (targets >= 0).astype(jnp.float32)
    logits = contract(all_rows, table, 1, 1)
    hits = jnp.arange(vocab_part)[None, :] == (targets - device * vocab_part)[:, None]
    top = jnp.max(logits, axis=1)
    part = top + jnp.log(jnp.sum(jnp.exp(logits - top[:, None]), axis=1))
    parts = wire.small(part.reshape(-1, 128), 5).reshape(devices, -1)
    peak = jnp.max(parts, axis=0)
    log_total = peak + jnp.log(jnp.sum(jnp.exp(parts - peak), axis=0))
    target_part = jnp.sum(jnp.where(hits, logits, 0.0))
    log_own = lax.dynamic_slice_in_dim(log_total * valid, device * slots, slots, 0)
    valid_own = lax.dynamic_slice_in_dim(valid, device * slots, slots, 0)
    loss_own = jnp.sum(log_own) - target_part
    count_own = jnp.sum(valid_own)
    grad_logits = (
        valid[:, None] * (jnp.exp(logits - log_total[:, None]) - hits.astype(jnp.float32))
    ).astype(low)
    grad_table = contract(grad_logits, all_rows, 0, 0)
    grad_rows = jnp.dot(grad_logits, table, preferred_element_type=jnp.float32).astype(low)
    grad_picked = wire.scatter_rows(grad_rows.reshape(HEADS, planes, 2, slots, width))

    parcels, of_up, of_down, of_qkv, of_bias, of_misc, *of_start = wire.backward(
        grad_picked, chosen, norms, labels, home, ranks, saved, gathered
    )

    def unpacked(parcels, which):
        return contract(parcel_marks(which), parcels.reshape(-1, width), 0, 0)

    grad_table = grad_table + unpacked(parcels, which)

    def again_back(state):
        turn, so_far = state
        back = contract(token_marks(turn), of_start[0], 0, 0).astype(low)
        back = wire.hand_back(back.reshape(2, HEADS, planes, ROOM, width))
        return turn + 1, so_far + unpacked(back, which_in(turn))

    _, grad_table = lax.while_loop(
        lambda state: state[0] < rounds, again_back, (jnp.int32(1), grad_table)
    )
    grads = (
        grad_table,
        of_misc[share : 2 * share, :SEQ].T,
        of_qkv,
        of_misc[:share].T,
        of_up.T,
        of_down,
        of_misc[share : 2 * share, SEQ : SEQ + 8].T,
        of_bias,
    )
    squares = sum((jnp.sum(g * g) for g in grads))
    scalars = padded(jnp.stack([squares, loss_own, count_own]), 8, 128)
    scalars = jnp.sum(wire.small(scalars, 6).reshape(devices, 8, 128)[:, 0, :3], axis=0)
    squares, loss_sum, live_count = scalars[0], scalars[1], scalars[2]
    grad_norm = jnp.sqrt(squares) / live_count
    factor = jnp.minimum(1.0, CLIP / grad_norm) / live_count
    weights = (
        embedding,
        position_table,
        qkv_weight,
        out_weight,
        up_weight,
        down_weight,
        norm_params,
        up_bias,
    )
    firsts = (m_embedding, m_position, m_qkv, m_out, m_up, m_down, m_norm, m_bias)
    seconds = (v_embedding, v_position, v_qkv, v_out, v_up, v_down, v_norm, v_bias)
    decays = (DECAY,) * 6 + (0.0, 0.0)
    rates = (LEARN_RATE,) * 6 + (GAIN_RATE,) * 2
    results = [
        adamw(w, g * factor, m, v, d, r)
        for w, g, m, v, d, r in zip(weights, grads, firsts, seconds, decays, rates)
    ]
    return (
        *(r[0] for r in results),
        *(r[1] for r in results),
        *(r[2] for r in results),
        loss_sum,
        live_count,
        grad_norm,
    )


def solution(mesh):
    vocab = P(("head", "row"), None)
    columns = P(None, ("head", "row"))
    flat = P(("head", "row"))
    weights = (vocab, columns, P("row", "head"), columns, columns, vocab, columns, flat)
    data = (P("row"), P("row"), P("row", None), P("row", None))
    return jax.shard_map(
        on_device,
        mesh=mesh,
        in_specs=(*data, *weights, *weights, *weights),
        out_specs=(*weights, *weights, *weights, P(), P(), P()),
        check_vma=False,
    )
```

```python
import functools

import jax
import jax.numpy as jnp
from jax import lax
from jax.experimental import pallas as pl
from jax.experimental.pallas import tpu as pltpu
from jax.sharding import PartitionSpec as P

HD = 64
SEQ = 512
STEP = 5
RAMP = 10
OLD_HEADS = 8
OLD_FF = 2048


EPSILON = 1e-05
LEARN_RATE = 0.03
GAIN_RATE = 0.5
BETA_ONE = 0.9
BETA_TWO = 0.999
ADAM_EPSILON = 1e-08
DECAY = 0.01
CLIP = 0.02

ROOM = 64
HEADS = 4
MESH = pl.DeviceIdType.MESH
ANY = pl.BlockSpec(memory_space=pl.ANY)
VMEM = pl.BlockSpec(memory_space=pltpu.VMEM)


def place():
    h = lax.axis_index("head")
    r = lax.axis_index("row")
    return h, lax.div(r, 2), lax.rem(r, 2)


def across(h, q):
    if q == 0:
        return h
    if q == 1:
        return h + 1 - 2 * lax.rem(h, 2)
    if q == 2:
        return lax.rem(h + 2, 4)
    return 3 - h


class Wires:
    def __init__(self, send, recv):
        self.send, self.recv, self.used, self.made = send, recv, 0, []

    def copy(self, src, dst, to):
        i = self.used
        self.used += 1
        one = pltpu.make_async_remote_copy(
            src_ref=src,
            dst_ref=dst,
            send_sem=self.send.at[i],
            recv_sem=self.recv.at[i],
            device_id=to,
            device_id_type=MESH,
        )
        one.start()
        self.made.append(one)
        return one

    def sent(self):
        for one in self.made:
            one.wait_send()


def greet(peers):
    barrier = pltpu.get_barrier_semaphore()
    for to in peers:
        pl.semaphore_signal(barrier, inc=1, device_id=to, device_id_type=MESH)
    pl.semaphore_wait(barrier, len(peers))


def near(planes):
    h, z, c = place()
    peers = [(h, 2 * z + 1 - c), (across(h, 1), 2 * z + c), (across(h, 2), 2 * z + c)]
    peers += [(h, 2 * lax.rem(z + s, planes) + c) for s in range(1, planes)]
    return peers


def every_chip(planes):
    h, z, c = place()
    peers = [(h, 2 * z + 1 - c)]
    for q in range(4):
        for s in range(planes):
            if q or s:
                peers.append((across(h, q), 2 * lax.rem(z + s, planes) + c))
    return peers


def split(rows):
    first = -(-rows // 32) * 16
    return pl.ds(0, first), pl.ds(first, rows - first)


def spread_start(wires, local, planes, parcels, out):
    h, z, c = place()
    sib = (h, 2 * z + 1 - c)
    got = {}
    for q in range(4):
        for s in range(planes):
            if q or s:
                th, tz = across(h, q), lax.rem(z + s, planes)
                got[q, s] = wires.copy(parcels(th, tz), out.at[c, h, z], (th, 2 * tz + c))
    mine = pltpu.make_async_copy(parcels(h, z), out.at[c, h, z], local)
    mine.start()
    passed = [wires.copy(parcels(h, z), out.at[c, h, z], sib)]
    return got, mine, passed


def spread_finish(wires, planes, out, state):
    h, z, c = place()
    sib = (h, 2 * z + 1 - c)
    got, mine, passed = state
    for (q, s), one in got.items():
        one.wait_recv()
        there = out.at[c, across(h, q), lax.rem(z - s + planes, planes)]
        passed.append(wires.copy(there, there, sib))
    for one in passed:
        one.wait_recv()
    mine.wait()


def deliver_kernel(planes, parcels, out, send, recv, local):
    greet(every_chip(planes))
    wires = Wires(send, recv)
    state = spread_start(wires, local, planes, lambda h, z: parcels.at[h, z], out)
    spread_finish(wires, planes, out, state)
    wires.sent()


def add_rows(target, others, rows):
    @pl.loop(0, rows // 16)
    def _(i):
        at = pl.ds(pl.multiple_of(i * 16, 16), 16)
        total = target[at, :].astype(jnp.float32)
        for other in others:
            total = total + other[at, :].astype(jnp.float32)
        target[at, :] = total.astype(target.dtype)


class Scatter:
    def __init__(self, wires, planes, groups):
        self.wires, self.planes, self.groups = wires, planes, groups
        h, z, c = place()
        self.h, self.z, self.c = h, z, c
        row = 2 * z + c
        self.sib = (h, 2 * z + 1 - c)
        self.hx, self.hy, self.hd = across(h, 1), across(h, 2), across(h, 3)
        self.xn, self.yn = (self.hx, row), (self.hy, row)
        self.to = [lax.rem(z + 1 + s, planes) for s in range(planes)]
        self.got = {}

    def post(self, k, s):
        grads, out, sibs, px, pz = self.groups[k]
        t = self.to[s]
        for q in (3, 1, 2, 0):
            th = across(self.h, q)
            self.got[k, s, q] = self.wires.copy(
                grads.at[th, t, 1 - self.c], sibs.at[th, t], self.sib
            )

    def pair(self, k, s):
        grads, out, sibs, px, pz = self.groups[k]
        t, rows = self.to[s], sibs.shape[2]
        a, b = split(rows)
        copy, got = self.wires.copy, self.got
        for q in (3, 1, 2, 0):
            got[k, s, q].wait_recv()
            th = across(self.h, q)
            own = grads.at[th, t, self.c]
            add_rows(own, [sibs.at[th, t]], rows)
            if q == 3:
                got[k, s, "xd"] = copy(own.at[a], px.at[t, 0].at[a], self.xn)
                got[k, s, "yd"] = copy(own.at[b], px.at[t, 0].at[b], self.yn)
            if q == 1:
                got[k, s, "x"] = copy(own.at[a], px.at[t, 1].at[a], self.xn)
            if q == 2:
                got[k, s, "y"] = copy(own.at[b], px.at[t, 1].at[b], self.yn)

    def plane(self, k, s):
        grads, out, sibs, px, pz = self.groups[k]
        t, rows = self.to[s], sibs.shape[2]
        a, b = split(rows)
        copy, got = self.wires.copy, self.got
        got[k, s, "xd"].wait_recv()
        own = grads.at[self.hy, t, self.c].at[a]
        add_rows(own, [px.at[t, 0].at[a]], a.size)
        got[k, s, "y2"] = copy(own, px.at[t, 2].at[a], self.yn)
        got[k, s, "yd"].wait_recv()
        own = grads.at[self.hx, t, self.c].at[b]
        add_rows(own, [px.at[t, 0].at[b]], b.size)
        got[k, s, "x2"] = copy(own, px.at[t, 2].at[b], self.xn)

    def line(self, k, s):
        grads, out, sibs, px, pz = self.groups[k]
        t = self.to[s]
        for part in ("x", "y2", "y", "x2"):
            self.got[k, s, part].wait_recv()
        own = grads.at[self.h, t, self.c]
        add_rows(own, [px.at[t, 1], px.at[t, 2]], sibs.shape[2])
        if s < self.planes - 1:
            self.got[k, s, "z"] = self.wires.copy(own, pz.at[s], (self.h, 2 * t + self.c))

    def total(self, k):
        grads, out, sibs, px, pz = self.groups[k]
        h, z, c = self.h, self.z, self.c
        for s in range(self.planes - 1):
            self.got[k, s, "z"].wait_recv()

        @pl.loop(0, out.shape[0] // 16)
        def _(i):
            at = pl.ds(pl.multiple_of(i * 16, 16), 16)
            value = grads[h, z, c, at, :].astype(jnp.float32)
            for s in range(self.planes - 1):
                value = value + pz[s, at, :].astype(jnp.float32)
            out[at, :] = value


def give_steps(wires, planes, parcels, out, other, keep):
    h, z, c = place()
    sib = (h, 2 * z + 1 - c)
    passed = wires.copy(parcels.at[1 - c], other, sib)
    passed.wait_recv()
    given = []
    for q in (3, 1, 2, 0):
        for s in range(planes - 1, -1, -1):
            th, tz = across(h, q), lax.rem(z + s, planes)
            mine = parcels.at[c, th, tz]
            add_rows(mine, [other.at[th, tz]], other.shape[2])
            if q or s:
                given.append(wires.copy(mine, out.at[h, z], (th, 2 * tz + c)))
    stay = pltpu.make_async_copy(parcels.at[c, h, z], out.at[h, z], keep)
    stay.start()
    return given, stay


def return_kernel(planes, parcels, out, other, send, recv, keep):
    greet(every_chip(planes))
    wires = Wires(send, recv)
    given, stay = give_steps(wires, planes, parcels, out, other, keep)
    for one in given:
        one.wait_recv()
    stay.wait()
    wires.sent()


def guarded(ok, act):
    if ok is None:
        act()
    else:
        pl.when(ok)(act)


class Lines:
    def __init__(self, send, recv):
        self.send, self.recv, self.used, self.made = send, recv, 0, []

    def make(self, src, dst, to, ok):
        i = self.used
        self.used += 1
        one = pltpu.make_async_remote_copy(
            src_ref=src,
            dst_ref=dst,
            send_sem=self.send.at[i],
            recv_sem=self.recv.at[i],
            device_id=to,
            device_id_type=MESH,
        )
        self.made.append((one, ok))
        return one

    def sent(self):
        for one, ok in self.made:
            guarded(ok, one.wait_send)


def line_steps(planes):
    return [0] + [d * s for s in range(1, planes) for d in (1, -1)]


class Gather:
    def __init__(self, wires, local, planes, pairs):
        self.wires, self.planes, self.pairs = wires, planes, pairs
        h, z, c = place()
        self.h, self.z, self.c = h, z, c
        row = 2 * z + c
        self.sib = (h, 2 * z + 1 - c)
        self.hx, self.hy, self.hd = across(h, 1), across(h, 2), across(h, 3)
        self.xn, self.yn = (self.hx, row), (self.hy, row)
        self.at, self.have, self.on = {0: z}, {0: None}, {}
        for s in line_steps(planes)[1:]:
            t = z - s
            self.have[s] = (t >= 0) & (t < planes)
            self.at[s] = jnp.clip(t, 0, planes - 1)
        for s in range(planes - 1):
            for d in (1, -1):
                u = z + d
                ok = (u >= 0) & (u < planes)
                self.on[d, s] = (ok & self.have[d * s]) if s else ok
        self.here = []
        for k, (x, out) in enumerate(pairs):
            one = pltpu.make_async_copy(x, out.at[h, z, c], local.at[k])
            one.start()
            self.here.append(one)
        self.line, self.copies = {}, {}

    def onward(self, k, d, s):
        x, out = self.pairs[k]
        t = self.at[d * s]
        ref = x if s == 0 else out.at[self.h, t, self.c]
        u = jnp.clip(self.z + d, 0, self.planes - 1)
        ok = self.on[d, s]
        one = self.wires.make(ref, out.at[self.h, t, self.c], (self.h, 2 * u + self.c), ok)
        self.line[k, d, s] = one
        guarded(ok, one.start)

    def launch(self, k, s):
        x, out = self.pairs[k]
        t, ok = self.at[s], self.have[s]
        here = out.at[self.h, t, self.c]
        ref = x if s == 0 else here
        if s == 0:
            self.onward(k, 1, 0)
            self.onward(k, -1, 0)
        else:
            d, a = (1, s) if s > 0 else (-1, -s)
            guarded(ok, self.line[k, d, a - 1].wait_recv)
            if a < self.planes - 1:
                self.onward(k, d, a)
        make = self.wires.make
        ones = [make(ref, here, to, ok) for to in (self.xn, self.yn, self.sib)]
        self.copies[k, s, "x"], self.copies[k, s, "y"], self.copies[k, s, "s"] = ones

        def act():
            for one in ones:
                one.start()

        guarded(ok, act)

    def relay(self, k, s):
        out = self.pairs[k][1]
        t, ok = self.at[s], self.have[s]
        first, second = split(out.shape[3])
        make, got = self.wires.make, self.copies
        gx, gy = out.at[self.hx, t, self.c], out.at[self.hy, t, self.c]
        got[k, s, "yd"] = make(gx.at[second], gx.at[second], self.yn, ok)
        got[k, s, "sx"] = make(gx, gx, self.sib, ok)
        got[k, s, "xd"] = make(gy.at[first], gy.at[first], self.xn, ok)
        got[k, s, "sy"] = make(gy, gy, self.sib, ok)

        def act():
            got[k, s, "x"].wait_recv()
            got[k, s, "yd"].start()
            got[k, s, "sx"].start()
            got[k, s, "y"].wait_recv()
            got[k, s, "xd"].start()
            got[k, s, "sy"].start()

        guarded(ok, act)

    def finish(self, k, s):
        out = self.pairs[k][1]
        t, ok = self.at[s], self.have[s]
        got = self.copies
        gd = out.at[self.hd, t, self.c]
        got[k, s, "sd"] = self.wires.make(gd, gd, self.sib, ok)

        def act():
            got[k, s, "yd"].wait_recv()
            got[k, s, "xd"].wait_recv()
            got[k, s, "sd"].start()

        guarded(ok, act)

    def done(self, k, s):
        if s == 0:
            self.here[k].wait()

        def act():
            for part in ("s", "sx", "sy", "sd"):
                self.copies[k, s, part].wait_recv()

        guarded(self.have[s], act)


def line_wires(planes, count):
    return count * (2 * planes - 1) * 9


def iota(shape, dim):
    return lax.broadcasted_iota(jnp.int32, shape, dim)


def ones_where(marks):
    return marks.astype(jnp.float32).astype(jnp.bfloat16)


def column(lines):
    turned = lines.T
    return jnp.concatenate([turned[:, i : i + 1] for i in range(lines.shape[0])], axis=0)


def prepare_kernel(planes, room, *refs):
    (tokens, picks, goals, segments, norms_in, bias_in, table) = refs[:7]
    (out_w, places_w, qkv_w, up_w) = refs[7:11]
    (numbers, small_all, home, rank_out, which_out, rounds, box) = refs[11:18]
    (misc_all, wq_all, wu_all) = refs[18:21]
    (block, small, misc, wq, wu, parcels, send, recv, send2, recv2, local) = refs[21:]
    low, f32 = jnp.bfloat16, jnp.float32
    h, z, c = place()
    row = 2 * z + c
    rows = 2 * planes
    device = h * rows + row
    part = table.shape[0]
    lines = tokens.shape[0]
    each = lines // 4
    peers = [(s, e) for s in range(planes) for e in range(2) if s or e]
    peers = [(h, 2 * lax.rem(z + s, planes) + lax.rem(c + e, 2)) for s, e in peers]
    chips = [
        (across(h, q), 2 * lax.rem(z + s, planes) + c) for q in (1, 2, 3) for s in range(planes)
    ]
    padding = ones_where(segments[...] == SEQ - 1)
    at = iota((128, picks.shape[1]), 0) == lax.rem(picks[...], 128)
    padded_at = mul(padding, ones_where(at))
    line = iota((lines, picks.shape[1]), 0) == lax.div(picks[...], 128)
    padded_at = jnp.sum(jnp.where(line, padded_at, 0.0), axis=0, keepdims=True)
    goal = jnp.where(padded_at == 0.0, goals[...], -1)
    block[...] = jnp.zeros_like(block)
    block[0:lines, :] = tokens[...]
    for i in range(goal.shape[1] // 128):
        block[lines + i : lines + i + 1, :] = goal[:, 128 * i : 128 * (i + 1)]
    share, width = norms_in.shape[1], table.shape[1]
    small[...] = jnp.zeros_like(small)
    small[0:8, 0:share] = norms_in[...].astype(low).astype(f32)
    small[8:9, 0 : bias_in.shape[1]] = bias_in[...].astype(low).astype(f32)
    greet(peers + chips)
    posts = Wires(send2, recv2)
    mine = pltpu.make_async_copy(block, numbers.at[row], local.at[0])
    mine.start()
    ids = [posts.copy(block, numbers.at[row], to) for to in peers]
    spread = spread_start(posts, local.at[1], planes, lambda th, tz: small, small_all)
    wq[...] = qkv_w[...].astype(low)
    wu[...] = up_w[...].astype(low)
    places_row = jnp.concatenate([places_w[...], jnp.zeros((share, width - SEQ), f32)], axis=1)
    misc[...] = jnp.concatenate([out_w[...], places_row], axis=0).astype(low)
    lines_of = Lines(send, recv)
    pairs = [(misc, misc_all), (wq, wq_all), (wu, wu_all)]
    gather = Gather(lines_of, local.at[pl.ds(2, 3)], planes, pairs)
    for k in range(3):
        gather.launch(k, 0)
    for one in ids:
        one.wait_recv()
    mine.wait()

    everyone = numbers[...][:, :lines, :].reshape(rows * lines, 128)
    total = rows * lines
    by_row, by_col = iota((total, total), 0), iota((total, total), 1)

    def parts(n):
        return n // (2 * lines), (n // lines) % 2, (n // each) % 4, n % each

    def parts_of(n):
        plane = lax.div(n, 2 * lines)
        core = lax.rem(lax.div(n, lines), 2)
        head = lax.rem(lax.div(n, each), 4)
        return plane, core, head, lax.rem(n, each)

    pr, cr, hr, ir = parts_of(by_row)
    pc, cc, hc, ic = parts_of(by_col)
    same = (pr == pc) & (hr == hc)
    earlier = same & (cc * each + ic < cr * each + ir)
    earlier = ones_where(earlier)
    before = ones_where(iota((128, 128), 0) < iota((128, 128), 1))
    ones = jnp.ones((128, 128), low)

    near_id = everyone - device * part
    inside = (near_id >= 0) & (near_id < part)
    marks = ones_where(inside)
    in_row = mul(marks, ones).astype(low)
    rank = (mul(marks, before) + mul(earlier, in_row)).astype(jnp.int32)
    rank = jnp.where(inside, rank, -1)

    counts = jnp.zeros((total, 128), f32)
    for d in range(4 * rows):
        owned = ones_where((everyone >= d * part) & (everyone < (d + 1) * part))
        counts = counts + mul(owned, ones_where(iota((128, 128), 1) == d))
    fullest = jnp.max(mul(ones_where(same), counts.astype(low)))
    rounds[...] = jnp.full(rounds.shape, fullest.astype(jnp.int32))

    slot = iota((room, 128), 0)
    low_table = table[...].astype(low)
    vocab = iota((room, part), 1)
    for th in range(4):
        for tz in range(planes):
            found = jnp.zeros((room, 128), jnp.int32)
            for core in range(2):
                for i in range(each):
                    n = (tz * 2 + core) * lines + th * each + i
                    hit = rank[n : n + 1, :] == slot
                    found = found + jnp.where(hit, near_id[n : n + 1, :] + 1, 0)
            which = jnp.sum(found.astype(f32), axis=1, keepdims=True).astype(jnp.int32) - 1
            at = (th * planes + tz) * room
            which_out[at : at + room, :] = which
            parcels[th, tz] = mul(ones_where(which == vocab), low_table).astype(low)
    post = spread_start(posts, local.at[5], planes, lambda th, tz: parcels.at[th, tz], box)

    for k in range(3):
        gather.launch(k, 1)
        gather.launch(k, -1)
    for k in range(3):
        gather.relay(k, 0)

    ids_here = [
        numbers[2 * z + core, pl.ds(each * h, each), :].astype(f32) for core in range(2)
    ]
    own = column(numbers[row, pl.ds(each * h, each), :].astype(f32))
    count = each * 128

    def owners(values):
        owner = jnp.zeros(values.shape, f32)
        for d in range(1, 4 * rows):
            owner = owner + jnp.where(values >= float(d * part), 1.0, 0.0)
        return owner

    own_owner = owners(own)
    own_spot = iota((count, 128), 0) + c * count
    ahead = jnp.zeros((count, 128), f32)
    for core in range(2):
        them = owners(ids_here[core])
        for i in range(each):
            spot = core * count + 128 * i + iota((count, 128), 1)
            hit = (own_owner == them[i : i + 1, :]) & (spot < own_spot)
            ahead = ahead + jnp.where(hit, 1.0, 0.0)
    rank_out[...] = jnp.sum(ahead, axis=1, keepdims=True).astype(jnp.int32)
    owner = own_owner.astype(jnp.int32)
    home[...] = lax.rem(owner, 2) * (2 * rows) + lax.div(owner, 2)

    order = [(k, s) for k in range(3) for s in (1, -1)]
    order += [(k, s) for a in range(2, planes) for k in range(3) for s in (a, -a)]
    for k in range(3):
        gather.finish(k, 0)
    lag = 3
    for i in range(len(order) + 2 * lag):
        if 6 <= i < len(order):
            gather.launch(*order[i])
        if lag <= i < len(order) + lag:
            gather.relay(*order[i - lag])
        if i >= 2 * lag:
            gather.finish(*order[i - 2 * lag])
    spread_finish(posts, planes, small_all, spread)
    spread_finish(posts, planes, box, post)
    for k in range(3):
        for s in line_steps(planes):
            gather.done(k, s)
    posts.sent()
    lines_of.sent()


def mul(left, right, left_dim=1, right_dim=0):
    return lax.dot_general(
        left, right, (((left_dim,), (right_dim,)), ((), ())), preferred_element_type=jnp.float32
    )


def unit_of(values):
    center = values - jnp.mean(values, axis=-1, keepdims=True)
    scale = lax.rsqrt(jnp.mean(center * center, axis=-1, keepdims=True) + EPSILON)
    return center * scale, scale


ERF_TOP = (
    -2.72614225801306e-10,
    2.77068142495902e-08,
    -2.10102402082508e-06,
    -5.69250639462346e-05,
    -7.34990630326855e-04,
    -2.95459980854025e-03,
    -1.60960333262415e-02,
)
ERF_LOW = (
    -1.45660718464996e-05,
    -2.13374055278905e-04,
    -1.68282697438203e-03,
    -7.37332916720468e-03,
    -1.42647390514189e-02,
)


def erf(x):
    x = jnp.clip(x, -4.0, 4.0)
    square = x * x
    top = jnp.full_like(x, ERF_TOP[0])
    for c in ERF_TOP[1:]:
        top = top * square + c
    bottom = jnp.full_like(x, ERF_LOW[0])
    for c in ERF_LOW[1:]:
        bottom = bottom * square + c
    return x * top / bottom


def gelu_parts(u, ramp):
    cdf = 0.5 + 0.5 * erf(u * (0.5**0.5))
    density = jnp.exp(-0.5 * u * u) * 0.3989422804014327
    return u * cdf * ramp, (cdf + u * density) * ramp


def head_slice(ref, head, part):
    group, i = head // 3, head % 3
    start = (3 * i + part) * HD
    return ref[group, :, start : start + HD]


def masked_scores(q, k, labels_col, labels_row):
    s = mul(q, k, 1, 1) * HD**-0.5
    return jnp.where(labels_col == labels_row, s, -1000000000.0)


def forward_kernel(planes, room, *refs):
    (box, misc_all, wq_all, wu_all, wd, home, ranks, extra) = refs[:8]
    (lab_col, lab_row, norms, bias, ramp, chosen) = refs[8:14]
    wd_all = refs[14]
    (unit0, scale0, mixed, lse, heads, unit1, scale1, active, slope, unit2, scale2, picked) = refs[
        15:27
    ]
    (misc_v, wq_v, wu_v, wd_v, hidden, total, lab_one) = refs[27:34]
    send, recv, local, loads = refs[34:]
    low = jnp.bfloat16
    h, z, c = place()
    greet(near(planes))
    lines = Lines(send, recv)
    pairs = [(wd, wd_all)]
    gather = Gather(lines, local, planes, pairs)
    tokens, width = unit0.shape

    def load(i, src, dst):
        one = pltpu.make_async_copy(src, dst, loads.at[i])
        one.start()
        return one

    ready_misc = load(0, misc_all, misc_v)
    ready_q = load(1, wq_all, wq_v)

    def start_norm():
        lab_one[...] = column(lab_col[...].astype(jnp.float32)).astype(jnp.int32)
        ready_misc.wait()
        spots = iota((tokens, box.shape[3] * 8 * planes), 1)
        seat = jnp.where(ranks[...] < room, home[...] * room + ranks[...], -1)
        rows = box[...].reshape(-1, width)
        looked = mul(ones_where(seat == spots), rows) + extra[...]
        pieces = misc_v[...].astype(jnp.float32)
        share = misc_v.shape[3] // 2
        places = pieces[:, :, :, share:, :SEQ].reshape(width, SEQ).T
        unit, scale = unit_of(looked + places)
        unit0[...] = unit
        scale0[...] = scale
        hidden[...] = unit * norms[0:1, :] + norms[1:2, :]

    def project(group):
        weight = wq_v[group].reshape(width, wq_v.shape[4])
        mixed[group] = mul(hidden[...].astype(low), weight).astype(low)

    def attend(pair):
        outs = []
        for head in (2 * pair, 2 * pair + 1):
            q, k, v = (head_slice(mixed, head, j) for j in range(3))
            s = masked_scores(q, k, lab_one[...], lab_row[...])
            top = jnp.max(s, axis=1, keepdims=True)
            e = jnp.exp(s - top)
            sums = jnp.sum(e, axis=1, keepdims=True)
            lse[:, head : head + 1] = top + jnp.log(sums)
            p = (e / sums).astype(low)
            scale = 1.0 if head < OLD_HEADS else STEP / RAMP
            outs.append((mul(p, v) * scale).astype(low))
        heads[:, 2 * HD * pair : 2 * HD * (pair + 1)] = jnp.concatenate(outs, axis=1)

    def middle():
        share = misc_v.shape[3] // 2
        weight = misc_v[...].astype(jnp.float32)[:, :, :, :share].reshape(width, width).astype(low)
        value = hidden[...] + mul(heads[...], weight, 1, 1) + norms[6:7, :]
        unit, scale = unit_of(value)
        unit1[...] = unit
        scale1[...] = scale
        hidden[...] = unit * norms[2:3, :] + norms[3:4, :]
        total[...] = hidden[...] + norms[7:8, :]

    def chunk(t):
        one = load(2, wu_all.at[:, t], wu_v.at[0])
        two = load(3, wd_all.at[:, t], wd_v.at[0])
        one.wait()
        units = wu_v.shape[1] * 2 * wu_v.shape[3]
        u = mul(hidden[...].astype(low), wu_v[0].reshape(units, width), 1, 1) + bias[t]
        value, rise = gelu_parts(u, ramp[t])
        value = value.astype(low)
        active[t] = value
        slope[t] = rise.astype(low)
        two.wait()
        total[...] += mul(value, wd_v[0].reshape(units, width))

    def last():
        unit, scale = unit_of(total[...])
        unit2[...] = unit
        scale2[...] = scale
        final = (unit * norms[4:5, :] + norms[5:6, :]).astype(low)
        marks = ones_where(iota((tokens, chosen.shape[1]), 0) == chosen[...])
        picked[...] = mul(marks, final, 0, 0).astype(low)

    planes_near = near_first(planes, z)
    lag = 3
    whole = [(0, s) for s in line_steps(planes)]
    events = []
    for i in range(len(whole) + 2 * lag):
        if i < len(whole):
            events.append((gather.launch, *whole[i]))
        if lag <= i < len(whole) + lag:
            events.append((gather.relay, *whole[i - lag]))
        if i >= 2 * lag:
            events.append((gather.finish, *whole[i - 2 * lag]))

    def settle(a):
        for s in (a, -a) if a else (0,):
            gather.done(0, s)

    def take(upto):
        while events and (upto is None or upto > 0):
            event, k, s = events.pop(0)
            event(k, s)
            if upto is not None:
                upto -= 1

    take(3)
    work = [start_norm, lambda: (ready_q.wait(), project(0))]
    work += [functools.partial(project, g) for g in range(1, 4)]
    work += [functools.partial(attend, p) for p in range(6)]
    work += [middle]
    stop = len(events)
    count = len(work)
    shares = [stop * (i + 1) // count - stop * i // count for i in range(count)]
    for act, some in zip(work, shares):
        act()
        take(some)
    for a in range(planes):
        settle(a)
        chunk(planes_near[a])
    last()
    lines.sent()


def unit_back(grad, unit, scale, gain):
    inner = grad * gain
    back = scale * (
        inner
        - jnp.mean(inner, axis=-1, keepdims=True)
        - unit * jnp.mean(inner * unit, axis=-1, keepdims=True)
    )
    return (back, grad * unit)


def backward_kernel(planes, room, *refs):
    (picked, chosen, norms, lab_lines, lab_row, home, ranks) = refs[:7]
    (scale0, scale1, scale2, lse) = refs[7:11]
    (unit0, unit1, unit2, mixed, heads, active, slope) = refs[11:18]
    (misc_all, wq_all, wu_all, wd_all) = refs[18:22]
    (back, up_sum, down_sum, q_sum, misc_sum, grad_low) = refs[22:28]
    (ups, downs, qs, miscs) = (refs[28 + 4 * k : 32 + 4 * k] for k in range(4))
    (parcels, other, unit_v, grad, extra, act_low, heads_v) = refs[44:51]
    (wu_v, wd_v, active_v, slope_v, wq_v, mixed_v, norm_sums, lab_one) = refs[51:59]
    send, recv, local = refs[59:]
    low, f32 = jnp.bfloat16, jnp.float32
    h, z, c = place()
    tokens, width = unit_v.shape
    units = active_v.shape[1]
    share = wu_v.shape[2]
    lanes = mixed_v.shape[1]
    up_g, down_g, q_g, misc_g = ups[0], downs[0], qs[0], miscs[0]
    loads = {}

    def load(i, src, dst):
        one = pltpu.make_async_copy(src, dst, local.at[i])
        one.start()
        loads[i] = one

    def ready(*which):
        for i in which:
            loads.pop(i).wait()

    greet(every_chip(planes))
    wires = Wires(send, recv)
    sums = [up_sum, down_sum, q_sum, misc_sum]
    groups = [(g[0], out, *g[1:]) for g, out in zip((ups, downs, qs, miscs), sums)]
    scatter = Scatter(wires, planes, groups)
    order = scatter.to
    load(0, unit2, unit_v)
    load(1, wd_all.at[:, order[0]], wd_v)
    load(2, active.at[order[0]], active_v)
    load(3, slope.at[order[0]], slope_v)
    load(4, wu_all.at[:, order[0]], wu_v)
    load(5, heads, heads_v)
    load(6, misc_all, misc_g)

    def row_sum(i, values):
        norm_sums[i : i + 1, :] = jnp.sum(values, axis=0, keepdims=True)

    def start():
        lab_one[...] = column(lab_lines[...].astype(f32)).astype(jnp.int32)
        marks = (iota((tokens, chosen.shape[1]), 0) == chosen[...]).astype(f32)
        final = lax.dot_general(
            marks,
            picked[...],
            (((1,), (0,)), ((), ())),
            precision=lax.Precision.HIGHEST,
            preferred_element_type=f32,
        )
        ready(0)
        value, gains = unit_back(final, unit_v[...], scale2[...], norms[4:5, :])
        row_sum(4, gains)
        row_sum(5, final)
        row_sum(7, value)
        grad[...] = value
        grad_low[...] = value.astype(low)
        load(0, unit1, unit_v)
        ready(0)
        act_low[...] = (unit_v[...] * norms[2:3, :] + norms[3:4, :]).astype(low)
        extra[0:tokens, :] = jnp.zeros((tokens, width), f32)

    def spread_out(ref, t, value):
        parts = value.reshape(4, 2, value.shape[0] // 8, value.shape[1])
        for th in range(4):
            ref[th, t] = parts[th]

    def chunk(s):
        t = order[s]
        ahead = order[s + 1] if s + 1 < planes else None
        ready(1, 2, 3, 4)
        pulled = mul(grad_low[...], wd_v[...].reshape(units, width), 1, 1)
        if ahead is not None:
            load(1, wd_all.at[:, ahead], wd_v)
        spread_out(down_g, t, mul(active_v[...], grad_low[...], 0, 0).astype(low))
        if ahead is not None:
            load(2, active.at[ahead], active_v)
        pulled = pulled * slope_v[...].astype(f32)
        if ahead is not None:
            load(3, slope.at[ahead], slope_v)
        sums_row = jnp.sum(pulled, axis=0, keepdims=True)
        col = jnp.broadcast_to(sums_row, (8, units)).T[:, 0:1]
        first = iota((units, q_g.shape[4] - lanes), 1) == 0
        bias = jnp.where(first, col, 0.0).astype(low).reshape(4, 2, share, -1)
        for th in range(4):
            q_g[th, t, :, :, lanes:] = bias[th]
        pulled = pulled.astype(low)
        spread_out(up_g, t, mul(pulled, act_low[...], 0, 0).astype(low))
        extra[0:tokens, :] += mul(pulled, wu_v[...].reshape(units, width))
        if ahead is not None:
            load(4, wu_all.at[:, ahead], wu_v)

    def middle():
        total = grad[...] + extra[0:tokens, :]
        value, gains = unit_back(total, unit_v[...], scale1[...], norms[2:3, :])
        row_sum(2, gains)
        row_sum(3, total)
        row_sum(6, value)
        load(0, unit0, unit_v)
        load(7, wq_all.at[0], wq_v)
        load(8, mixed.at[0], mixed_v)
        grad[...] = value
        value = value.astype(low)
        ready(5, 6)
        extra[...] = mul(value, heads_v[...], 0, 0)
        weight = misc_g[...].astype(f32)[:, :, :, : misc_g.shape[3] // 2]
        weight = weight.reshape(width, width).astype(low)
        heads_v[...] = mul(value, weight).astype(low)
        ready(0)
        act_low[...] = (unit_v[...] * norms[0:1, :] + norms[1:2, :]).astype(low)

    def attend(group):
        ready(7, 8)
        parts = []
        for i in range(3):
            head = 3 * group + i
            q, k, v = (mixed_v[:, (3 * i + j) * HD : (3 * i + j + 1) * HD] for j in range(3))
            pull = heads_v[:, head * HD : (head + 1) * HD]
            if head >= OLD_HEADS:
                pull = (pull.astype(f32) * (STEP / RAMP)).astype(low)
            s = masked_scores(q, k, lab_one[...], lab_row[...])
            p = jnp.exp(s - lse[:, head : head + 1])
            of_v = mul(p.astype(low), pull, 0, 0)
            of_p = mul(pull, v, 1, 1)
            ds = (p * (of_p - jnp.sum(of_p * p, axis=1, keepdims=True))).astype(low)
            of_q = mul(ds, k) * HD**-0.5
            of_k = mul(ds, q, 0, 0) * HD**-0.5
            parts += [of_q, of_k, of_v]
        pulled = jnp.concatenate(parts, axis=1).astype(low)
        if group < 3:
            load(8, mixed.at[group + 1], mixed_v)
        grad[...] += mul(pulled, wq_v[...].reshape(width, lanes), 1, 1)
        if group < 3:
            load(7, wq_all.at[group + 1], wq_v)
        value = mul(act_low[...], pulled, 0, 0).astype(low)
        q_g[group, :, :, :, 0:lanes] = value.reshape(planes, 2, width // (2 * planes), lanes)

    def finish():
        total = grad[...]
        value, gains = unit_back(total, unit_v[...], scale0[...], norms[0:1, :])
        row_sum(0, gains)
        row_sum(1, total)
        seat = jnp.where(ranks[...] < room, home[...] * room + ranks[...], -1)
        marks = ones_where(seat == iota((tokens, parcels.shape[3] * 8 * planes), 1))
        grad_low[...] = value.astype(low)
        parcels[...] = mul(marks, grad_low[...], 0, 0).astype(low).reshape(parcels.shape)
        rest = jnp.zeros((width, width - tokens - 8), f32)
        rows = jnp.concatenate([value.T, norm_sums[...].T, rest], axis=1)
        split_rows = misc_g.shape[3] // 2
        shape = (4, planes, 2, split_rows, width)
        both = jnp.concatenate([extra[...].reshape(shape), rows.reshape(shape)], axis=3)
        misc_g[...] = both.astype(low)

    last = planes - 1
    start()
    for s in range(planes):
        chunk(s)
        for k in (0, 1):
            scatter.post(k, s)
        for k in (0, 1):
            if s >= 1:
                scatter.pair(k, s - 1)
        if s == last:
            for k in (0, 1):
                scatter.plane(k, 0)
    middle()
    for k in (0, 1):
        scatter.pair(k, last)
    for k in (0, 1):
        scatter.line(k, 0)
    ahead = [(f, k, s) for s in range(1, planes) for f in (scatter.plane, scatter.line) for k in (0, 1)]
    cuts = [len(ahead) * i // 5 for i in range(6)]
    for group in range(4):
        attend(group)
        for f, k, s in ahead[cuts[group] : cuts[group + 1]]:
            f(k, s)
    for s in range(planes):
        scatter.post(2, s)
    finish()
    given, stay = give_steps(wires, planes, parcels, back, other, local.at[9])
    for s in range(planes):
        scatter.post(3, s)
    for f, k, s in ahead[cuts[4] :]:
        f(k, s)
    rest = [(k, s) for k in (2, 3) for s in range(planes)]
    for i in range(len(rest) + 4):
        if i < len(rest):
            scatter.pair(*rest[i])
        if 2 <= i < len(rest) + 2:
            scatter.plane(*rest[i - 2])
        if i >= 4:
            scatter.line(*rest[i - 4])
    for k in range(4):
        scatter.total(k)
    for one in given:
        one.wait_recv()
    stay.wait()
    wires.sent()


def collect_kernel(planes, *refs):
    (back, which, logits_part, up, down, q, misc, own) = refs[:8]
    table_grad, total = refs[8:10]
    block, parts, send, recv, local = refs[10:]
    low = jnp.bfloat16
    part, width = table_grad.shape
    marks = ones_where(which[...] == iota((which.shape[0], part), 1))
    table_grad[...] = logits_part[...] + mul(marks, back[...].reshape(-1, width), 0, 0)
    greet(every_chip(planes))
    squares = jnp.zeros((8, width), jnp.float32)
    for i in range(part // 8):
        value = table_grad[8 * i : 8 * i + 8, :]
        squares = squares + value * value
    squares = jnp.sum(squares)
    for ref in (up, down, q, misc):
        squares = squares + jnp.sum(ref[...] * ref[...])
    spot = (iota(block.shape, 0) == 0) & (iota(block.shape, 1) == 0)
    block[...] = jnp.where(spot, squares, own[...])
    wires = Wires(send, recv)
    state = spread_start(wires, local, planes, lambda h, z: block, parts)
    spread_finish(wires, planes, parts, state)
    total[...] = jnp.sum(parts[...].reshape(8 * planes, *block.shape), axis=0)
    wires.sent()


def stepped(weight, grad, first, second, decay, rate):
    first = BETA_ONE * first + (1 - BETA_ONE) * grad
    second = BETA_TWO * second + (1 - BETA_TWO) * grad * grad
    moved = (first * (1 / (1 - BETA_ONE**STEP))) / (
        jnp.sqrt(second * (1 / (1 - BETA_TWO**STEP))) + ADAM_EPSILON
    )
    return (weight - rate * (moved + decay * weight), first, second)


def update_kernel(cuts, *refs):
    count = len(cuts)
    totals = refs[0]
    ins = [refs[1 + 4 * k : 5 + 4 * k] for k in range(count)]
    outs = [refs[1 + 4 * count + 3 * k : 4 + 4 * count + 3 * k] for k in range(count)]
    squares, live = totals[0:1, 0:1], totals[0:1, 2:3]
    norm = jnp.sqrt(squares) / live
    factor = jnp.minimum(1.0, CLIP / norm) / live

    def step(k, at):
        grad, weight, first, second = ins[k]
        row, lane, turned, decay, rate = cuts[k]
        rows, lanes = weight.shape if not turned else weight.shape[::-1]
        if at is None:
            value = grad[row : row + rows, lane : lane + lanes]
            if turned:
                value = value.T
            results = stepped(
                weight[...], value * factor, first[...], second[...], decay, rate
            )
            for ref, result in zip(outs[k], results):
                ref[...] = result
        else:
            results = stepped(
                weight[at, :],
                grad[at, lane : lane + lanes] * factor,
                first[at, :],
                second[at, :],
                decay,
                rate,
            )
            for ref, result in zip(outs[k], results):
                ref[at, :] = result

    @pl.loop(0, ins[0][1].shape[0] // 32)
    def _(i):
        step(0, pl.ds(pl.multiple_of(32 * i, 32), 32))

    @pl.when(pl.program_id(0) == 0)
    def _():
        for k in range(1, count):
            rows = ins[k][1].shape[0]
            if rows % 32 == 0 and cuts[k][0] == 0 and not cuts[k][2]:

                @pl.loop(0, rows // 32)
                def _(i, k=k):
                    step(k, pl.ds(pl.multiple_of(32 * i, 32), 32))

            else:
                step(k, None)


def update(totals, cuts, grads, weights, firsts, seconds, tiles):
    count = len(weights)
    flat, specs, shapes, out_specs = [totals], [pl.BlockSpec(totals.shape, lambda i: (0, 0))], [], []
    for k in range(count):
        for array in (grads[k], weights[k], firsts[k], seconds[k]):
            flat.append(array)
            rows, lanes = array.shape
            if k == 0:
                specs.append(pl.BlockSpec((rows // tiles, lanes), lambda i: (i, 0)))
            else:
                specs.append(pl.BlockSpec((rows, lanes), lambda i: (0, 0)))
        shapes += [jax.ShapeDtypeStruct(weights[k].shape, jnp.float32)] * 3
        out_specs += [specs[-1]] * 3
    result = pl.pallas_call(
        functools.partial(update_kernel, cuts),
        grid=(tiles,),
        out_shape=shapes,
        in_specs=specs,
        out_specs=out_specs,
        compiler_params=pltpu.CompilerParams(vmem_limit_bytes=48 << 20),
        name="update",
    )(*flat)
    return [result[3 * k : 3 * k + 3] for k in range(count)]


def near_first(planes, z):
    order = []
    for j in range(planes):
        spot = jnp.int32(0)
        for zz in range(planes):
            ranked = sorted(range(planes), key=lambda t: (abs(t - zz), t))
            spot = jnp.where(z == zz, ranked[j], spot)
        order.append(spot)
    return order


def head_kernel(planes, first_line, *refs):
    (picked, numbers, table_in) = refs[:3]
    (table_grad, grad_picked, own) = refs[3:6]
    (rows, logits, pulls, table, goals, lse_cols, block, parts) = refs[6:14]
    (grads, sibs, px, pz) = refs[14:18]
    send, recv, send2, recv2, local = refs[18:]
    low, f32 = jnp.bfloat16, jnp.float32
    h, z, c = place()
    part, width = table.shape
    slots = picked.shape[0]
    count = 8 * slots
    device = h * 2 * planes + 2 * z + c
    greet(every_chip(planes))
    lines = Lines(send, recv)
    wires = Wires(send2, recv2)
    gather = Gather(lines, local, planes, [(picked, rows)])
    steps = line_steps(planes)
    gather.launch(0, 0)
    table[...] = table_in[...].astype(low)
    for r in range(2 * planes):
        some = numbers[r, first_line : first_line + 4 * slots // 128, :]
        goals[r] = column(some.astype(f32)).astype(jnp.int32)
    lag = 1
    for i in range(len(steps) + 2 * lag):
        if 1 <= i < len(steps):
            gather.launch(0, steps[i])
        if lag <= i < len(steps) + lag:
            gather.relay(0, steps[i - lag])
        if i >= 2 * lag:
            gather.finish(0, steps[i - 2 * lag])

    def goals_of(t):
        return jnp.concatenate(
            [
                goals[2 * t + core, slots * head : slots * (head + 1), :]
                for head in range(4)
                for core in range(2)
            ],
            axis=0,
        )

    for a, t in enumerate(near_first(planes, z)):
        for s in (a, -a) if a else (0,):
            gather.done(0, s)
        value = mul(rows[:, t].reshape(count, width), table[...], 1, 1)
        logits[t] = value
        top = jnp.max(value, axis=1, keepdims=True)
        lse_cols[t] = top + jnp.log(jnp.sum(jnp.exp(value - top), axis=1, keepdims=True))
    each = count // 128
    for t in range(planes):
        turned = jnp.broadcast_to(lse_cols[t], (count, 128)).T[0:1, :]
        for i in range(each):
            block[each * t + i : each * t + i + 1, :] = turned[:, 128 * i : 128 * (i + 1)]
    state = spread_start(wires, local.at[1], planes, lambda th, tz: block, parts)
    spread_finish(wires, planes, parts, state)
    every = parts[...].reshape(8 * planes, *block.shape)
    peak = jnp.max(every, axis=0)
    total = peak + jnp.log(jnp.sum(jnp.exp(every - peak[None]), axis=0))
    for t in range(planes):
        lse_cols[t] = column(total[each * t : each * (t + 1), :])

    scatter = Scatter(wires, planes, [(grads, grad_picked, sibs, px, pz)])
    order = scatter.to
    hit_sum = jnp.zeros((1, 1), f32)
    for s in range(planes):
        t = order[s]
        goal = goals_of(t)
        value = logits[t]
        hits = iota((count, part), 1) == goal - device * part
        hit_sum = hit_sum + jnp.sum(
            jnp.sum(jnp.where(hits, value, 0.0), axis=1, keepdims=True), axis=0, keepdims=True
        )
        pull = jnp.exp(value - lse_cols[t]) - jnp.where(hits, 1.0, 0.0)
        pulls[t] = jnp.where(goal >= 0, pull, 0.0).astype(low)
        back = mul(pulls[t], table[...]).astype(low).reshape(4, 2, slots, width)
        for th in range(4):
            grads[th, t] = back[th]
        scatter.post(0, s)
        if s:
            scatter.pair(0, s - 1)
    scatter.pair(0, planes - 1)
    mine = goals[2 * z + c, pl.ds(slots * h, slots), :] >= 0
    lse = lse_cols[z, pl.ds(slots * (2 * h + c), slots), :]
    loss = jnp.sum(jnp.where(mine, lse, 0.0), axis=0, keepdims=True) - hit_sum
    live = jnp.sum(jnp.where(mine, 1.0, 0.0), axis=0, keepdims=True)
    lane = iota(own.shape, 1)
    own[...] = jnp.where(lane == 1, loss, jnp.where(lane == 2, live, 0.0))
    own[...] = jnp.where(iota(own.shape, 0) == 0, own[...], 0.0)
    for s in range(planes):
        scatter.plane(0, s)
        if s:
            scatter.line(0, s - 1)
        t = order[s]
        add = mul(pulls[t], rows[:, t].reshape(count, width), 0, 0)
        table_grad[...] = add if s == 0 else table_grad[...] + add
    scatter.line(0, planes - 1)
    scatter.total(0)
    wires.sent()
    lines.sent()


def params(number):
    return pltpu.CompilerParams(
        collective_id=number, has_side_effects=True, vmem_limit_bytes=56 << 20
    )


def dma(count):
    return pltpu.SemaphoreType.DMA((count,))


def spread_wires(planes):
    return 2 * 4 * planes


def scatter_wires(planes, count):
    return count * planes * 11


class Kernels:
    def __init__(self, planes):
        self.planes = planes

    def prepare(self, token_ids, masked_pos, masked_target, segment_ids, norms, bias, table, rest):
        planes = self.planes
        low, f32, i32 = jnp.bfloat16, jnp.float32, jnp.int32
        out_w, places_w, qkv_w, up_w = rest
        part, width = table.shape
        lines = token_ids.shape[0] // 128
        block = (-(-(lines + masked_pos.shape[1] // 128) // 8) * 8, 128)
        small = (16, 128)
        seq = token_ids.shape[0] // 4
        misc = (2 * norms.shape[1], width)
        shape = jax.ShapeDtypeStruct
        count = line_wires(planes, 3)
        posts = 2 * planes - 1 + 2 * spread_wires(planes)
        return pl.pallas_call(
            functools.partial(prepare_kernel, planes, ROOM),
            out_shape=[
                shape((2 * planes, *block), i32),
                shape((2, 4, planes, *small), f32),
                shape((seq, 1), i32),
                shape((seq, 1), i32),
                shape((4 * planes * ROOM, 1), i32),
                shape((8, 128), i32),
                shape((2, 4, planes, ROOM, width), low),
                shape((4, planes, 2, *misc), low),
                shape((4, planes, 2, *qkv_w.shape), low),
                shape((4, planes, 2, *up_w.shape), low),
            ],
            in_specs=[VMEM] * 11,
            out_specs=[VMEM] * 6 + [ANY] * 4,
            scratch_shapes=[
                pltpu.VMEM(block, i32),
                pltpu.VMEM(small, f32),
                pltpu.VMEM(misc, low),
                pltpu.VMEM(qkv_w.shape, low),
                pltpu.VMEM(up_w.shape, low),
                pltpu.VMEM((4, planes, ROOM, width), low),
                dma(count),
                dma(count),
                dma(posts),
                dma(posts),
                dma(6),
            ],
            compiler_params=params(1),
            name="prepare",
        )(
            token_ids.reshape(lines, 128),
            masked_pos,
            masked_target,
            segment_ids.reshape(lines, 128),
            norms,
            bias.reshape(1, -1),
            table,
            out_w,
            places_w,
            qkv_w,
            up_w,
        )

    def forward(self, box, gathered, blocks, home, ranks, extra, labels, norms, bias, ramp, chosen):
        planes = self.planes
        low, f32 = jnp.bfloat16, jnp.float32
        tokens, width = extra.shape
        units = bias.shape[2]
        whole = [jax.ShapeDtypeStruct((4, planes, 2, *b.shape), b.dtype) for b in blocks]
        saved = [
            ((tokens, width), f32),
            ((tokens, 1), f32),
            ((4, tokens, gathered[1].shape[4]), low),
            ((tokens, 128), f32),
            ((tokens, width), low),
            ((tokens, width), f32),
            ((tokens, 1), f32),
            ((planes, tokens, units), low),
            ((planes, tokens, units), low),
            ((tokens, width), f32),
            ((tokens, 1), f32),
            ((chosen.shape[0], width), low),
        ]
        count = line_wires(planes, 1)
        share = blocks[0].shape[0]
        result = pl.pallas_call(
            functools.partial(forward_kernel, planes, ROOM),
            out_shape=whole + [jax.ShapeDtypeStruct(s, t) for s, t in saved],
            in_specs=[VMEM] + [ANY] * 4 + [VMEM] * 9,
            out_specs=[ANY] + [VMEM] * len(saved),
            scratch_shapes=[
                pltpu.VMEM(gathered[0].shape, low),
                pltpu.VMEM(gathered[1].shape, low),
                pltpu.VMEM((1, 4, 2, share, width), low),
                pltpu.VMEM((1, 4, 2, share, width), low),
                pltpu.VMEM((tokens, width), f32),
                pltpu.VMEM((tokens, width), f32),
                pltpu.VMEM((tokens, 1), jnp.int32),
                dma(count),
                dma(count),
                dma(1),
                dma(4),
            ],
            compiler_params=params(2),
            name="forward",
        )(
            box,
            *gathered,
            *blocks,
            home,
            ranks,
            extra,
            labels.reshape(-1, 128),
            labels.reshape(1, -1),
            norms,
            bias,
            ramp,
            chosen.reshape(1, -1),
        )
        return result[:1], result[1:]

    def deliver(self, parcels):
        planes = self.planes
        wires = spread_wires(planes)
        return pl.pallas_call(
            functools.partial(deliver_kernel, planes),
            out_shape=jax.ShapeDtypeStruct((2, *parcels.shape), parcels.dtype),
            in_specs=[ANY],
            out_specs=ANY,
            scratch_shapes=[dma(wires), dma(wires), pltpu.SemaphoreType.DMA],
            compiler_params=params(3),
            name="deliver",
        )(parcels)

    def head(self, picked, numbers, table, first_line):
        planes = self.planes
        low, f32 = jnp.bfloat16, jnp.float32
        part, width = table.shape
        slots = picked.shape[0]
        count = 8 * slots
        block = (planes * count // 128, 128)
        wires = line_wires(planes, 1)
        wires2 = spread_wires(planes) + scatter_wires(planes, 1)
        return pl.pallas_call(
            functools.partial(head_kernel, planes, first_line),
            out_shape=[
                jax.ShapeDtypeStruct((part, width), f32),
                jax.ShapeDtypeStruct((slots, width), f32),
                jax.ShapeDtypeStruct((8, 128), f32),
            ],
            in_specs=[VMEM] * 3,
            out_specs=[VMEM] * 3,
            scratch_shapes=[
                pltpu.VMEM((4, planes, 2, slots, width), low),
                pltpu.VMEM((planes, count, part), f32),
                pltpu.VMEM((planes, count, part), low),
                pltpu.VMEM((part, width), low),
                pltpu.VMEM((2 * planes, 4 * slots, 1), jnp.int32),
                pltpu.VMEM((planes, count, 1), f32),
                pltpu.VMEM(block, f32),
                pltpu.VMEM((2, 4, planes, *block), f32),
                pltpu.VMEM((4, planes, 2, slots, width), low),
                pltpu.VMEM((4, planes, slots, width), low),
                pltpu.VMEM((planes, 3, slots, width), low),
                pltpu.VMEM((planes - 1, slots, width), low),
                dma(wires),
                dma(wires),
                dma(wires2),
                dma(wires2),
                dma(2),
            ],
            compiler_params=params(4),
            name="head",
        )(picked, numbers, table)

    def collect(self, back, which, logits_part, sums, own):
        planes = self.planes
        wires = spread_wires(planes)
        f32 = jnp.float32
        return pl.pallas_call(
            functools.partial(collect_kernel, planes),
            out_shape=[
                jax.ShapeDtypeStruct(logits_part.shape, f32),
                jax.ShapeDtypeStruct(own.shape, f32),
            ],
            in_specs=[VMEM] * 8,
            out_specs=[VMEM] * 2,
            scratch_shapes=[
                pltpu.VMEM(own.shape, f32),
                pltpu.VMEM((2, 4, planes, *own.shape), f32),
                dma(wires),
                dma(wires),
                pltpu.SemaphoreType.DMA,
            ],
            compiler_params=params(6),
            name="collect",
        )(back, which, logits_part, *sums, own)

    def hand_back(self, parcels):
        planes = self.planes
        layer = parcels.shape[1:]
        wires = spread_wires(planes)
        return pl.pallas_call(
            functools.partial(return_kernel, planes),
            out_shape=jax.ShapeDtypeStruct(layer, parcels.dtype),
            in_specs=[VMEM],
            out_specs=ANY,
            scratch_shapes=[pltpu.VMEM(layer, parcels.dtype)]
            + [dma(wires), dma(wires), pltpu.SemaphoreType.DMA],
            compiler_params=params(9),
            name="hand_back",
        )(parcels)

    def backward(self, grad_picked, chosen, norms, labels, home, ranks, saved, gathered):
        planes = self.planes
        low, f32 = jnp.bfloat16, jnp.float32
        unit0, scale0, mixed, lse, heads, unit1, scale1, active, slope, unit2, scale2 = saved
        misc_all, wq_all, wu_all, wd_all = gathered
        tokens, width = unit0.shape
        share = wu_all.shape[3]
        rows, lanes = wq_all.shape[3:]
        wide = -(-(lanes + 1) // 128) * 128
        blocks = [(share, width), (share, width), (rows, wide), misc_all.shape[3:]]
        count = scatter_wires(planes, 4) + spread_wires(planes)

        def held(shape):
            n, m = shape
            return [
                pltpu.VMEM((4, planes, 2, n, m), low),
                pltpu.VMEM((4, planes, n, m), low),
                pltpu.VMEM((planes, 3, n, m), low),
                pltpu.VMEM((planes - 1, n, m), low),
            ]

        units = active.shape[2]
        out = pl.pallas_call(
            functools.partial(backward_kernel, planes, ROOM),
            out_shape=[jax.ShapeDtypeStruct((4, planes, ROOM, width), low)]
            + [jax.ShapeDtypeStruct(b, f32) for b in blocks]
            + [jax.ShapeDtypeStruct((tokens, width), low)],
            in_specs=[VMEM] * 11 + [ANY] * 11,
            out_specs=[ANY] + [VMEM] * 5,
            scratch_shapes=[x for b in blocks for x in held(b)]
            + [
                pltpu.VMEM((2, 4, planes, ROOM, width), low),
                pltpu.VMEM((4, planes, ROOM, width), low),
                pltpu.VMEM((tokens, width), f32),
                pltpu.VMEM((tokens, width), f32),
                pltpu.VMEM((width, width), f32),
                pltpu.VMEM((tokens, width), low),
                pltpu.VMEM((tokens, width), low),
                pltpu.VMEM((4, 2, share, width), low),
                pltpu.VMEM((4, 2, share, width), low),
                pltpu.VMEM((tokens, units), low),
                pltpu.VMEM((tokens, units), low),
                pltpu.VMEM((planes, 2, rows, lanes), low),
                pltpu.VMEM((tokens, lanes), low),
                pltpu.VMEM((8, width), f32),
                pltpu.VMEM((tokens, 1), jnp.int32),
                dma(count),
                dma(count),
                dma(12),
            ],
            compiler_params=pltpu.CompilerParams(
                collective_id=8, has_side_effects=True, vmem_limit_bytes=62 << 20
            ),
            name="backward",
        )(
            grad_picked,
            chosen.reshape(1, -1),
            norms,
            labels.reshape(-1, 128),
            labels.reshape(1, -1),
            home,
            ranks,
            scale0,
            scale1,
            scale2,
            lse,
            unit0,
            unit1,
            unit2,
            mixed,
            heads,
            active,
            slope,
            misc_all,
            wq_all,
            wu_all,
            wd_all,
        )
        return out


class Plain:
    def __init__(self, planes):
        self.planes = planes

    def prepare(self, token_ids, masked_pos, masked_target, segment_ids, norms, bias, table, rest):
        return prepare_plain(
            self, token_ids, masked_pos, masked_target, segment_ids, norms, bias, table, rest
        )

    def gather(self, block):
        whole = lax.all_gather(block, ("head", "row"))
        return whole.reshape(4, self.planes, 2, *block.shape)

    def forward(self, box, gathered, blocks, home, ranks, extra, labels, norms, bias, ramp, chosen):
        whole = [self.gather(b) for b in blocks]
        seat = jnp.where(ranks < ROOM, home * ROOM + ranks, -1)
        saved = forward_plain(
            box, [*gathered, *whole], seat, extra, labels, norms, bias, ramp, chosen
        )
        return whole, saved

    def deliver(self, parcels):
        shape = parcels.shape
        both = jnp.broadcast_to(parcels[:, :, None], (*shape[:2], 2, *shape[2:]))
        flat = both.reshape(8 * self.planes, *shape[2:])
        got = lax.all_to_all(flat, ("head", "row"), split_axis=0, concat_axis=0, tiled=True)
        return jnp.moveaxis(got.reshape(4, self.planes, 2, *shape[2:]), 2, 0)

    def head(self, picked, numbers, table, first_line):
        return head_plain(self, picked, numbers, table, first_line)

    def small(self, block, number):
        return jnp.moveaxis(self.gather(block), 2, 0)

    def scatter_rows(self, grads):
        flat = grads.reshape(-1, grads.shape[-1]).astype(jnp.float32)
        return lax.psum_scatter(flat, ("head", "row"), scatter_dimension=0, tiled=True)

    def backward(self, grad_picked, chosen, norms, labels, home, ranks, saved, gathered):
        return backward_plain(
            self, grad_picked, chosen, norms, labels, home, ranks, saved, gathered
        )

    def collect(self, back, which, logits_part, sums, own):
        part, width = logits_part.shape
        marks = (which == jnp.arange(part)[None, :]).astype(jnp.bfloat16)
        table_grad = logits_part + contract(marks, back.reshape(-1, width), 0, 0)
        squares = sum(jnp.sum(g * g) for g in (table_grad, *sums))
        return table_grad, lax.psum(own.at[0, 0].set(squares), ("head", "row"))

    def hand_back(self, parcels):
        shape = parcels.shape
        flat = jnp.moveaxis(parcels, 0, 2).reshape(8 * self.planes, *shape[3:])
        got = lax.all_to_all(flat, ("head", "row"), split_axis=0, concat_axis=0, tiled=True)
        got = got.reshape(4, self.planes, 2, *shape[3:]).astype(jnp.float32)
        return jnp.sum(got, axis=2).astype(parcels.dtype)


def contract(left, right, left_dim, right_dim):
    return lax.dot_general(
        left, right, (((left_dim,), (right_dim,)), ((), ())), preferred_element_type=jnp.float32
    )


def by_plane(blocks):
    planes, lanes = blocks.shape[1], blocks.shape[4]
    return blocks.transpose(1, 0, 2, 3, 4).reshape(planes, -1, lanes)


def heads_of(mixed):
    tokens = mixed.shape[1]
    parts = mixed.reshape(4, tokens, -1, 3, HD).transpose(3, 1, 0, 2, 4)
    parts = parts.reshape(3, tokens, -1, HD)
    return parts[0], parts[1], parts[2]


def prepare_plain(
    wire, token_ids, masked_pos, masked_target, segment_ids, norms, bias, table, rest
):
    low, f32 = jnp.bfloat16, jnp.float32
    out_w, places_w, qkv_w, up_w = rest
    planes = wire.planes
    rows = 2 * planes
    device = lax.axis_index("head") * rows + lax.axis_index("row")
    chip = lax.axis_index("head") * planes + lax.axis_index("row") // 2
    part, width = table.shape
    share = norms.shape[1]
    lines = token_ids.shape[0] // 128
    at = masked_pos[0][:, None] == jnp.arange(segment_ids.shape[0])[None, :]
    labels = jnp.sum(jnp.where(at, segment_ids[None, :], 0), axis=1)
    target = jnp.where(labels != SEQ - 1, masked_target[0], -1)
    block = jnp.concatenate([token_ids, target])
    block_rows = -(-block.shape[0] // 1024) * 8
    numbers = lax.all_gather(padded(block, block_rows, 128), "row")
    small = jnp.zeros((16, 128), f32).at[:8, :share].set(norms).at[8, : bias.shape[0]].set(bias)
    small_all = wire.small(small.astype(low), 0)
    tokens = token_ids.shape[0] // HEADS
    ids = numbers[:, :lines].reshape(planes, 2, HEADS, tokens)
    ids = ids.transpose(2, 0, 1, 3).reshape(HEADS * planes, 2 * tokens)
    owner = ids // part
    devices = HEADS * rows
    counts = jnp.sum(owner[:, :, None] == jnp.arange(devices), axis=1)
    order = jnp.arange(2 * tokens)
    before = (order[:, None] < order[None, :]).astype(low)
    inside = owner == device
    rank = jnp.dot(inside.astype(low), before, preferred_element_type=f32).astype(jnp.int32)
    hit = jnp.where(inside, rank, -1)[:, None, :] == jnp.arange(ROOM)[None, :, None]
    which = jnp.sum(jnp.where(hit, ids[:, None, :] - device * part + 1, 0), axis=2) - 1
    marks = (which.reshape(-1, 1) == jnp.arange(part)[None, :]).astype(low)
    parcels = jnp.dot(marks, table.astype(low), preferred_element_type=f32).astype(low)
    box = wire.deliver(parcels.reshape(HEADS, planes, ROOM, width))
    own = lax.dynamic_index_in_dim(owner, chip, 0, keepdims=False)
    own_marks = own[:, None] == jnp.arange(devices)
    own_before = contract(before, own_marks.astype(low), 0, 0).astype(jnp.int32)
    own_rank = jnp.sum(jnp.where(own_marks, own_before, 0), axis=1)
    core = lax.axis_index("row") % 2
    own = lax.dynamic_slice_in_dim(own, core * tokens, tokens, 0)
    own_rank = lax.dynamic_slice_in_dim(own_rank, core * tokens, tokens, 0)
    home = (own % 2) * (devices // 2) + own // 2
    misc = jnp.concatenate(
        [out_w, jnp.pad(places_w, ((0, 0), (0, width - SEQ)))], axis=0
    ).astype(low)
    return (
        numbers,
        small_all,
        home[:, None],
        own_rank[:, None],
        which.reshape(-1, 1),
        jnp.max(counts).reshape(1, 1),
        box,
        wire.gather(misc),
        wire.gather(qkv_w.astype(low)),
        wire.gather(up_w.astype(low)),
    )


def forward_plain(parcels, gathered, home, extra, labels, norms, bias, ramp, chosen):
    low = jnp.bfloat16
    misc, wq, wu, wd = gathered
    tokens, width = extra.shape
    share = misc.shape[3] // 2
    rows = parcels.reshape(-1, width)
    looked = jnp.dot(
        (home == jnp.arange(rows.shape[0])[None, :]).astype(low),
        rows,
        preferred_element_type=jnp.float32,
    )
    places = misc[:, :, :, share:, :SEQ].reshape(width, SEQ).T.astype(jnp.float32)
    unit0, scale0 = unit_of(looked + extra + places)
    normed = unit0 * norms[0] + norms[1]
    weight = wq.reshape(4, width, wq.shape[4])
    mixed = jnp.einsum("td,hdj->htj", normed.astype(low), weight, preferred_element_type=jnp.float32)
    mixed = mixed.astype(low)
    query, keys, values = heads_of(mixed)
    attended, summary = attend_fwd(query, keys, values, labels)
    head_ramp = jnp.where(jnp.arange(query.shape[1]) < OLD_HEADS, 1.0, STEP / RAMP)
    heads = (attended * head_ramp[:, None]).astype(low).reshape(tokens, width)
    lse = jnp.pad(summary.T, ((0, 0), (0, 128 - summary.shape[0])))
    weight = misc[:, :, :, :share].reshape(width, width)
    unit1, scale1 = unit_of(normed + contract(heads, weight, 1, 1) + norms[6])
    hidden = unit1 * norms[2] + norms[3]
    u = jnp.einsum(
        "td,pud->ptu", hidden.astype(low), by_plane(wu), preferred_element_type=jnp.float32
    )
    value, rise = gelu_parts(u + bias, ramp)
    active = value.astype(low)
    down = jnp.einsum("ptu,pud->td", active, by_plane(wd), preferred_element_type=jnp.float32)
    unit2, scale2 = unit_of(hidden + down + norms[7])
    final = (unit2 * norms[4] + norms[5]).astype(low)
    marks = (chosen[:, None] == jnp.arange(tokens)[None, :]).astype(low)
    picked = jnp.dot(marks, final, preferred_element_type=jnp.float32).astype(low)
    slope = rise.astype(low)
    return (unit0, scale0, mixed, lse, heads, unit1, scale1, active, slope, unit2, scale2, picked)


def score_block(query, keys, labels):
    scores = jnp.einsum("qhe,khe->hqk", query, keys, preferred_element_type=jnp.float32) * HD ** (
        -0.5
    )
    allowed = labels[:, None] == labels[None, :]
    return jnp.where(allowed[None], scores, -1000000000.0)


def attend_fwd(query, keys, values, labels):
    scores = score_block(query, keys, labels)
    top = jnp.max(scores, axis=-1, keepdims=True)
    weights = jnp.exp(scores - top)
    total = jnp.sum(weights, axis=-1, keepdims=True)
    probs = weights / total
    output = jnp.einsum(
        "hqk,khe->qhe", probs.astype(jnp.bfloat16), values, preferred_element_type=jnp.float32
    )
    return (output, (top + jnp.log(total))[..., 0])


def attend_back(query, keys, values, labels, summary, grad_out):
    scores = score_block(query, keys, labels)
    probs = jnp.exp(scores - summary[..., None])
    grad_values = jnp.einsum(
        "hqk,qhe->khe", probs.astype(jnp.bfloat16), grad_out, preferred_element_type=jnp.float32
    )
    grad_probs = jnp.einsum("qhe,khe->hqk", grad_out, values, preferred_element_type=jnp.float32)
    grad_scores = probs * (grad_probs - jnp.sum(grad_probs * probs, axis=-1, keepdims=True))
    grad_low = grad_scores.astype(jnp.bfloat16)
    grad_query = jnp.einsum(
        "hqk,khe->qhe", grad_low, keys, preferred_element_type=jnp.float32
    ) * HD ** (-0.5)
    grad_keys = jnp.einsum(
        "hqk,qhe->khe", grad_low, query, preferred_element_type=jnp.float32
    ) * HD ** (-0.5)
    return jnp.stack([grad_query, grad_keys, grad_values], axis=2)


def head_plain(wire, picked, numbers, table, first_line):
    low = jnp.bfloat16
    planes = wire.planes
    row_count = 2 * planes
    devices = HEADS * row_count
    device = lax.axis_index("head") * row_count + lax.axis_index("row")
    slots, width = picked.shape
    vocab_part = table.shape[0]
    table = table.astype(low)
    flat = numbers.reshape(row_count, -1)
    targets = flat[:, first_line * 128 : first_line * 128 + HEADS * slots]
    targets = targets.reshape(row_count, HEADS, slots).transpose(1, 0, 2).reshape(-1)
    all_rows = wire.gather(picked).reshape(devices * slots, width)
    valid = (targets >= 0).astype(jnp.float32)
    logits = contract(all_rows, table, 1, 1)
    hits = jnp.arange(vocab_part)[None, :] == (targets - device * vocab_part)[:, None]
    top = jnp.max(logits, axis=1)
    part = top + jnp.log(jnp.sum(jnp.exp(logits - top[:, None]), axis=1))
    parts = wire.gather(part.reshape(-1, 128)).reshape(devices, -1)
    peak = jnp.max(parts, axis=0)
    log_total = peak + jnp.log(jnp.sum(jnp.exp(parts - peak), axis=0))
    target_part = jnp.sum(jnp.where(hits, logits, 0.0))
    log_own = lax.dynamic_slice_in_dim(log_total * valid, device * slots, slots, 0)
    valid_own = lax.dynamic_slice_in_dim(valid, device * slots, slots, 0)
    loss_own = jnp.sum(log_own) - target_part
    count_own = jnp.sum(valid_own)
    grad_logits = (
        valid[:, None] * (jnp.exp(logits - log_total[:, None]) - hits.astype(jnp.float32))
    ).astype(low)
    grad_table = contract(grad_logits, all_rows, 0, 0)
    grad_rows = jnp.dot(grad_logits, table, preferred_element_type=jnp.float32).astype(low)
    grad_picked = wire.scatter_rows(grad_rows.reshape(HEADS, planes, 2, slots, width))
    own = padded(jnp.stack([jnp.float32(0), loss_own, count_own]), 8, 128)
    return grad_table, grad_picked, own


def backward_plain(wire, grad_picked, chosen, norms, labels, home, ranks, saved, gathered):
    low, f32 = jnp.bfloat16, jnp.float32
    unit_zero, scale_zero, mixed, lse, heads_low, unit_one, scale_one = saved[:7]
    active, slope, unit_two, scale_two = saved[7:]
    planes = wire.planes
    devices = 8 * planes
    tokens, width = unit_zero.shape
    share, share_inner = width // devices, gathered[2].shape[3]
    out_full = gathered[0][:, :, :, :share].reshape(width, width)
    qkv_full = gathered[1].reshape(HEADS, width, -1)
    up_full, down_full = by_plane(gathered[2]), by_plane(gathered[3])
    normed_low = (unit_zero * norms[0] + norms[1]).astype(low)
    hidden_low = (unit_one * norms[2] + norms[3]).astype(low)
    query, keys, values = heads_of(mixed)
    heads = query.shape[1]
    summary = lse[:, :heads].T
    head_ramp = jnp.where(jnp.arange(heads) < OLD_HEADS, 1.0, STEP / RAMP).astype(f32)
    chosen_marks = chosen[:, None] == jnp.arange(tokens)[None, :]
    grad_final = lax.dot_general(
        chosen_marks.astype(jnp.float32),
        grad_picked,
        (((0,), (0,)), ((), ())),
        precision=lax.Precision.HIGHEST,
    )
    grad_sum, gain_two = unit_back(grad_final, unit_two, scale_two, norms[4])
    grad_sum_low = grad_sum.astype(low)
    grad_down = jnp.einsum("ptu,td->pud", active, grad_sum_low, preferred_element_type=f32)
    grad_upper = jnp.einsum("td,pud->ptu", grad_sum_low, down_full, preferred_element_type=f32)
    grad_upper = grad_upper * slope.astype(f32)
    grad_upper_low = grad_upper.astype(low)
    grad_up = jnp.einsum("ptu,td->pud", grad_upper_low, hidden_low, preferred_element_type=f32)
    grad_hidden = grad_sum + jnp.einsum(
        "ptu,pud->td", grad_upper_low, up_full, preferred_element_type=f32
    )
    grad_res, gain_one = unit_back(grad_hidden, unit_one, scale_one, norms[2])
    grad_res_low = grad_res.astype(low)
    grad_out = contract(grad_res_low, heads_low, 0, 0)
    grad_heads = jnp.dot(grad_res_low, out_full, preferred_element_type=jnp.float32).astype(low)
    grad_attended = (
        grad_heads.reshape(tokens, heads, HD).astype(jnp.float32) * head_ramp[:, None]
    ).astype(low)
    grad_mixed = attend_back(query, keys, values, labels, summary, grad_attended)
    grad_mixed_low = grad_mixed.astype(low).reshape(tokens, HEADS, -1)
    grad_qkv = jnp.einsum(
        "td,thj->hdj", normed_low, grad_mixed_low, preferred_element_type=jnp.float32
    )
    grad_normed = grad_res + jnp.einsum(
        "thj,hdj->td", grad_mixed_low, qkv_full, preferred_element_type=jnp.float32
    )
    grad_start, gain_zero = unit_back(grad_normed, unit_zero, scale_zero, norms[0])
    grad_start_low = grad_start.astype(low)
    grad_norms = jnp.stack(
        [
            jnp.sum(gain_zero, axis=0),
            jnp.sum(grad_normed, axis=0),
            jnp.sum(gain_one, axis=0),
            jnp.sum(grad_hidden, axis=0),
            jnp.sum(gain_two, axis=0),
            jnp.sum(grad_final, axis=0),
            jnp.sum(grad_res, axis=0),
            jnp.sum(grad_sum, axis=0),
        ]
    )
    grad_bias = jnp.sum(grad_upper, axis=1).reshape(planes, HEADS, 2, share_inner)
    seat = jnp.where(ranks < ROOM, home * ROOM + ranks, -1)
    marks = (seat == jnp.arange(devices * ROOM)[None, :]).astype(low)
    back = contract(marks, grad_start_low, 0, 0).astype(low)
    back = wire.hand_back(back.reshape(2, HEADS, planes, ROOM, width))

    def by_head(grad):
        grad = grad.reshape(planes, HEADS, 2, share_inner, width).astype(low)
        return grad.transpose(1, 0, 2, 3, 4)

    rows = jnp.concatenate(
        [grad_start.T, grad_norms.T, jnp.zeros((width, width - tokens - 8), f32)], axis=1
    )
    misc = jnp.concatenate(
        [grad_out.reshape(devices, share, width), rows.reshape(devices, share, width)], axis=1
    )
    bias = grad_bias.transpose(1, 0, 2, 3).reshape(devices, 1, share_inner)
    return (
        back,
        wire.scatter_rows(by_head(grad_up)),
        wire.scatter_rows(by_head(grad_down)),
        jnp.concatenate(
            [
                wire.scatter_rows(grad_qkv.astype(low).reshape(devices, -1, qkv_full.shape[2])),
                wire.scatter_rows(bias).T,
            ],
            axis=1,
        ),
        wire.scatter_rows(misc.astype(low)),
        grad_start_low,
    )


def adamw(weight, grad, first, second, decay, rate):
    first = BETA_ONE * first + (1 - BETA_ONE) * grad
    second = BETA_TWO * second + (1 - BETA_TWO) * grad * grad
    moved = first / (1 - BETA_ONE**STEP) / (jnp.sqrt(second / (1 - BETA_TWO**STEP)) + ADAM_EPSILON)
    return (weight - rate * (moved + decay * weight), first, second)


def padded(flat, rows, lanes):
    return jnp.pad(flat, (0, rows * lanes - flat.shape[0])).reshape(rows, lanes)


def on_device(
    token_ids,
    segment_ids,
    masked_pos,
    masked_target,
    embedding,
    position_table,
    qkv_weight,
    out_weight,
    up_weight,
    down_weight,
    norm_params,
    up_bias,
    m_embedding,
    m_position,
    m_qkv,
    m_out,
    m_up,
    m_down,
    m_norm,
    m_bias,
    v_embedding,
    v_position,
    v_qkv,
    v_out,
    v_up,
    v_down,
    v_norm,
    v_bias,
):
    low = jnp.bfloat16
    row_count = lax.axis_size("row")
    devices = HEADS * row_count
    planes = row_count // 2
    wire = Kernels(planes) if planes <= 4 else Plain(planes)
    head = lax.axis_index("head")
    row = lax.axis_index("row")
    core = row % 2
    device = head * row_count + row
    vocab_part, width = embedding.shape
    tokens = token_ids.shape[0] // HEADS
    inner = up_weight.shape[1] * devices

    share = width // devices
    share_inner = inner // devices

    labels_all = segment_ids.reshape(HEADS, tokens)
    slots = masked_pos.shape[1] // HEADS
    numbers, small_all, home, ranks, which, fullest, box, *first = wire.prepare(
        token_ids,
        masked_pos,
        masked_target,
        segment_ids,
        norm_params,
        up_bias,
        embedding,
        (out_weight.T, position_table.T, qkv_weight, up_weight.T),
    )
    rounds = -(-fullest[0, 0] // ROOM)
    lines = token_ids.shape[0] // 128
    numbers = numbers.reshape(row_count, -1)
    small_all = jnp.moveaxis(small_all, 0, 2).astype(jnp.float32)
    norms = small_all[..., :8, :share].transpose(3, 0, 1, 2, 4).reshape(8, width)
    bias = small_all[..., 8, :share_inner].transpose(1, 0, 2, 3).reshape(planes, 1, -1)
    ramp = jnp.where(jnp.arange(inner) < OLD_FF, 1.0, STEP / RAMP).astype(jnp.float32)
    ramp = ramp.reshape(HEADS, planes, -1).transpose(1, 0, 2).reshape(planes, 1, -1)
    table = embedding.astype(low)

    def which_in(turn):
        ids = numbers[:, : lines * 128].reshape(planes, 2, HEADS, tokens)
        ids = ids.transpose(2, 0, 1, 3).reshape(HEADS * planes, 2 * tokens) - device * vocab_part
        inside = (ids >= 0) & (ids < vocab_part)
        order = jnp.arange(2 * tokens)
        before = (order[:, None] < order[None, :]).astype(low)
        rank = jnp.dot(inside.astype(low), before, preferred_element_type=jnp.float32)
        rank = jnp.where(inside, rank.astype(jnp.int32), -1)
        spot = jnp.arange(ROOM) + turn * ROOM
        hit = rank[:, None, :] == spot[None, :, None]
        return (jnp.sum(jnp.where(hit, ids[:, None, :] + 1, 0), axis=2) - 1).reshape(-1, 1)

    def parcel_marks(which):
        return (which == jnp.arange(vocab_part)[None, :]).astype(low)

    def token_marks(turn):
        seat = ranks - turn * ROOM
        seat = jnp.where((seat >= 0) & (seat < ROOM), home * ROOM + seat, -1)
        return (seat == jnp.arange(devices * ROOM)[None, :]).astype(low)

    def again(state):
        turn, so_far = state
        parcels = jnp.dot(parcel_marks(which_in(turn)), table, preferred_element_type=jnp.float32)
        more = wire.deliver(parcels.astype(low).reshape(HEADS, planes, ROOM, width))
        more = jnp.dot(
            token_marks(turn),
            more.reshape(devices * ROOM, width),
            preferred_element_type=jnp.float32,
        )
        return turn + 1, so_far + more

    _, extra = lax.while_loop(
        lambda state: state[0] < rounds,
        again,
        (jnp.int32(1), jnp.zeros((tokens, width), jnp.float32)),
    )

    labels = lax.dynamic_index_in_dim(labels_all, head, 0, keepdims=False)
    chosen = lax.dynamic_slice_in_dim(masked_pos[0], head * slots, slots, 0) - head * tokens
    second, saved = wire.forward(
        box,
        first,
        [down_weight.astype(low)],
        home,
        ranks,
        extra,
        labels,
        norms,
        bias,
        ramp,
        chosen,
    )
    gathered = [*first, *second]
    *saved, picked = saved

    grad_table, grad_picked, own = wire.head(
        picked, numbers.reshape(row_count, -1, 128), embedding, lines
    )

    parcels, *sums, of_start = wire.backward(
        grad_picked, chosen, norms, labels, home, ranks, saved, gathered
    )

    def again_back(state):
        turn, so_far = state
        back = contract(token_marks(turn), of_start, 0, 0).astype(low)
        back = wire.hand_back(back.reshape(2, HEADS, planes, ROOM, width))
        more = contract(parcel_marks(which_in(turn)), back.reshape(-1, width), 0, 0)
        return turn + 1, so_far + more

    _, grad_table = lax.while_loop(
        lambda state: state[0] < rounds, again_back, (jnp.int32(1), grad_table)
    )
    grad_table, totals = wire.collect(parcels, which, grad_table, sums, own)
    of_up, of_down, of_qkv, of_misc = sums
    squares, loss_sum, live_count = totals[0, 0], totals[0, 1], totals[0, 2]
    grad_norm = jnp.sqrt(squares) / live_count
    weights = (
        embedding,
        position_table,
        qkv_weight,
        out_weight,
        up_weight,
        down_weight,
        norm_params,
        up_bias,
    )
    firsts = (m_embedding, m_position, m_qkv, m_out, m_up, m_down, m_norm, m_bias)
    seconds = (v_embedding, v_position, v_qkv, v_out, v_up, v_down, v_norm, v_bias)
    decays = (DECAY,) * 6 + (0.0, 0.0)
    rates = (LEARN_RATE,) * 6 + (GAIN_RATE,) * 2
    wide = qkv_weight.shape[1]
    if isinstance(wire, Kernels):
        turned = (False, True, False, True, True, False, False, None)
        view = [
            (lambda a: a.reshape(1, -1)) if t is None else (lambda a: a.T) if t else (lambda a: a)
            for t in turned
        ]
        spots = [(0, 0), (share, 0), (0, 0), (0, 0), (0, 0), (0, 0), (share, SEQ), (0, wide)]
        cuts = [(*spots[k], k > 5, decays[k], rates[k]) for k in range(8)]
        of = (grad_table, of_misc, of_qkv, of_misc, of_up, of_down, of_misc, of_qkv)
        arrays = [[view[k](a) for k, a in enumerate(group)] for group in (weights, firsts, seconds)]
        results = update(totals, cuts, of, *arrays, 10)
        undo = [
            (lambda a: a.reshape(-1)) if t is None else (lambda a: a.T) if t else (lambda a: a)
            for t in turned
        ]
        results = [[undo[k](a) for a in three] for k, three in enumerate(results)]
    else:
        factor = jnp.minimum(1.0, CLIP / grad_norm) / live_count
        grads = (
            grad_table,
            of_misc[share : 2 * share, :SEQ].T,
            of_qkv[:, :wide],
            of_misc[:share].T,
            of_up.T,
            of_down,
            of_misc[share : 2 * share, SEQ : SEQ + 8].T,
            of_qkv[:, wide],
        )
        results = [
            adamw(w, g * factor, m, v, d, r)
            for w, g, m, v, d, r in zip(weights, grads, firsts, seconds, decays, rates)
        ]
    return (
        *(r[0] for r in results),
        *(r[1] for r in results),
        *(r[2] for r in results),
        loss_sum,
        live_count,
        grad_norm,
    )


def solution(mesh):
    vocab = P(("head", "row"), None)
    columns = P(None, ("head", "row"))
    flat = P(("head", "row"))
    weights = (vocab, columns, P("row", "head"), columns, columns, vocab, columns, flat)
    data = (P("row"), P("row"), P("row", None), P("row", None))
    return jax.shard_map(
        on_device,
        mesh=mesh,
        in_specs=(*data, *weights, *weights, *weights),
        out_specs=(*weights, *weights, *weights, P(), P(), P()),
        check_vma=False,
    )
```

```python
import functools

import jax
import jax.numpy as jnp
from jax import lax
from jax.experimental import pallas as pl
from jax.experimental.pallas import tpu as pltpu
from jax.sharding import PartitionSpec as P

HD = 64
SEQ = 512
STEP = 5
RAMP = 10
OLD_HEADS = 8
OLD_FF = 2048


EPSILON = 1e-05
LEARN_RATE = 0.03
GAIN_RATE = 0.5
BETA_ONE = 0.9
BETA_TWO = 0.999
ADAM_EPSILON = 1e-08
DECAY = 0.01
CLIP = 0.02

ROOM = 64
HEADS = 4
MESH = pl.DeviceIdType.MESH
ANY = pl.BlockSpec(memory_space=pl.ANY)
VMEM = pl.BlockSpec(memory_space=pltpu.VMEM)


def place():
    h = lax.axis_index("head")
    r = lax.axis_index("row")
    return h, lax.div(r, 2), lax.rem(r, 2)


def across(h, q):
    if q == 0:
        return h
    if q == 1:
        return h + 1 - 2 * lax.rem(h, 2)
    if q == 2:
        return lax.rem(h + 2, 4)
    return 3 - h


class Wires:
    def __init__(self, send, recv):
        self.send, self.recv, self.used, self.made = send, recv, 0, []

    def copy(self, src, dst, to):
        i = self.used
        self.used += 1
        one = pltpu.make_async_remote_copy(
            src_ref=src,
            dst_ref=dst,
            send_sem=self.send.at[i],
            recv_sem=self.recv.at[i],
            device_id=to,
            device_id_type=MESH,
        )
        one.start()
        self.made.append(one)
        return one

    def sent(self):
        for one in self.made:
            one.wait_send()


def greet(peers):
    barrier = pltpu.get_barrier_semaphore()
    for to in peers:
        pl.semaphore_signal(barrier, inc=1, device_id=to, device_id_type=MESH)
    pl.semaphore_wait(barrier, len(peers))


def near(planes):
    h, z, c = place()
    peers = [(h, 2 * z + 1 - c), (across(h, 1), 2 * z + c), (across(h, 2), 2 * z + c)]
    peers += [(h, 2 * lax.rem(z + s, planes) + c) for s in range(1, planes)]
    return peers


def every_chip(planes):
    h, z, c = place()
    peers = [(h, 2 * z + 1 - c)]
    for q in range(4):
        for s in range(planes):
            if q or s:
                peers.append((across(h, q), 2 * lax.rem(z + s, planes) + c))
    return peers


def split(rows):
    first = -(-rows // 32) * 16
    return pl.ds(0, first), pl.ds(first, rows - first)


def spread_start(wires, local, planes, parcels, out):
    h, z, c = place()
    sib = (h, 2 * z + 1 - c)
    got = {}
    for q in range(4):
        for s in range(planes):
            if q or s:
                th, tz = across(h, q), lax.rem(z + s, planes)
                got[q, s] = wires.copy(parcels(th, tz), out.at[c, h, z], (th, 2 * tz + c))
    mine = pltpu.make_async_copy(parcels(h, z), out.at[c, h, z], local)
    mine.start()
    passed = [wires.copy(parcels(h, z), out.at[c, h, z], sib)]
    return got, mine, passed


def spread_finish(wires, planes, out, state):
    h, z, c = place()
    sib = (h, 2 * z + 1 - c)
    got, mine, passed = state
    for (q, s), one in got.items():
        one.wait_recv()
        there = out.at[c, across(h, q), lax.rem(z - s + planes, planes)]
        passed.append(wires.copy(there, there, sib))
    for one in passed:
        one.wait_recv()
    mine.wait()


def deliver_kernel(planes, parcels, out, send, recv, local):
    greet(every_chip(planes))
    wires = Wires(send, recv)
    state = spread_start(wires, local, planes, lambda h, z: parcels.at[h, z], out)
    spread_finish(wires, planes, out, state)
    wires.sent()


def add_rows(target, others, rows):
    @pl.loop(0, rows // 16)
    def _(i):
        at = pl.ds(pl.multiple_of(i * 16, 16), 16)
        total = target[at, :].astype(jnp.float32)
        for other in others:
            total = total + other[at, :].astype(jnp.float32)
        target[at, :] = total.astype(target.dtype)


class Scatter:
    def __init__(self, wires, planes, groups):
        self.wires, self.planes, self.groups = wires, planes, groups
        h, z, c = place()
        self.h, self.z, self.c = h, z, c
        row = 2 * z + c
        self.sib = (h, 2 * z + 1 - c)
        self.hx, self.hy, self.hd = across(h, 1), across(h, 2), across(h, 3)
        self.xn, self.yn = (self.hx, row), (self.hy, row)
        self.to = [lax.rem(z + 1 + s, planes) for s in range(planes)]
        self.got = {}

    def post(self, k, s):
        grads, out, sibs, px, pz = self.groups[k]
        t = self.to[s]
        for q in (3, 1, 2, 0):
            th = across(self.h, q)
            self.got[k, s, q] = self.wires.copy(
                grads.at[th, t, 1 - self.c], sibs.at[th, t], self.sib
            )

    def pair(self, k, s):
        grads, out, sibs, px, pz = self.groups[k]
        t, rows = self.to[s], sibs.shape[2]
        a, b = split(rows)
        copy, got = self.wires.copy, self.got
        for q in (3, 1, 2, 0):
            got[k, s, q].wait_recv()
            th = across(self.h, q)
            own = grads.at[th, t, self.c]
            add_rows(own, [sibs.at[th, t]], rows)
            if q == 3:
                got[k, s, "xd"] = copy(own.at[a], px.at[t, 0].at[a], self.xn)
                got[k, s, "yd"] = copy(own.at[b], px.at[t, 0].at[b], self.yn)
            if q == 1:
                got[k, s, "x"] = copy(own.at[a], px.at[t, 1].at[a], self.xn)
            if q == 2:
                got[k, s, "y"] = copy(own.at[b], px.at[t, 1].at[b], self.yn)

    def plane(self, k, s):
        grads, out, sibs, px, pz = self.groups[k]
        t, rows = self.to[s], sibs.shape[2]
        a, b = split(rows)
        copy, got = self.wires.copy, self.got
        got[k, s, "xd"].wait_recv()
        own = grads.at[self.hy, t, self.c].at[a]
        add_rows(own, [px.at[t, 0].at[a]], a.size)
        got[k, s, "y2"] = copy(own, px.at[t, 2].at[a], self.yn)
        got[k, s, "yd"].wait_recv()
        own = grads.at[self.hx, t, self.c].at[b]
        add_rows(own, [px.at[t, 0].at[b]], b.size)
        got[k, s, "x2"] = copy(own, px.at[t, 2].at[b], self.xn)

    def line(self, k, s):
        grads, out, sibs, px, pz = self.groups[k]
        t = self.to[s]
        for part in ("x", "y2", "y", "x2"):
            self.got[k, s, part].wait_recv()
        own = grads.at[self.h, t, self.c]
        add_rows(own, [px.at[t, 1], px.at[t, 2]], sibs.shape[2])
        if s < self.planes - 1:
            self.got[k, s, "z"] = self.wires.copy(own, pz.at[s], (self.h, 2 * t + self.c))

    def total(self, k):
        grads, out, sibs, px, pz = self.groups[k]
        h, z, c = self.h, self.z, self.c
        for s in range(self.planes - 1):
            self.got[k, s, "z"].wait_recv()

        @pl.loop(0, out.shape[0] // 16)
        def _(i):
            at = pl.ds(pl.multiple_of(i * 16, 16), 16)
            value = grads[h, z, c, at, :].astype(jnp.float32)
            for s in range(self.planes - 1):
                value = value + pz[s, at, :].astype(jnp.float32)
            out[at, :] = value


def give_steps(wires, planes, parcels, out, other, keep):
    h, z, c = place()
    sib = (h, 2 * z + 1 - c)
    passed = wires.copy(parcels.at[1 - c], other, sib)
    passed.wait_recv()
    given = []
    for q in (3, 1, 2, 0):
        for s in range(planes - 1, -1, -1):
            th, tz = across(h, q), lax.rem(z + s, planes)
            mine = parcels.at[c, th, tz]
            add_rows(mine, [other.at[th, tz]], other.shape[2])
            if q or s:
                given.append(wires.copy(mine, out.at[h, z], (th, 2 * tz + c)))
    stay = pltpu.make_async_copy(parcels.at[c, h, z], out.at[h, z], keep)
    stay.start()
    return given, stay


def return_kernel(planes, parcels, out, other, send, recv, keep):
    greet(every_chip(planes))
    wires = Wires(send, recv)
    given, stay = give_steps(wires, planes, parcels, out, other, keep)
    for one in given:
        one.wait_recv()
    stay.wait()
    wires.sent()


def guarded(ok, act):
    if ok is None:
        act()
    else:
        pl.when(ok)(act)


class Lines:
    def __init__(self, send, recv):
        self.send, self.recv, self.used, self.made = send, recv, 0, []

    def make(self, src, dst, to, ok):
        i = self.used
        self.used += 1
        one = pltpu.make_async_remote_copy(
            src_ref=src,
            dst_ref=dst,
            send_sem=self.send.at[i],
            recv_sem=self.recv.at[i],
            device_id=to,
            device_id_type=MESH,
        )
        self.made.append((one, ok))
        return one

    def sent(self):
        for one, ok in self.made:
            guarded(ok, one.wait_send)


def line_steps(planes):
    return [0] + [d * s for s in range(1, planes) for d in (1, -1)]


class Gather:
    def __init__(self, wires, local, planes, pairs):
        self.wires, self.planes, self.pairs = wires, planes, pairs
        h, z, c = place()
        self.h, self.z, self.c = h, z, c
        row = 2 * z + c
        self.sib = (h, 2 * z + 1 - c)
        self.hx, self.hy, self.hd = across(h, 1), across(h, 2), across(h, 3)
        self.xn, self.yn = (self.hx, row), (self.hy, row)
        self.at, self.have, self.on = {0: z}, {0: None}, {}
        for s in line_steps(planes)[1:]:
            t = z - s
            self.have[s] = (t >= 0) & (t < planes)
            self.at[s] = jnp.clip(t, 0, planes - 1)
        for s in range(planes - 1):
            for d in (1, -1):
                u = z + d
                ok = (u >= 0) & (u < planes)
                self.on[d, s] = (ok & self.have[d * s]) if s else ok
        self.here = []
        for k, (x, out) in enumerate(pairs):
            one = pltpu.make_async_copy(x, out.at[h, z, c], local.at[k])
            one.start()
            self.here.append(one)
        self.line, self.copies = {}, {}

    def onward(self, k, d, s):
        x, out = self.pairs[k]
        t = self.at[d * s]
        ref = x if s == 0 else out.at[self.h, t, self.c]
        u = jnp.clip(self.z + d, 0, self.planes - 1)
        ok = self.on[d, s]
        one = self.wires.make(ref, out.at[self.h, t, self.c], (self.h, 2 * u + self.c), ok)
        self.line[k, d, s] = one
        guarded(ok, one.start)

    def launch(self, k, s):
        x, out = self.pairs[k]
        t, ok = self.at[s], self.have[s]
        here = out.at[self.h, t, self.c]
        ref = x if s == 0 else here
        if s == 0:
            self.onward(k, 1, 0)
            self.onward(k, -1, 0)
        else:
            d, a = (1, s) if s > 0 else (-1, -s)
            guarded(ok, self.line[k, d, a - 1].wait_recv)
            if a < self.planes - 1:
                self.onward(k, d, a)
        make = self.wires.make
        ones = [make(ref, here, to, ok) for to in (self.xn, self.yn, self.sib)]
        self.copies[k, s, "x"], self.copies[k, s, "y"], self.copies[k, s, "s"] = ones

        def act():
            for one in ones:
                one.start()

        guarded(ok, act)

    def relay(self, k, s):
        out = self.pairs[k][1]
        t, ok = self.at[s], self.have[s]
        first, second = split(out.shape[3])
        make, got = self.wires.make, self.copies
        gx, gy = out.at[self.hx, t, self.c], out.at[self.hy, t, self.c]
        got[k, s, "yd"] = make(gx.at[second], gx.at[second], self.yn, ok)
        got[k, s, "sx"] = make(gx, gx, self.sib, ok)
        got[k, s, "xd"] = make(gy.at[first], gy.at[first], self.xn, ok)
        got[k, s, "sy"] = make(gy, gy, self.sib, ok)

        def act():
            got[k, s, "x"].wait_recv()
            got[k, s, "yd"].start()
            got[k, s, "sx"].start()
            got[k, s, "y"].wait_recv()
            got[k, s, "xd"].start()
            got[k, s, "sy"].start()

        guarded(ok, act)

    def finish(self, k, s):
        out = self.pairs[k][1]
        t, ok = self.at[s], self.have[s]
        got = self.copies
        gd = out.at[self.hd, t, self.c]
        got[k, s, "sd"] = self.wires.make(gd, gd, self.sib, ok)

        def act():
            got[k, s, "yd"].wait_recv()
            got[k, s, "xd"].wait_recv()
            got[k, s, "sd"].start()

        guarded(ok, act)

    def done(self, k, s):
        if s == 0:
            self.here[k].wait()

        def act():
            for part in ("s", "sx", "sy", "sd"):
                self.copies[k, s, part].wait_recv()

        guarded(self.have[s], act)


def line_wires(planes, count):
    return count * (2 * planes - 1) * 9


def iota(shape, dim):
    return lax.broadcasted_iota(jnp.int32, shape, dim)


def ones_where(marks):
    return marks.astype(jnp.float32).astype(jnp.bfloat16)


def column(lines):
    turned = lines.T
    return jnp.concatenate([turned[:, i : i + 1] for i in range(lines.shape[0])], axis=0)


def prepare_kernel(planes, room, *refs):
    (tokens, picks, goals, segments, norms_in, bias_in, table) = refs[:7]
    (out_w, places_w, qkv_w, up_w, down_w) = refs[7:12]
    (numbers, norms, bias, extra, home, rank_out, which_out, rounds, box) = refs[12:21]
    (misc_all, wq_all, wu_all, wd_all) = refs[21:25]
    (small_all, block, small, misc, wq, wu, wd, parcels) = refs[25:33]
    send, recv, send2, recv2, local = refs[33:]
    low, f32 = jnp.bfloat16, jnp.float32
    h, z, c = place()
    row = 2 * z + c
    rows = 2 * planes
    device = h * rows + row
    part = table.shape[0]
    lines = tokens.shape[0]
    each = lines // 4
    peers = [(s, e) for s in range(planes) for e in range(2) if s or e]
    peers = [(h, 2 * lax.rem(z + s, planes) + lax.rem(c + e, 2)) for s, e in peers]
    chips = [
        (across(h, q), 2 * lax.rem(z + s, planes) + c) for q in (1, 2, 3) for s in range(planes)
    ]
    padding = ones_where(segments[...] == SEQ - 1)
    at = iota((128, picks.shape[1]), 0) == lax.rem(picks[...], 128)
    padded_at = mul(padding, ones_where(at))
    line = iota((lines, picks.shape[1]), 0) == lax.div(picks[...], 128)
    padded_at = jnp.sum(jnp.where(line, padded_at, 0.0), axis=0, keepdims=True)
    goal = jnp.where(padded_at == 0.0, goals[...], -1)
    block[...] = jnp.zeros_like(block)
    block[0:lines, :] = tokens[...]
    for i in range(goal.shape[1] // 128):
        block[lines + i : lines + i + 1, :] = goal[:, 128 * i : 128 * (i + 1)]
    share, width = norms_in.shape[1], table.shape[1]
    small[...] = jnp.zeros_like(small)
    small[0:8, 0:share] = norms_in[...].astype(low).astype(f32)
    small[8:9, 0 : bias_in.shape[1]] = bias_in[...].astype(low).astype(f32)
    greet(peers + chips)
    posts = Wires(send2, recv2)
    mine = pltpu.make_async_copy(block, numbers.at[row], local.at[0])
    mine.start()
    ids = [posts.copy(block, numbers.at[row], to) for to in peers]
    spread = spread_start(posts, local.at[1], planes, lambda th, tz: small, small_all)
    wq[...] = qkv_w[...].astype(low)
    wu[...] = up_w[...].astype(low)
    wd[...] = down_w[...].astype(low)
    places_row = jnp.concatenate([places_w[...], jnp.zeros((share, width - SEQ), f32)], axis=1)
    misc[...] = jnp.concatenate([out_w[...], places_row], axis=0).astype(low)
    lines_of = Lines(send, recv)
    pairs = [(misc, misc_all), (wq, wq_all), (wu, wu_all), (wd, wd_all)]
    kinds = range(4)
    gather = Gather(lines_of, local.at[pl.ds(2, 4)], planes, pairs)
    for k in kinds:
        gather.launch(k, 0)
    for one in ids:
        one.wait_recv()
    mine.wait()
    for k in kinds:
        gather.launch(k, 1)
        gather.launch(k, -1)

    everyone = numbers[...][:, :lines, :].reshape(rows * lines, 128)
    total = rows * lines
    by_row, by_col = iota((total, total), 0), iota((total, total), 1)

    def parts(n):
        return n // (2 * lines), (n // lines) % 2, (n // each) % 4, n % each

    def parts_of(n):
        plane = lax.div(n, 2 * lines)
        core = lax.rem(lax.div(n, lines), 2)
        head = lax.rem(lax.div(n, each), 4)
        return plane, core, head, lax.rem(n, each)

    pr, cr, hr, ir = parts_of(by_row)
    pc, cc, hc, ic = parts_of(by_col)
    same = (pr == pc) & (hr == hc)
    earlier = same & (cc * each + ic < cr * each + ir)
    earlier = ones_where(earlier)
    before = ones_where(iota((128, 128), 0) < iota((128, 128), 1))
    ones = jnp.ones((128, 128), low)

    near_id = everyone - device * part
    inside = (near_id >= 0) & (near_id < part)
    marks = ones_where(inside)
    in_row = mul(marks, ones).astype(low)
    rank = (mul(marks, before) + mul(earlier, in_row)).astype(jnp.int32)
    rank = jnp.where(inside, rank, -1)

    slot = iota((room, 128), 0)
    low_table = table[...].astype(low)
    vocab = iota((room, part), 1)
    for th in range(4):
        for tz in range(planes):
            found = jnp.zeros((room, 128), jnp.int32)
            for core in range(2):
                for i in range(each):
                    n = (tz * 2 + core) * lines + th * each + i
                    hit = rank[n : n + 1, :] == slot
                    found = found + jnp.where(hit, near_id[n : n + 1, :] + 1, 0)
            which = jnp.sum(found.astype(f32), axis=1, keepdims=True).astype(jnp.int32) - 1
            at = (th * planes + tz) * room
            which_out[at : at + room, :] = which
            parcels[th, tz] = mul(ones_where(which == vocab), low_table).astype(low)
    post = spread_start(posts, local.at[6], planes, lambda th, tz: parcels.at[th, tz], box)

    for k in kinds:
        gather.relay(k, 0)

    counts = jnp.zeros((total, 128), f32)
    for d in range(4 * rows):
        owned = ones_where((everyone >= d * part) & (everyone < (d + 1) * part))
        counts = counts + mul(owned, ones_where(iota((128, 128), 1) == d))
    fullest = jnp.max(mul(ones_where(same), counts.astype(low)))
    rounds[...] = jnp.full(rounds.shape, fullest.astype(jnp.int32))

    ids_here = [
        numbers[2 * z + core, pl.ds(each * h, each), :].astype(f32) for core in range(2)
    ]
    own = column(numbers[row, pl.ds(each * h, each), :].astype(f32))
    count = each * 128

    def owners(values):
        owner = jnp.zeros(values.shape, f32)
        for d in range(1, 4 * rows):
            owner = owner + jnp.where(values >= float(d * part), 1.0, 0.0)
        return owner

    own_owner = owners(own)
    own_spot = iota((count, 128), 0) + c * count
    ahead = jnp.zeros((count, 128), f32)
    for core in range(2):
        them = owners(ids_here[core])
        for i in range(each):
            spot = core * count + 128 * i + iota((count, 128), 1)
            hit = (own_owner == them[i : i + 1, :]) & (spot < own_spot)
            ahead = ahead + jnp.where(hit, 1.0, 0.0)
    rank_out[...] = jnp.sum(ahead, axis=1, keepdims=True).astype(jnp.int32)
    owner = own_owner.astype(jnp.int32)
    home[...] = lax.rem(owner, 2) * (2 * rows) + lax.div(owner, 2)

    order = [(k, s) for k in kinds for s in (1, -1)]
    order += [(k, s) for a in range(2, planes) for k in kinds for s in (a, -a)]
    for k in kinds:
        gather.finish(k, 0)
    extra[...] = jnp.zeros_like(extra)
    spread_finish(posts, planes, small_all, spread)
    norms[...] = jnp.zeros_like(norms)
    wide_row, wide_lane = iota((128, width), 0), iota((128, width), 1)
    units = bias.shape[2]
    unit_row, unit_lane = iota((128, units), 0), iota((128, units), 1)
    span = bias_in.shape[1]
    for tz in range(planes):
        of_units = jnp.zeros((8, units), f32)
        for th in range(4):
            for core in range(2):
                piece = small_all[core, th, tz].astype(low)
                at = share * (th * rows + 2 * tz + core)
                pick = ones_where((wide_lane == wide_row + at) & (wide_row < share))
                norms[...] += mul(piece[0:8, :], pick)
                at = span * (2 * th + core)
                pick = ones_where((unit_lane == unit_row + at) & (unit_row < span))
                of_units = of_units + mul(piece[8:16, :], pick)
        bias[tz] = of_units[0:1, :]
    lag = 4
    for i in range(len(order) + 2 * lag):
        if i == len(order):
            spread_finish(posts, planes, box, post)
        if 8 <= i < len(order):
            gather.launch(*order[i])
        if lag <= i < len(order) + lag:
            gather.relay(*order[i - lag])
        if i >= 2 * lag:
            gather.finish(*order[i - 2 * lag])
    for k in kinds:
        for s in line_steps(planes):
            gather.done(k, s)
    posts.sent()
    lines_of.sent()


def mul(left, right, left_dim=1, right_dim=0):
    return lax.dot_general(
        left, right, (((left_dim,), (right_dim,)), ((), ())), preferred_element_type=jnp.float32
    )


def unit_of(values):
    center = values - jnp.mean(values, axis=-1, keepdims=True)
    scale = lax.rsqrt(jnp.mean(center * center, axis=-1, keepdims=True) + EPSILON)
    return center * scale, scale


ERF_TOP = (
    -2.72614225801306e-10,
    2.77068142495902e-08,
    -2.10102402082508e-06,
    -5.69250639462346e-05,
    -7.34990630326855e-04,
    -2.95459980854025e-03,
    -1.60960333262415e-02,
)
ERF_LOW = (
    -1.45660718464996e-05,
    -2.13374055278905e-04,
    -1.68282697438203e-03,
    -7.37332916720468e-03,
    -1.42647390514189e-02,
)


def erf(x):
    x = jnp.clip(x, -4.0, 4.0)
    square = x * x
    top = jnp.full_like(x, ERF_TOP[0])
    for c in ERF_TOP[1:]:
        top = top * square + c
    bottom = jnp.full_like(x, ERF_LOW[0])
    for c in ERF_LOW[1:]:
        bottom = bottom * square + c
    return x * top / bottom


def gelu_parts(u, ramp):
    cdf = 0.5 + 0.5 * erf(u * (0.5**0.5))
    density = jnp.exp(-0.5 * u * u) * 0.3989422804014327
    return u * cdf * ramp, (cdf + u * density) * ramp


def head_slice(ref, head, part):
    group, i = head // 3, head % 3
    start = (3 * i + part) * HD
    return ref[group, :, start : start + HD]


def masked_scores(q, k, labels_col, labels_row):
    s = mul(q, k, 1, 1) * HD**-0.5
    return jnp.where(labels_col == labels_row, s, -1000000000.0)


def forward_kernel(planes, room, *refs):
    (box, misc_all, wq_all, wu_all, wd_all, home, ranks, extra) = refs[:8]
    (lab_col, lab_row, norms, bias, chosen) = refs[8:13]
    (unit0, scale0, mixed, lse, heads, unit1, scale1, active, slope, unit2, scale2, picked) = refs[
        13:25
    ]
    (misc_v, wq_v, wu_v, wd_v, hidden, total, lab_one, loads) = refs[25:]
    low = jnp.bfloat16
    tokens, width = unit0.shape

    def load(i, src, dst):
        one = pltpu.make_async_copy(src, dst, loads.at[i])
        one.start()
        return one

    ready_misc = load(0, misc_all, misc_v)
    ready_q = load(1, wq_all, wq_v)
    up_ready = load(2, wu_all, wu_v)
    down_ready = load(3, wd_all, wd_v)

    def start_norm():
        lab_one[...] = column(lab_col[...].astype(jnp.float32)).astype(jnp.int32)
        ready_misc.wait()
        spots = iota((tokens, box.shape[3] * 8 * planes), 1)
        seat = jnp.where(ranks[...] < room, home[...] * room + ranks[...], -1)
        rows = box[...].reshape(-1, width)
        looked = mul(ones_where(seat == spots), rows) + extra[...]
        pieces = misc_v[...].astype(jnp.float32)
        share = misc_v.shape[3] // 2
        places = pieces[:, :, :, share:, :SEQ].reshape(width, SEQ).T
        unit, scale = unit_of(looked + places)
        unit0[...] = unit
        scale0[...] = scale
        hidden[...] = unit * norms[0:1, :] + norms[1:2, :]

    def project(group):
        weight = wq_v[group].reshape(width, wq_v.shape[4])
        mixed[group] = mul(hidden[...].astype(low), weight).astype(low)

    def attend(pair):
        outs = []
        for head in (2 * pair, 2 * pair + 1):
            q, k, v = (head_slice(mixed, head, j) for j in range(3))
            s = masked_scores(q, k, lab_one[...], lab_row[...])
            top = jnp.max(s, axis=1, keepdims=True)
            e = jnp.exp(s - top)
            sums = jnp.sum(e, axis=1, keepdims=True)
            lse[:, head : head + 1] = top + jnp.log(sums)
            p = (e / sums).astype(low)
            scale = 1.0 if head < OLD_HEADS else STEP / RAMP
            outs.append((mul(p, v) * scale).astype(low))
        heads[:, 2 * HD * pair : 2 * HD * (pair + 1)] = jnp.concatenate(outs, axis=1)

    def middle():
        share = misc_v.shape[3] // 2
        weight = misc_v[...].astype(jnp.float32)[:, :, :, :share].reshape(width, width).astype(low)
        value = hidden[...] + mul(heads[...], weight, 1, 1) + norms[6:7, :]
        unit, scale = unit_of(value)
        unit1[...] = unit
        scale1[...] = scale
        hidden[...] = unit * norms[2:3, :] + norms[3:4, :]
        total[...] = hidden[...] + norms[7:8, :]

    def chunk(t):
        units = wu_v.shape[0] * 2 * wu_v.shape[3]
        u = mul(hidden[...].astype(low), wu_v[:, t].reshape(units, width), 1, 1) + bias[t]
        value, rise = gelu_parts(u, unit_ramp(planes, t, units))
        value = value.astype(low)
        active[t] = value
        slope[t] = rise.astype(low)
        total[...] += mul(value, wd_v[:, t].reshape(units, width))

    def last():
        unit, scale = unit_of(total[...])
        unit2[...] = unit
        scale2[...] = scale
        final = (unit * norms[4:5, :] + norms[5:6, :]).astype(low)
        marks = ones_where(iota((tokens, chosen.shape[1]), 0) == chosen[...])
        picked[...] = mul(marks, final, 0, 0).astype(low)

    start_norm()
    ready_q.wait()
    for group in range(4):
        project(group)
    for pair in range(6):
        attend(pair)
    middle()
    up_ready.wait()
    down_ready.wait()
    for t in range(planes):
        chunk(t)
    last()


def unit_back(grad, unit, scale, gain):
    inner = grad * gain
    back = scale * (
        inner
        - jnp.mean(inner, axis=-1, keepdims=True)
        - unit * jnp.mean(inner * unit, axis=-1, keepdims=True)
    )
    return (back, grad * unit)


def backward_kernel(planes, room, *refs):
    (picked, chosen, norms, lab_lines, lab_row, home, ranks) = refs[:7]
    (scale0, scale1, scale2, lse) = refs[7:11]
    (unit0, unit1, unit2, mixed, heads, active, slope) = refs[11:18]
    (misc_all, wq_all, wu_all, wd_all) = refs[18:22]
    (back, up_sum, down_sum, q_sum, misc_sum, grad_low) = refs[22:28]
    (ups, downs, qs, miscs) = (refs[28 + 4 * k : 32 + 4 * k] for k in range(4))
    (parcels, other, unit_v, grad, extra, act_low, heads_v) = refs[44:51]
    (wu_v, wd_v, active_v, slope_v, wq_v, mixed_v, pulled_v, norm_sums, lab_one) = refs[51:60]
    send, recv, local = refs[60:]
    low, f32 = jnp.bfloat16, jnp.float32
    h, z, c = place()
    tokens, width = unit_v.shape
    units = active_v.shape[1]
    share = wu_v.shape[2]
    lanes = mixed_v.shape[1]
    up_g, down_g, q_g, misc_g = ups[0], downs[0], qs[0], miscs[0]
    loads = {}

    def load(i, src, dst):
        one = pltpu.make_async_copy(src, dst, local.at[i])
        one.start()
        loads[i] = one

    def ready(*which):
        for i in which:
            loads.pop(i).wait()

    greet(every_chip(planes))
    wires = Wires(send, recv)
    sums = [up_sum, down_sum, q_sum, misc_sum]
    groups = [(g[0], out, *g[1:]) for g, out in zip((ups, downs, qs, miscs), sums)]
    scatter = Scatter(wires, planes, groups)
    order = scatter.to
    load(0, unit2, unit_v)
    load(1, wd_all.at[:, order[0]], wd_v)
    load(2, active.at[order[0]], active_v)
    load(3, slope.at[order[0]], slope_v)
    load(4, wu_all.at[:, order[0]], wu_v)
    load(5, heads, heads_v)
    load(6, misc_all, misc_g)

    def row_sum(i, values):
        norm_sums[i : i + 1, :] = jnp.sum(values, axis=0, keepdims=True)

    def start():
        lab_one[...] = column(lab_lines[...].astype(f32)).astype(jnp.int32)
        marks = (iota((tokens, chosen.shape[1]), 0) == chosen[...]).astype(f32)
        final = lax.dot_general(
            marks,
            picked[...],
            (((1,), (0,)), ((), ())),
            precision=lax.Precision.HIGHEST,
            preferred_element_type=f32,
        )
        ready(0)
        value, gains = unit_back(final, unit_v[...], scale2[...], norms[4:5, :])
        row_sum(4, gains)
        row_sum(5, final)
        row_sum(7, value)
        grad[...] = value
        grad_low[...] = value.astype(low)
        load(0, unit1, unit_v)
        ready(0)
        act_low[...] = (unit_v[...] * norms[2:3, :] + norms[3:4, :]).astype(low)
        extra[0:tokens, :] = jnp.zeros((tokens, width), f32)

    def spread_out(ref, t, value):
        parts = value.reshape(4, 2, value.shape[0] // 8, value.shape[1])
        for th in range(4):
            ref[th, t] = parts[th]

    def chunk(s):
        t = order[s]
        ahead = order[s + 1] if s + 1 < planes else None
        ready(1, 2, 3, 4)
        pulled = mul(grad_low[...], wd_v[...].reshape(units, width), 1, 1)
        if ahead is not None:
            load(1, wd_all.at[:, ahead], wd_v)
        spread_out(down_g, t, mul(active_v[...], grad_low[...], 0, 0).astype(low))
        if ahead is not None:
            load(2, active.at[ahead], active_v)
        pulled = pulled * slope_v[...].astype(f32)
        if ahead is not None:
            load(3, slope.at[ahead], slope_v)
        sums_row = jnp.sum(pulled, axis=0, keepdims=True)
        col = jnp.broadcast_to(sums_row, (8, units)).T[:, 0:1]
        first = iota((units, q_g.shape[4] - lanes), 1) == 0
        bias = jnp.where(first, col, 0.0).astype(low).reshape(4, 2, share, -1)
        for th in range(4):
            q_g[th, t, :, :, lanes:] = bias[th]
        pulled = pulled.astype(low)
        spread_out(up_g, t, mul(pulled, act_low[...], 0, 0).astype(low))
        extra[0:tokens, :] += mul(pulled, wu_v[...].reshape(units, width))
        if ahead is not None:
            load(4, wu_all.at[:, ahead], wu_v)

    def middle():
        total = grad[...] + extra[0:tokens, :]
        value, gains = unit_back(total, unit_v[...], scale1[...], norms[2:3, :])
        row_sum(2, gains)
        row_sum(3, total)
        row_sum(6, value)
        load(0, unit0, unit_v)
        load(7, wq_all.at[0], wq_v)
        load(8, mixed.at[0], mixed_v)
        grad[...] = value
        value = value.astype(low)
        ready(5, 6)
        extra[...] = mul(value, heads_v[...], 0, 0)
        weight = misc_g[...].astype(f32)[:, :, :, : misc_g.shape[3] // 2]
        weight = weight.reshape(width, width).astype(low)
        heads_v[...] = mul(value, weight).astype(low)
        ready(0)
        act_low[...] = (unit_v[...] * norms[0:1, :] + norms[1:2, :]).astype(low)

    def attend(group):
        ready(7, 8)
        parts = []
        for i in range(3):
            head = 3 * group + i
            q, k, v = (mixed_v[:, (3 * i + j) * HD : (3 * i + j + 1) * HD] for j in range(3))
            pull = heads_v[:, head * HD : (head + 1) * HD]
            if head >= OLD_HEADS:
                pull = (pull.astype(f32) * (STEP / RAMP)).astype(low)
            s = masked_scores(q, k, lab_one[...], lab_row[...])
            p = jnp.exp(s - lse[:, head : head + 1])
            of_v = mul(p.astype(low), pull, 0, 0)
            of_p = mul(pull, v, 1, 1)
            ds = (p * (of_p - jnp.sum(of_p * p, axis=1, keepdims=True))).astype(low)
            of_q = mul(ds, k) * HD**-0.5
            of_k = mul(ds, q, 0, 0) * HD**-0.5
            parts += [of_q, of_k, of_v]
        pulled = jnp.concatenate(parts, axis=1).astype(low)
        if group < 3:
            load(8, mixed.at[group + 1], mixed_v)
        grad[...] += mul(pulled, wq_v[...].reshape(width, lanes), 1, 1)
        if group < 3:
            load(7, wq_all.at[group + 1], wq_v)
        pulled_v[group] = pulled

    def weigh(group):
        value = mul(act_low[...], pulled_v[group], 0, 0).astype(low)
        q_g[group, :, :, :, 0:lanes] = value.reshape(planes, 2, width // (2 * planes), lanes)

    def finish():
        total = grad[...]
        value, gains = unit_back(total, unit_v[...], scale0[...], norms[0:1, :])
        row_sum(0, gains)
        row_sum(1, total)
        seat = jnp.where(ranks[...] < room, home[...] * room + ranks[...], -1)
        marks = ones_where(seat == iota((tokens, parcels.shape[3] * 8 * planes), 1))
        grad[...] = value
        grad_low[...] = value.astype(low)
        parcels[...] = mul(marks, grad_low[...], 0, 0).astype(low).reshape(parcels.shape)

    def assemble():
        rest = jnp.zeros((width, width - tokens - 8), f32)
        rows = jnp.concatenate([grad[...].T, norm_sums[...].T, rest], axis=1)
        split_rows = misc_g.shape[3] // 2
        shape = (4, planes, 2, split_rows, width)
        both = jnp.concatenate([extra[...].reshape(shape), rows.reshape(shape)], axis=3)
        misc_g[...] = both.astype(low)

    last = planes - 1
    both = (0, 1)

    def pass_on(*events):
        for event, s in events:
            for k in both:
                if 0 <= s <= last:
                    event(k, s)

    start()
    for s in range(planes):
        chunk(s)
        pass_on((scatter.post, s), (scatter.pair, s - 1))
    pass_on((scatter.plane, 0))
    middle()
    pass_on((scatter.pair, last))
    pass_on((scatter.plane, 1 if last > 1 else -1))
    attend(0)
    pass_on((scatter.line, 0))
    for group in range(1, 4):
        attend(group)
        pass_on((scatter.plane, group + 1 if group + 1 < last else -1))
        pass_on((scatter.line, group if group < last - 1 else -1))
    pass_on((scatter.plane, last))
    for s in range(4, last):
        pass_on((scatter.line, s - 1), (scatter.plane, s + 1 if s + 1 < last else -1))
    finish()
    given, stay = give_steps(wires, planes, parcels, back, other, local.at[9])
    if last > 1:
        pass_on((scatter.line, last - 1))
    for group in range(4):
        weigh(group)
    for s in range(planes):
        scatter.post(2, s)
    pass_on((scatter.line, last))
    assemble()
    for s in range(planes):
        scatter.post(3, s)
    rest = [(k, s) for k in (2, 3) for s in range(planes)]
    for i in range(len(rest) + 4):
        if i < len(rest):
            scatter.pair(*rest[i])
        if 2 <= i < len(rest) + 2:
            scatter.plane(*rest[i - 2])
        if i >= 4:
            scatter.line(*rest[i - 4])
    for k in range(4):
        scatter.total(k)
    for one in given:
        one.wait_recv()
    stay.wait()
    wires.sent()


def collect_kernel(planes, *refs):
    (back, which, logits_part, up, down, q, misc, own) = refs[:8]
    table_grad, total = refs[8:10]
    block, parts, send, recv, local = refs[10:]
    low = jnp.bfloat16
    part, width = table_grad.shape
    marks = ones_where(which[...] == iota((which.shape[0], part), 1))
    table_grad[...] = logits_part[...] + mul(marks, back[...].reshape(-1, width), 0, 0)
    greet(every_chip(planes))
    squares = jnp.zeros((8, width), jnp.float32)
    for i in range(part // 8):
        value = table_grad[8 * i : 8 * i + 8, :]
        squares = squares + value * value
    squares = jnp.sum(squares)
    for ref in (up, down, q, misc):
        squares = squares + jnp.sum(ref[...] * ref[...])
    spot = (iota(block.shape, 0) == 0) & (iota(block.shape, 1) == 0)
    block[...] = jnp.where(spot, squares, own[...])
    wires = Wires(send, recv)
    state = spread_start(wires, local, planes, lambda h, z: block, parts)
    spread_finish(wires, planes, parts, state)
    total[...] = jnp.sum(parts[...].reshape(8 * planes, *block.shape), axis=0)
    wires.sent()


def stepped(weight, grad, first, second, decay, rate):
    first = BETA_ONE * first + (1 - BETA_ONE) * grad
    second = BETA_TWO * second + (1 - BETA_TWO) * grad * grad
    moved = (first * (1 / (1 - BETA_ONE**STEP))) / (
        jnp.sqrt(second * (1 / (1 - BETA_TWO**STEP))) + ADAM_EPSILON
    )
    return (weight - rate * (moved + decay * weight), first, second)


def update_kernel(cuts, *refs):
    count = len(cuts)
    totals = refs[0]
    ins = [refs[1 + 4 * k : 5 + 4 * k] for k in range(count)]
    outs = [refs[1 + 4 * count + 3 * k : 4 + 4 * count + 3 * k] for k in range(count)]
    squares, live = totals[0:1, 0:1], totals[0:1, 2:3]
    norm = jnp.sqrt(squares) / live
    factor = jnp.minimum(1.0, CLIP / norm) / live

    def step(k, at):
        grad, weight, first, second = ins[k]
        row, lane, turned, decay, rate = cuts[k]
        rows, lanes = weight.shape if not turned else weight.shape[::-1]
        if at is None:
            value = grad[row : row + rows, lane : lane + lanes]
            if turned:
                value = value.T
            results = stepped(
                weight[...], value * factor, first[...], second[...], decay, rate
            )
            for ref, result in zip(outs[k], results):
                ref[...] = result
        else:
            results = stepped(
                weight[at, :],
                grad[at, lane : lane + lanes] * factor,
                first[at, :],
                second[at, :],
                decay,
                rate,
            )
            for ref, result in zip(outs[k], results):
                ref[at, :] = result

    @pl.loop(0, ins[0][1].shape[0] // 32)
    def _(i):
        step(0, pl.ds(pl.multiple_of(32 * i, 32), 32))

    @pl.when(pl.program_id(0) == 0)
    def _():
        for k in range(1, count):
            rows = ins[k][1].shape[0]
            if rows % 32 == 0 and cuts[k][0] == 0 and not cuts[k][2]:

                @pl.loop(0, rows // 32)
                def _(i, k=k):
                    step(k, pl.ds(pl.multiple_of(32 * i, 32), 32))

            else:
                step(k, None)


def update(totals, cuts, grads, weights, firsts, seconds, tiles):
    count = len(weights)
    flat, specs, shapes, out_specs = [totals], [pl.BlockSpec(totals.shape, lambda i: (0, 0))], [], []
    for k in range(count):
        for array in (grads[k], weights[k], firsts[k], seconds[k]):
            flat.append(array)
            rows, lanes = array.shape
            if k == 0:
                specs.append(pl.BlockSpec((rows // tiles, lanes), lambda i: (i, 0)))
            else:
                specs.append(pl.BlockSpec((rows, lanes), lambda i: (0, 0)))
        shapes += [jax.ShapeDtypeStruct(weights[k].shape, jnp.float32)] * 3
        out_specs += [specs[-1]] * 3
    result = pl.pallas_call(
        functools.partial(update_kernel, cuts),
        grid=(tiles,),
        out_shape=shapes,
        in_specs=specs,
        out_specs=out_specs,
        compiler_params=pltpu.CompilerParams(vmem_limit_bytes=48 << 20),
        name="update",
    )(*flat)
    return [result[3 * k : 3 * k + 3] for k in range(count)]


def near_first(planes, z):
    order = []
    for j in range(planes):
        spot = jnp.int32(0)
        for zz in range(planes):
            ranked = sorted(range(planes), key=lambda t: (abs(t - zz), t))
            spot = jnp.where(z == zz, ranked[j], spot)
        order.append(spot)
    return order


def head_kernel(planes, first_line, *refs):
    (picked, numbers, table_in) = refs[:3]
    (table_grad, grad_picked, own) = refs[3:6]
    (rows, logits, pulls, table, goals, lse_cols, block, parts) = refs[6:14]
    (grads, sibs, px, pz) = refs[14:18]
    send, recv, send2, recv2, local = refs[18:]
    low, f32 = jnp.bfloat16, jnp.float32
    h, z, c = place()
    part, width = table.shape
    slots = picked.shape[0]
    count = 8 * slots
    device = h * 2 * planes + 2 * z + c
    greet(every_chip(planes))
    lines = Lines(send, recv)
    wires = Wires(send2, recv2)
    gather = Gather(lines, local, planes, [(picked, rows)])
    steps = line_steps(planes)
    gather.launch(0, 0)
    table[...] = table_in[...].astype(low)
    for r in range(2 * planes):
        some = numbers[r, first_line : first_line + 4 * slots // 128, :]
        goals[r] = column(some.astype(f32)).astype(jnp.int32)
    lag = 1
    for i in range(len(steps) + 2 * lag):
        if 1 <= i < len(steps):
            gather.launch(0, steps[i])
        if lag <= i < len(steps) + lag:
            gather.relay(0, steps[i - lag])
        if i >= 2 * lag:
            gather.finish(0, steps[i - 2 * lag])

    def goals_of(t):
        return jnp.concatenate(
            [
                goals[2 * t + core, slots * head : slots * (head + 1), :]
                for head in range(4)
                for core in range(2)
            ],
            axis=0,
        )

    for a, t in enumerate(near_first(planes, z)):
        for s in (a, -a) if a else (0,):
            gather.done(0, s)
        value = mul(rows[:, t].reshape(count, width), table[...], 1, 1)
        logits[t] = value
        top = jnp.max(value, axis=1, keepdims=True)
        lse_cols[t] = top + jnp.log(jnp.sum(jnp.exp(value - top), axis=1, keepdims=True))
    each = count // 128
    for t in range(planes):
        turned = jnp.broadcast_to(lse_cols[t], (count, 128)).T[0:1, :]
        for i in range(each):
            block[each * t + i : each * t + i + 1, :] = turned[:, 128 * i : 128 * (i + 1)]
    state = spread_start(wires, local.at[1], planes, lambda th, tz: block, parts)
    spread_finish(wires, planes, parts, state)
    every = parts[...].reshape(8 * planes, *block.shape)
    peak = jnp.max(every, axis=0)
    total = peak + jnp.log(jnp.sum(jnp.exp(every - peak[None]), axis=0))
    for t in range(planes):
        lse_cols[t] = column(total[each * t : each * (t + 1), :])

    scatter = Scatter(wires, planes, [(grads, grad_picked, sibs, px, pz)])
    order = scatter.to
    hit_sum = jnp.zeros((1, 1), f32)
    for s in range(planes):
        t = order[s]
        goal = goals_of(t)
        value = logits[t]
        hits = iota((count, part), 1) == goal - device * part
        hit_sum = hit_sum + jnp.sum(
            jnp.sum(jnp.where(hits, value, 0.0), axis=1, keepdims=True), axis=0, keepdims=True
        )
        pull = jnp.exp(value - lse_cols[t]) - jnp.where(hits, 1.0, 0.0)
        pulls[t] = jnp.where(goal >= 0, pull, 0.0).astype(low)
        back = mul(pulls[t], table[...]).astype(low).reshape(4, 2, slots, width)
        for th in range(4):
            grads[th, t] = back[th]
        scatter.post(0, s)
        if s:
            scatter.pair(0, s - 1)
    scatter.pair(0, planes - 1)
    mine = goals[2 * z + c, pl.ds(slots * h, slots), :] >= 0
    lse = lse_cols[z, pl.ds(slots * (2 * h + c), slots), :]
    loss = jnp.sum(jnp.where(mine, lse, 0.0), axis=0, keepdims=True) - hit_sum
    live = jnp.sum(jnp.where(mine, 1.0, 0.0), axis=0, keepdims=True)
    lane = iota(own.shape, 1)
    own[...] = jnp.where(lane == 1, loss, jnp.where(lane == 2, live, 0.0))
    own[...] = jnp.where(iota(own.shape, 0) == 0, own[...], 0.0)
    for s in range(planes):
        scatter.plane(0, s)
        if s:
            scatter.line(0, s - 1)
        t = order[s]
        add = mul(pulls[t], rows[:, t].reshape(count, width), 0, 0)
        table_grad[...] = add if s == 0 else table_grad[...] + add
    scatter.line(0, planes - 1)
    scatter.total(0)
    wires.sent()
    lines.sent()


def params(number):
    return pltpu.CompilerParams(
        collective_id=number, has_side_effects=True, vmem_limit_bytes=56 << 20
    )


def dma(count):
    return pltpu.SemaphoreType.DMA((count,))


def spread_wires(planes):
    return 2 * 4 * planes


def scatter_wires(planes, count):
    return count * planes * 11


class Kernels:
    def __init__(self, planes):
        self.planes = planes

    def prepare(self, token_ids, masked_pos, masked_target, segment_ids, norms, bias, table, rest):
        planes = self.planes
        low, f32, i32 = jnp.bfloat16, jnp.float32, jnp.int32
        out_w, places_w, qkv_w, up_w, down_w = rest
        part, width = table.shape
        lines = token_ids.shape[0] // 128
        block = (-(-(lines + masked_pos.shape[1] // 128) // 8) * 8, 128)
        small = (16, 128)
        seq = token_ids.shape[0] // 4
        misc = (2 * norms.shape[1], width)
        shape = jax.ShapeDtypeStruct
        count = line_wires(planes, 4)
        posts = 2 * planes - 1 + 2 * spread_wires(planes)
        return pl.pallas_call(
            functools.partial(prepare_kernel, planes, ROOM),
            out_shape=[
                shape((2 * planes, *block), i32),
                shape((8, width), f32),
                shape((planes, 1, 8 * bias.shape[0]), f32),
                shape((seq, width), f32),
                shape((seq, 1), i32),
                shape((seq, 1), i32),
                shape((4 * planes * ROOM, 1), i32),
                shape((8, 128), i32),
                shape((2, 4, planes, ROOM, width), low),
                shape((4, planes, 2, *misc), low),
                shape((4, planes, 2, *qkv_w.shape), low),
                shape((4, planes, 2, *up_w.shape), low),
                shape((4, planes, 2, *down_w.shape), low),
            ],
            in_specs=[VMEM] * 12,
            out_specs=[VMEM] * 8 + [ANY] * 5,
            scratch_shapes=[
                pltpu.VMEM((2, 4, planes, *small), f32),
                pltpu.VMEM(block, i32),
                pltpu.VMEM(small, f32),
                pltpu.VMEM(misc, low),
                pltpu.VMEM(qkv_w.shape, low),
                pltpu.VMEM(up_w.shape, low),
                pltpu.VMEM(down_w.shape, low),
                pltpu.VMEM((4, planes, ROOM, width), low),
                dma(count),
                dma(count),
                dma(posts),
                dma(posts),
                dma(7),
            ],
            compiler_params=params(1),
            name="prepare",
        )(
            token_ids.reshape(lines, 128),
            masked_pos,
            masked_target,
            segment_ids.reshape(lines, 128),
            norms,
            bias.reshape(1, -1),
            table,
            out_w,
            places_w,
            qkv_w,
            up_w,
            down_w,
        )

    def forward(self, box, gathered, home, ranks, extra, labels, norms, bias, chosen):
        planes = self.planes
        low, f32 = jnp.bfloat16, jnp.float32
        tokens, width = extra.shape
        units = bias.shape[2]
        saved = [
            ((tokens, width), f32),
            ((tokens, 1), f32),
            ((4, tokens, gathered[1].shape[4]), low),
            ((tokens, 128), f32),
            ((tokens, width), low),
            ((tokens, width), f32),
            ((tokens, 1), f32),
            ((planes, tokens, units), low),
            ((planes, tokens, units), low),
            ((tokens, width), f32),
            ((tokens, 1), f32),
            ((chosen.shape[0], width), low),
        ]
        return pl.pallas_call(
            functools.partial(forward_kernel, planes, ROOM),
            out_shape=[jax.ShapeDtypeStruct(s, t) for s, t in saved],
            in_specs=[VMEM] + [ANY] * 4 + [VMEM] * 8,
            out_specs=[VMEM] * len(saved),
            scratch_shapes=[pltpu.VMEM(g.shape, low) for g in gathered]
            + [
                pltpu.VMEM((tokens, width), f32),
                pltpu.VMEM((tokens, width), f32),
                pltpu.VMEM((tokens, 1), jnp.int32),
                dma(4),
            ],
            compiler_params=pltpu.CompilerParams(vmem_limit_bytes=60 << 20),
            name="forward",
        )(
            box,
            *gathered,
            home,
            ranks,
            extra,
            labels.reshape(-1, 128),
            labels.reshape(1, -1),
            norms,
            bias,
            chosen.reshape(1, -1),
        )

    def deliver(self, parcels):
        planes = self.planes
        wires = spread_wires(planes)
        return pl.pallas_call(
            functools.partial(deliver_kernel, planes),
            out_shape=jax.ShapeDtypeStruct((2, *parcels.shape), parcels.dtype),
            in_specs=[ANY],
            out_specs=ANY,
            scratch_shapes=[dma(wires), dma(wires), pltpu.SemaphoreType.DMA],
            compiler_params=params(3),
            name="deliver",
        )(parcels)

    def head(self, picked, numbers, table, first_line):
        planes = self.planes
        low, f32 = jnp.bfloat16, jnp.float32
        part, width = table.shape
        slots = picked.shape[0]
        count = 8 * slots
        block = (planes * count // 128, 128)
        wires = line_wires(planes, 1)
        wires2 = spread_wires(planes) + scatter_wires(planes, 1)
        return pl.pallas_call(
            functools.partial(head_kernel, planes, first_line),
            out_shape=[
                jax.ShapeDtypeStruct((part, width), f32),
                jax.ShapeDtypeStruct((slots, width), f32),
                jax.ShapeDtypeStruct((8, 128), f32),
            ],
            in_specs=[VMEM] * 3,
            out_specs=[VMEM] * 3,
            scratch_shapes=[
                pltpu.VMEM((4, planes, 2, slots, width), low),
                pltpu.VMEM((planes, count, part), f32),
                pltpu.VMEM((planes, count, part), low),
                pltpu.VMEM((part, width), low),
                pltpu.VMEM((2 * planes, 4 * slots, 1), jnp.int32),
                pltpu.VMEM((planes, count, 1), f32),
                pltpu.VMEM(block, f32),
                pltpu.VMEM((2, 4, planes, *block), f32),
                pltpu.VMEM((4, planes, 2, slots, width), low),
                pltpu.VMEM((4, planes, slots, width), low),
                pltpu.VMEM((planes, 3, slots, width), low),
                pltpu.VMEM((planes - 1, slots, width), low),
                dma(wires),
                dma(wires),
                dma(wires2),
                dma(wires2),
                dma(2),
            ],
            compiler_params=params(4),
            name="head",
        )(picked, numbers, table)

    def collect(self, back, which, logits_part, sums, own):
        planes = self.planes
        wires = spread_wires(planes)
        f32 = jnp.float32
        return pl.pallas_call(
            functools.partial(collect_kernel, planes),
            out_shape=[
                jax.ShapeDtypeStruct(logits_part.shape, f32),
                jax.ShapeDtypeStruct(own.shape, f32),
            ],
            in_specs=[VMEM] * 8,
            out_specs=[VMEM] * 2,
            scratch_shapes=[
                pltpu.VMEM(own.shape, f32),
                pltpu.VMEM((2, 4, planes, *own.shape), f32),
                dma(wires),
                dma(wires),
                pltpu.SemaphoreType.DMA,
            ],
            compiler_params=params(6),
            name="collect",
        )(back, which, logits_part, *sums, own)

    def hand_back(self, parcels):
        planes = self.planes
        layer = parcels.shape[1:]
        wires = spread_wires(planes)
        return pl.pallas_call(
            functools.partial(return_kernel, planes),
            out_shape=jax.ShapeDtypeStruct(layer, parcels.dtype),
            in_specs=[VMEM],
            out_specs=ANY,
            scratch_shapes=[pltpu.VMEM(layer, parcels.dtype)]
            + [dma(wires), dma(wires), pltpu.SemaphoreType.DMA],
            compiler_params=params(9),
            name="hand_back",
        )(parcels)

    def backward(self, grad_picked, chosen, norms, labels, home, ranks, saved, gathered):
        planes = self.planes
        low, f32 = jnp.bfloat16, jnp.float32
        unit0, scale0, mixed, lse, heads, unit1, scale1, active, slope, unit2, scale2 = saved
        misc_all, wq_all, wu_all, wd_all = gathered
        tokens, width = unit0.shape
        share = wu_all.shape[3]
        rows, lanes = wq_all.shape[3:]
        wide = -(-(lanes + 1) // 128) * 128
        blocks = [(share, width), (share, width), (rows, wide), misc_all.shape[3:]]
        count = scatter_wires(planes, 4) + spread_wires(planes)

        def held(shape):
            n, m = shape
            return [
                pltpu.VMEM((4, planes, 2, n, m), low),
                pltpu.VMEM((4, planes, n, m), low),
                pltpu.VMEM((planes, 3, n, m), low),
                pltpu.VMEM((planes - 1, n, m), low),
            ]

        units = active.shape[2]
        out = pl.pallas_call(
            functools.partial(backward_kernel, planes, ROOM),
            out_shape=[jax.ShapeDtypeStruct((4, planes, ROOM, width), low)]
            + [jax.ShapeDtypeStruct(b, f32) for b in blocks]
            + [jax.ShapeDtypeStruct((tokens, width), low)],
            in_specs=[VMEM] * 11 + [ANY] * 11,
            out_specs=[ANY] + [VMEM] * 5,
            scratch_shapes=[x for b in blocks for x in held(b)]
            + [
                pltpu.VMEM((2, 4, planes, ROOM, width), low),
                pltpu.VMEM((4, planes, ROOM, width), low),
                pltpu.VMEM((tokens, width), f32),
                pltpu.VMEM((tokens, width), f32),
                pltpu.VMEM((width, width), f32),
                pltpu.VMEM((tokens, width), low),
                pltpu.VMEM((tokens, width), low),
                pltpu.VMEM((4, 2, share, width), low),
                pltpu.VMEM((4, 2, share, width), low),
                pltpu.VMEM((tokens, units), low),
                pltpu.VMEM((tokens, units), low),
                pltpu.VMEM((planes, 2, rows, lanes), low),
                pltpu.VMEM((tokens, lanes), low),
                pltpu.VMEM((4, tokens, lanes), low),
                pltpu.VMEM((8, width), f32),
                pltpu.VMEM((tokens, 1), jnp.int32),
                dma(count),
                dma(count),
                dma(12),
            ],
            compiler_params=pltpu.CompilerParams(
                collective_id=8, has_side_effects=True, vmem_limit_bytes=62 << 20
            ),
            name="backward",
        )(
            grad_picked,
            chosen.reshape(1, -1),
            norms,
            labels.reshape(-1, 128),
            labels.reshape(1, -1),
            home,
            ranks,
            scale0,
            scale1,
            scale2,
            lse,
            unit0,
            unit1,
            unit2,
            mixed,
            heads,
            active,
            slope,
            misc_all,
            wq_all,
            wu_all,
            wd_all,
        )
        return out


class Plain:
    def __init__(self, planes):
        self.planes = planes

    def prepare(self, token_ids, masked_pos, masked_target, segment_ids, norms, bias, table, rest):
        return prepare_plain(
            self, token_ids, masked_pos, masked_target, segment_ids, norms, bias, table, rest
        )

    def gather(self, block):
        whole = lax.all_gather(block, ("head", "row"))
        return whole.reshape(4, self.planes, 2, *block.shape)

    def forward(self, box, gathered, home, ranks, extra, labels, norms, bias, chosen):
        seat = jnp.where(ranks < ROOM, home * ROOM + ranks, -1)
        return forward_plain(box, gathered, seat, extra, labels, norms, bias, chosen)

    def deliver(self, parcels):
        shape = parcels.shape
        both = jnp.broadcast_to(parcels[:, :, None], (*shape[:2], 2, *shape[2:]))
        flat = both.reshape(8 * self.planes, *shape[2:])
        got = lax.all_to_all(flat, ("head", "row"), split_axis=0, concat_axis=0, tiled=True)
        return jnp.moveaxis(got.reshape(4, self.planes, 2, *shape[2:]), 2, 0)

    def head(self, picked, numbers, table, first_line):
        return head_plain(self, picked, numbers, table, first_line)

    def small(self, block, number):
        return jnp.moveaxis(self.gather(block), 2, 0)

    def scatter_rows(self, grads):
        flat = grads.reshape(-1, grads.shape[-1]).astype(jnp.float32)
        return lax.psum_scatter(flat, ("head", "row"), scatter_dimension=0, tiled=True)

    def backward(self, grad_picked, chosen, norms, labels, home, ranks, saved, gathered):
        return backward_plain(
            self, grad_picked, chosen, norms, labels, home, ranks, saved, gathered
        )

    def collect(self, back, which, logits_part, sums, own):
        part, width = logits_part.shape
        marks = (which == jnp.arange(part)[None, :]).astype(jnp.bfloat16)
        table_grad = logits_part + contract(marks, back.reshape(-1, width), 0, 0)
        squares = sum(jnp.sum(g * g) for g in (table_grad, *sums))
        return table_grad, lax.psum(own.at[0, 0].set(squares), ("head", "row"))

    def hand_back(self, parcels):
        shape = parcels.shape
        flat = jnp.moveaxis(parcels, 0, 2).reshape(8 * self.planes, *shape[3:])
        got = lax.all_to_all(flat, ("head", "row"), split_axis=0, concat_axis=0, tiled=True)
        got = got.reshape(4, self.planes, 2, *shape[3:]).astype(jnp.float32)
        return jnp.sum(got, axis=2).astype(parcels.dtype)


def contract(left, right, left_dim, right_dim):
    return lax.dot_general(
        left, right, (((left_dim,), (right_dim,)), ((), ())), preferred_element_type=jnp.float32
    )


def by_plane(blocks):
    planes, lanes = blocks.shape[1], blocks.shape[4]
    return blocks.transpose(1, 0, 2, 3, 4).reshape(planes, -1, lanes)


def heads_of(mixed):
    tokens = mixed.shape[1]
    parts = mixed.reshape(4, tokens, -1, 3, HD).transpose(3, 1, 0, 2, 4)
    parts = parts.reshape(3, tokens, -1, HD)
    return parts[0], parts[1], parts[2]


def prepare_plain(
    wire, token_ids, masked_pos, masked_target, segment_ids, norms, bias, table, rest
):
    low, f32 = jnp.bfloat16, jnp.float32
    out_w, places_w, qkv_w, up_w, down_w = rest
    planes = wire.planes
    rows = 2 * planes
    device = lax.axis_index("head") * rows + lax.axis_index("row")
    chip = lax.axis_index("head") * planes + lax.axis_index("row") // 2
    part, width = table.shape
    share = norms.shape[1]
    lines = token_ids.shape[0] // 128
    at = masked_pos[0][:, None] == jnp.arange(segment_ids.shape[0])[None, :]
    labels = jnp.sum(jnp.where(at, segment_ids[None, :], 0), axis=1)
    target = jnp.where(labels != SEQ - 1, masked_target[0], -1)
    block = jnp.concatenate([token_ids, target])
    block_rows = -(-block.shape[0] // 1024) * 8
    numbers = lax.all_gather(padded(block, block_rows, 128), "row")
    small = jnp.zeros((16, 128), f32).at[:8, :share].set(norms).at[8, : bias.shape[0]].set(bias)
    small_all = wire.small(small.astype(low), 0)
    tokens = token_ids.shape[0] // HEADS
    ids = numbers[:, :lines].reshape(planes, 2, HEADS, tokens)
    ids = ids.transpose(2, 0, 1, 3).reshape(HEADS * planes, 2 * tokens)
    owner = ids // part
    devices = HEADS * rows
    counts = jnp.sum(owner[:, :, None] == jnp.arange(devices), axis=1)
    order = jnp.arange(2 * tokens)
    before = (order[:, None] < order[None, :]).astype(low)
    inside = owner == device
    rank = jnp.dot(inside.astype(low), before, preferred_element_type=f32).astype(jnp.int32)
    hit = jnp.where(inside, rank, -1)[:, None, :] == jnp.arange(ROOM)[None, :, None]
    which = jnp.sum(jnp.where(hit, ids[:, None, :] - device * part + 1, 0), axis=2) - 1
    marks = (which.reshape(-1, 1) == jnp.arange(part)[None, :]).astype(low)
    parcels = jnp.dot(marks, table.astype(low), preferred_element_type=f32).astype(low)
    box = wire.deliver(parcels.reshape(HEADS, planes, ROOM, width))
    own = lax.dynamic_index_in_dim(owner, chip, 0, keepdims=False)
    own_marks = own[:, None] == jnp.arange(devices)
    own_before = contract(before, own_marks.astype(low), 0, 0).astype(jnp.int32)
    own_rank = jnp.sum(jnp.where(own_marks, own_before, 0), axis=1)
    core = lax.axis_index("row") % 2
    own = lax.dynamic_slice_in_dim(own, core * tokens, tokens, 0)
    own_rank = lax.dynamic_slice_in_dim(own_rank, core * tokens, tokens, 0)
    home = (own % 2) * (devices // 2) + own // 2
    misc = jnp.concatenate(
        [out_w, jnp.pad(places_w, ((0, 0), (0, width - SEQ)))], axis=0
    ).astype(low)
    small_all = jnp.moveaxis(small_all, 0, 2).astype(f32)
    span = bias.shape[0]
    norms = small_all[..., :8, :share].transpose(3, 0, 1, 2, 4).reshape(8, width)
    bias = small_all[..., 8, :span].transpose(1, 0, 2, 3).reshape(planes, 1, -1)
    return (
        numbers,
        norms,
        bias,
        jnp.zeros((tokens, width), f32),
        home[:, None],
        own_rank[:, None],
        which.reshape(-1, 1),
        jnp.max(counts).reshape(1, 1),
        box,
        wire.gather(misc),
        wire.gather(qkv_w.astype(low)),
        wire.gather(up_w.astype(low)),
        wire.gather(down_w.astype(low)),
    )


def unit_ramp(planes, plane, units):
    share = units // 8
    lane = iota((1, units), 1)
    block = lax.div(lane, share)
    natural = (lax.div(block, 2) * 2 * planes + 2 * plane + lax.rem(block, 2)) * share
    natural = natural + lax.rem(lane, share)
    return jnp.where(natural < OLD_FF, 1.0, STEP / RAMP).astype(jnp.float32)


def forward_plain(parcels, gathered, home, extra, labels, norms, bias, chosen):
    low = jnp.bfloat16
    misc, wq, wu, wd = gathered
    tokens, width = extra.shape
    share = misc.shape[3] // 2
    rows = parcels.reshape(-1, width)
    looked = jnp.dot(
        (home == jnp.arange(rows.shape[0])[None, :]).astype(low),
        rows,
        preferred_element_type=jnp.float32,
    )
    places = misc[:, :, :, share:, :SEQ].reshape(width, SEQ).T.astype(jnp.float32)
    unit0, scale0 = unit_of(looked + extra + places)
    normed = unit0 * norms[0] + norms[1]
    weight = wq.reshape(4, width, wq.shape[4])
    mixed = jnp.einsum("td,hdj->htj", normed.astype(low), weight, preferred_element_type=jnp.float32)
    mixed = mixed.astype(low)
    query, keys, values = heads_of(mixed)
    attended, summary = attend_fwd(query, keys, values, labels)
    head_ramp = jnp.where(jnp.arange(query.shape[1]) < OLD_HEADS, 1.0, STEP / RAMP)
    heads = (attended * head_ramp[:, None]).astype(low).reshape(tokens, width)
    lse = jnp.pad(summary.T, ((0, 0), (0, 128 - summary.shape[0])))
    weight = misc[:, :, :, :share].reshape(width, width)
    unit1, scale1 = unit_of(normed + contract(heads, weight, 1, 1) + norms[6])
    hidden = unit1 * norms[2] + norms[3]
    u = jnp.einsum(
        "td,pud->ptu", hidden.astype(low), by_plane(wu), preferred_element_type=jnp.float32
    )
    planes = wu.shape[1]
    ramp = jnp.stack([unit_ramp(planes, t, bias.shape[2]) for t in range(planes)])
    value, rise = gelu_parts(u + bias, ramp)
    active = value.astype(low)
    down = jnp.einsum("ptu,pud->td", active, by_plane(wd), preferred_element_type=jnp.float32)
    unit2, scale2 = unit_of(hidden + down + norms[7])
    final = (unit2 * norms[4] + norms[5]).astype(low)
    marks = (chosen[:, None] == jnp.arange(tokens)[None, :]).astype(low)
    picked = jnp.dot(marks, final, preferred_element_type=jnp.float32).astype(low)
    slope = rise.astype(low)
    return (unit0, scale0, mixed, lse, heads, unit1, scale1, active, slope, unit2, scale2, picked)


def score_block(query, keys, labels):
    scores = jnp.einsum("qhe,khe->hqk", query, keys, preferred_element_type=jnp.float32) * HD ** (
        -0.5
    )
    allowed = labels[:, None] == labels[None, :]
    return jnp.where(allowed[None], scores, -1000000000.0)


def attend_fwd(query, keys, values, labels):
    scores = score_block(query, keys, labels)
    top = jnp.max(scores, axis=-1, keepdims=True)
    weights = jnp.exp(scores - top)
    total = jnp.sum(weights, axis=-1, keepdims=True)
    probs = weights / total
    output = jnp.einsum(
        "hqk,khe->qhe", probs.astype(jnp.bfloat16), values, preferred_element_type=jnp.float32
    )
    return (output, (top + jnp.log(total))[..., 0])


def attend_back(query, keys, values, labels, summary, grad_out):
    scores = score_block(query, keys, labels)
    probs = jnp.exp(scores - summary[..., None])
    grad_values = jnp.einsum(
        "hqk,qhe->khe", probs.astype(jnp.bfloat16), grad_out, preferred_element_type=jnp.float32
    )
    grad_probs = jnp.einsum("qhe,khe->hqk", grad_out, values, preferred_element_type=jnp.float32)
    grad_scores = probs * (grad_probs - jnp.sum(grad_probs * probs, axis=-1, keepdims=True))
    grad_low = grad_scores.astype(jnp.bfloat16)
    grad_query = jnp.einsum(
        "hqk,khe->qhe", grad_low, keys, preferred_element_type=jnp.float32
    ) * HD ** (-0.5)
    grad_keys = jnp.einsum(
        "hqk,qhe->khe", grad_low, query, preferred_element_type=jnp.float32
    ) * HD ** (-0.5)
    return jnp.stack([grad_query, grad_keys, grad_values], axis=2)


def head_plain(wire, picked, numbers, table, first_line):
    low = jnp.bfloat16
    planes = wire.planes
    row_count = 2 * planes
    devices = HEADS * row_count
    device = lax.axis_index("head") * row_count + lax.axis_index("row")
    slots, width = picked.shape
    vocab_part = table.shape[0]
    table = table.astype(low)
    flat = numbers.reshape(row_count, -1)
    targets = flat[:, first_line * 128 : first_line * 128 + HEADS * slots]
    targets = targets.reshape(row_count, HEADS, slots).transpose(1, 0, 2).reshape(-1)
    all_rows = wire.gather(picked).reshape(devices * slots, width)
    valid = (targets >= 0).astype(jnp.float32)
    logits = contract(all_rows, table, 1, 1)
    hits = jnp.arange(vocab_part)[None, :] == (targets - device * vocab_part)[:, None]
    top = jnp.max(logits, axis=1)
    part = top + jnp.log(jnp.sum(jnp.exp(logits - top[:, None]), axis=1))
    parts = wire.gather(part.reshape(-1, 128)).reshape(devices, -1)
    peak = jnp.max(parts, axis=0)
    log_total = peak + jnp.log(jnp.sum(jnp.exp(parts - peak), axis=0))
    target_part = jnp.sum(jnp.where(hits, logits, 0.0))
    log_own = lax.dynamic_slice_in_dim(log_total * valid, device * slots, slots, 0)
    valid_own = lax.dynamic_slice_in_dim(valid, device * slots, slots, 0)
    loss_own = jnp.sum(log_own) - target_part
    count_own = jnp.sum(valid_own)
    grad_logits = (
        valid[:, None] * (jnp.exp(logits - log_total[:, None]) - hits.astype(jnp.float32))
    ).astype(low)
    grad_table = contract(grad_logits, all_rows, 0, 0)
    grad_rows = jnp.dot(grad_logits, table, preferred_element_type=jnp.float32).astype(low)
    grad_picked = wire.scatter_rows(grad_rows.reshape(HEADS, planes, 2, slots, width))
    own = padded(jnp.stack([jnp.float32(0), loss_own, count_own]), 8, 128)
    return grad_table, grad_picked, own


def backward_plain(wire, grad_picked, chosen, norms, labels, home, ranks, saved, gathered):
    low, f32 = jnp.bfloat16, jnp.float32
    unit_zero, scale_zero, mixed, lse, heads_low, unit_one, scale_one = saved[:7]
    active, slope, unit_two, scale_two = saved[7:]
    planes = wire.planes
    devices = 8 * planes
    tokens, width = unit_zero.shape
    share, share_inner = width // devices, gathered[2].shape[3]
    out_full = gathered[0][:, :, :, :share].reshape(width, width)
    qkv_full = gathered[1].reshape(HEADS, width, -1)
    up_full, down_full = by_plane(gathered[2]), by_plane(gathered[3])
    normed_low = (unit_zero * norms[0] + norms[1]).astype(low)
    hidden_low = (unit_one * norms[2] + norms[3]).astype(low)
    query, keys, values = heads_of(mixed)
    heads = query.shape[1]
    summary = lse[:, :heads].T
    head_ramp = jnp.where(jnp.arange(heads) < OLD_HEADS, 1.0, STEP / RAMP).astype(f32)
    chosen_marks = chosen[:, None] == jnp.arange(tokens)[None, :]
    grad_final = lax.dot_general(
        chosen_marks.astype(jnp.float32),
        grad_picked,
        (((0,), (0,)), ((), ())),
        precision=lax.Precision.HIGHEST,
    )
    grad_sum, gain_two = unit_back(grad_final, unit_two, scale_two, norms[4])
    grad_sum_low = grad_sum.astype(low)
    grad_down = jnp.einsum("ptu,td->pud", active, grad_sum_low, preferred_element_type=f32)
    grad_upper = jnp.einsum("td,pud->ptu", grad_sum_low, down_full, preferred_element_type=f32)
    grad_upper = grad_upper * slope.astype(f32)
    grad_upper_low = grad_upper.astype(low)
    grad_up = jnp.einsum("ptu,td->pud", grad_upper_low, hidden_low, preferred_element_type=f32)
    grad_hidden = grad_sum + jnp.einsum(
        "ptu,pud->td", grad_upper_low, up_full, preferred_element_type=f32
    )
    grad_res, gain_one = unit_back(grad_hidden, unit_one, scale_one, norms[2])
    grad_res_low = grad_res.astype(low)
    grad_out = contract(grad_res_low, heads_low, 0, 0)
    grad_heads = jnp.dot(grad_res_low, out_full, preferred_element_type=jnp.float32).astype(low)
    grad_attended = (
        grad_heads.reshape(tokens, heads, HD).astype(jnp.float32) * head_ramp[:, None]
    ).astype(low)
    grad_mixed = attend_back(query, keys, values, labels, summary, grad_attended)
    grad_mixed_low = grad_mixed.astype(low).reshape(tokens, HEADS, -1)
    grad_qkv = jnp.einsum(
        "td,thj->hdj", normed_low, grad_mixed_low, preferred_element_type=jnp.float32
    )
    grad_normed = grad_res + jnp.einsum(
        "thj,hdj->td", grad_mixed_low, qkv_full, preferred_element_type=jnp.float32
    )
    grad_start, gain_zero = unit_back(grad_normed, unit_zero, scale_zero, norms[0])
    grad_start_low = grad_start.astype(low)
    grad_norms = jnp.stack(
        [
            jnp.sum(gain_zero, axis=0),
            jnp.sum(grad_normed, axis=0),
            jnp.sum(gain_one, axis=0),
            jnp.sum(grad_hidden, axis=0),
            jnp.sum(gain_two, axis=0),
            jnp.sum(grad_final, axis=0),
            jnp.sum(grad_res, axis=0),
            jnp.sum(grad_sum, axis=0),
        ]
    )
    grad_bias = jnp.sum(grad_upper, axis=1).reshape(planes, HEADS, 2, share_inner)
    seat = jnp.where(ranks < ROOM, home * ROOM + ranks, -1)
    marks = (seat == jnp.arange(devices * ROOM)[None, :]).astype(low)
    back = contract(marks, grad_start_low, 0, 0).astype(low)
    back = wire.hand_back(back.reshape(2, HEADS, planes, ROOM, width))

    def by_head(grad):
        grad = grad.reshape(planes, HEADS, 2, share_inner, width).astype(low)
        return grad.transpose(1, 0, 2, 3, 4)

    rows = jnp.concatenate(
        [grad_start.T, grad_norms.T, jnp.zeros((width, width - tokens - 8), f32)], axis=1
    )
    misc = jnp.concatenate(
        [grad_out.reshape(devices, share, width), rows.reshape(devices, share, width)], axis=1
    )
    bias = grad_bias.transpose(1, 0, 2, 3).reshape(devices, 1, share_inner)
    return (
        back,
        wire.scatter_rows(by_head(grad_up)),
        wire.scatter_rows(by_head(grad_down)),
        jnp.concatenate(
            [
                wire.scatter_rows(grad_qkv.astype(low).reshape(devices, -1, qkv_full.shape[2])),
                wire.scatter_rows(bias).T,
            ],
            axis=1,
        ),
        wire.scatter_rows(misc.astype(low)),
        grad_start_low,
    )


def adamw(weight, grad, first, second, decay, rate):
    first = BETA_ONE * first + (1 - BETA_ONE) * grad
    second = BETA_TWO * second + (1 - BETA_TWO) * grad * grad
    moved = first / (1 - BETA_ONE**STEP) / (jnp.sqrt(second / (1 - BETA_TWO**STEP)) + ADAM_EPSILON)
    return (weight - rate * (moved + decay * weight), first, second)


def padded(flat, rows, lanes):
    return jnp.pad(flat, (0, rows * lanes - flat.shape[0])).reshape(rows, lanes)


def on_device(
    token_ids,
    segment_ids,
    masked_pos,
    masked_target,
    embedding,
    position_table,
    qkv_weight,
    out_weight,
    up_weight,
    down_weight,
    norm_params,
    up_bias,
    m_embedding,
    m_position,
    m_qkv,
    m_out,
    m_up,
    m_down,
    m_norm,
    m_bias,
    v_embedding,
    v_position,
    v_qkv,
    v_out,
    v_up,
    v_down,
    v_norm,
    v_bias,
):
    low = jnp.bfloat16
    row_count = lax.axis_size("row")
    devices = HEADS * row_count
    planes = row_count // 2
    wire = Kernels(planes) if planes <= 4 else Plain(planes)
    head = lax.axis_index("head")
    row = lax.axis_index("row")
    core = row % 2
    device = head * row_count + row
    vocab_part, width = embedding.shape
    tokens = token_ids.shape[0] // HEADS
    inner = up_weight.shape[1] * devices

    share = width // devices
    share_inner = inner // devices

    labels_all = segment_ids.reshape(HEADS, tokens)
    slots = masked_pos.shape[1] // HEADS
    numbers, norms, bias, extra, home, ranks, which, fullest, box, *gathered = wire.prepare(
        token_ids,
        masked_pos,
        masked_target,
        segment_ids,
        norm_params,
        up_bias,
        embedding,
        (out_weight.T, position_table.T, qkv_weight, up_weight.T, down_weight),
    )
    rounds = -(-fullest[0, 0] // ROOM)
    lines = token_ids.shape[0] // 128
    numbers = numbers.reshape(row_count, -1)
    def which_in(turn):
        ids = numbers[:, : lines * 128].reshape(planes, 2, HEADS, tokens)
        ids = ids.transpose(2, 0, 1, 3).reshape(HEADS * planes, 2 * tokens) - device * vocab_part
        inside = (ids >= 0) & (ids < vocab_part)
        order = jnp.arange(2 * tokens)
        before = (order[:, None] < order[None, :]).astype(low)
        rank = jnp.dot(inside.astype(low), before, preferred_element_type=jnp.float32)
        rank = jnp.where(inside, rank.astype(jnp.int32), -1)
        spot = jnp.arange(ROOM) + turn * ROOM
        hit = rank[:, None, :] == spot[None, :, None]
        return (jnp.sum(jnp.where(hit, ids[:, None, :] + 1, 0), axis=2) - 1).reshape(-1, 1)

    def parcel_marks(which):
        return (which == jnp.arange(vocab_part)[None, :]).astype(low)

    def token_marks(turn):
        seat = ranks - turn * ROOM
        seat = jnp.where((seat >= 0) & (seat < ROOM), home * ROOM + seat, -1)
        return (seat == jnp.arange(devices * ROOM)[None, :]).astype(low)

    def again(state):
        turn, so_far = state
        marks = parcel_marks(which_in(turn)).astype(jnp.float32)
        parcels = jnp.dot(marks, embedding)
        more = wire.deliver(parcels.astype(low).reshape(HEADS, planes, ROOM, width))
        more = jnp.dot(
            token_marks(turn),
            more.reshape(devices * ROOM, width),
            preferred_element_type=jnp.float32,
        )
        return turn + 1, so_far + more

    _, extra = lax.while_loop(lambda state: state[0] < rounds, again, (jnp.int32(1), extra))

    labels = lax.dynamic_index_in_dim(labels_all, head, 0, keepdims=False)
    chosen = lax.dynamic_slice_in_dim(masked_pos[0], head * slots, slots, 0) - head * tokens
    *saved, picked = wire.forward(
        box, gathered, home, ranks, extra, labels, norms, bias, chosen
    )

    grad_table, grad_picked, own = wire.head(
        picked, numbers.reshape(row_count, -1, 128), embedding, lines
    )

    parcels, *sums, of_start = wire.backward(
        grad_picked, chosen, norms, labels, home, ranks, saved, gathered
    )

    def again_back(state):
        turn, so_far = state
        back = contract(token_marks(turn), of_start, 0, 0).astype(low)
        back = wire.hand_back(back.reshape(2, HEADS, planes, ROOM, width))
        more = contract(parcel_marks(which_in(turn)), back.reshape(-1, width), 0, 0)
        return turn + 1, so_far + more

    _, grad_table = lax.while_loop(
        lambda state: state[0] < rounds, again_back, (jnp.int32(1), grad_table)
    )
    grad_table, totals = wire.collect(parcels, which, grad_table, sums, own)
    of_up, of_down, of_qkv, of_misc = sums
    squares, loss_sum, live_count = totals[0, 0], totals[0, 1], totals[0, 2]
    grad_norm = jnp.sqrt(squares) / live_count
    weights = (
        embedding,
        position_table,
        qkv_weight,
        out_weight,
        up_weight,
        down_weight,
        norm_params,
        up_bias,
    )
    firsts = (m_embedding, m_position, m_qkv, m_out, m_up, m_down, m_norm, m_bias)
    seconds = (v_embedding, v_position, v_qkv, v_out, v_up, v_down, v_norm, v_bias)
    decays = (DECAY,) * 6 + (0.0, 0.0)
    rates = (LEARN_RATE,) * 6 + (GAIN_RATE,) * 2
    wide = qkv_weight.shape[1]
    if isinstance(wire, Kernels):
        turned = (False, True, False, True, True, False, False, None)
        view = [
            (lambda a: a.reshape(1, -1)) if t is None else (lambda a: a.T) if t else (lambda a: a)
            for t in turned
        ]
        spots = [(0, 0), (share, 0), (0, 0), (0, 0), (0, 0), (0, 0), (share, SEQ), (0, wide)]
        cuts = [(*spots[k], k > 5, decays[k], rates[k]) for k in range(8)]
        of = (grad_table, of_misc, of_qkv, of_misc, of_up, of_down, of_misc, of_qkv)
        arrays = [[view[k](a) for k, a in enumerate(group)] for group in (weights, firsts, seconds)]
        results = update(totals, cuts, of, *arrays, 10)
        undo = [
            (lambda a: a.reshape(-1)) if t is None else (lambda a: a.T) if t else (lambda a: a)
            for t in turned
        ]
        results = [[undo[k](a) for a in three] for k, three in enumerate(results)]
    else:
        factor = jnp.minimum(1.0, CLIP / grad_norm) / live_count
        grads = (
            grad_table,
            of_misc[share : 2 * share, :SEQ].T,
            of_qkv[:, :wide],
            of_misc[:share].T,
            of_up.T,
            of_down,
            of_misc[share : 2 * share, SEQ : SEQ + 8].T,
            of_qkv[:, wide],
        )
        results = [
            adamw(w, g * factor, m, v, d, r)
            for w, g, m, v, d, r in zip(weights, grads, firsts, seconds, decays, rates)
        ]
    return (
        *(r[0] for r in results),
        *(r[1] for r in results),
        *(r[2] for r in results),
        loss_sum,
        live_count,
        grad_norm,
    )


def solution(mesh):
    vocab = P(("head", "row"), None)
    columns = P(None, ("head", "row"))
    flat = P(("head", "row"))
    weights = (vocab, columns, P("row", "head"), columns, columns, vocab, columns, flat)
    data = (P("row"), P("row"), P("row", None), P("row", None))
    return jax.shard_map(
        on_device,
        mesh=mesh,
        in_specs=(*data, *weights, *weights, *weights),
        out_specs=(*weights, *weights, *weights, P(), P(), P()),
        check_vma=False,
    )
```
